32 devices in a mesh: shard: 4 (over y, x), dp: 8 (over z, core).
Axes of the slice: x: 2, y: 2, z: 4, core: 2. Of those that a mesh axis runs over, the one named last changes fastest.
Arguments:
- tokens: bfloat16 [32768, 768], P(('shard', 'dp')), may hold values from -6 to 6
- lengths: int32 [32, 3], P(('shard', 'dp')), may hold values from 1 to 768, 1024 in all within a row
- cotangent: bfloat16 [32768, 768], P(('shard', 'dp')), may hold values from -6 to 6
- heads_master: float32 [768, 2304], P('shard'), may hold values from -0.21875 to 0.21875
- output_master: float32 [768, 768], P('shard'), may hold values from -0.875 to 0.875
- expand_master: float32 [768, 3072], P('shard'), may hold values from -0.21875 to 0.21875
- reduce_master: float32 [3072, 768], P('shard'), may hold values from -0.109375 to 0.109375
- vector_master: float32 [9984], P('shard'), may hold values from -1 to 1.5
- heads_moment: float32 [768, 2304], P('shard'), may hold values from -64 to 64
- output_moment: float32 [768, 768], P('shard'), may hold values from -32 to 32
- expand_moment: float32 [768, 3072], P('shard'), may hold values from -32 to 32
- reduce_moment: float32 [3072, 768], P('shard'), may hold values from -64 to 64
- vector_moment: float32 [9984], P('shard'), may hold values from -128 to 128
- heads_square: float32 [768, 2304], P('shard'), may hold values from 432.5376 to 1723.5968
- output_square: float32 [768, 768], P('shard'), may hold values from 155.32031 to 622.592
- expand_square: float32 [768, 3072], P('shard'), may hold values from 155.32031 to 622.592
- reduce_square: float32 [3072, 768], P('shard'), may hold values from 619.3152 to 2483.8145
- vector_square: float32 [9984], P('shard'), may hold values from 1723.5968 to 6881.28
Outputs:
- block_output: bfloat16 [32768, 768], P(('shard', 'dp'))
- token_gradient: bfloat16 [32768, 768], P(('shard', 'dp'))
- heads_momentum: float32 [768, 2304], P('shard')
- heads_squares: float32 [768, 2304], P('shard')
- heads_updated: float32 [768, 2304], P('shard')
- output_momentum: float32 [768, 768], P('shard')
- output_squares: float32 [768, 768], P('shard')
- output_updated: float32 [768, 768], P('shard')
- expand_momentum: float32 [768, 3072], P('shard')
- expand_squares: float32 [768, 3072], P('shard')
- expand_updated: float32 [768, 3072], P('shard')
- reduce_momentum: float32 [3072, 768], P('shard')
- reduce_squares: float32 [3072, 768], P('shard')
- reduce_updated: float32 [3072, 768], P('shard')
- vector_momentum: float32 [9984], P('shard')
- vector_squares: float32 [9984], P('shard')
- vector_updated: float32 [9984], P('shard')
The draws below stay inside these ranges and needn't reach their ends.
Inputs may be any that keep to these rules, and one draw needn't show every extreme that they name: Each row holds the lengths of the 3 documents of one device's 1024 tokens; they sum to 1024 and the longest is exactly 768.
All inputs are finite; a program needn't handle non-finite values.
Results may differ from the reference program's by a relative error of at most 0.0045.
The reference program's roundings to bfloat16 on the way count: a program that leaves them out, or rounds other values in their place, can miss the bound.
Values may be sent and summed in bfloat16 or wider, within the bound.
A program may use at most 256 MiB of HBM per device.

```python
import math
import jax
import jax.numpy as jnp
import numpy as np
from jax import lax

D = 768
HEADS = 12
HEAD = 64
ROT = 16
FF = 3072
TOK_DEV = 1024
DOCS = 3
STEP = 10
TOKENS = 32768
VEC = 9984
N_SHARD = 4
N_DP = 8


def draw_vector_master(key, part):
    key = jax.random.fold_in(key, 7)
    gain_key, shift_key = jax.random.split(key)
    gain_part = 1.0 + 0.1 * jax.random.truncated_normal(gain_key, -5.0, 5.0, (2 * D,), jnp.float32)
    shift_part = 0.2 * jax.random.truncated_normal(shift_key, -5.0, 5.0, (7 * D + FF,), jnp.float32)
    return jnp.concatenate([gain_part[0:D], shift_part[0:D], gain_part[D:2 * D], shift_part[D:2 * D], shift_part[2 * D:]], 0)


def block_scale(key, dims, shards, low, top_value):
    factor_of = 1.0
    for dim, blocks in shards:
        draws = jax.random.uniform(jax.random.fold_in(jax.random.fold_in(key, 6), dim), (blocks,), jnp.float32, low / len(shards), top_value / len(shards))
        factor_of = factor_of * jnp.repeat(jnp.exp(draws), dims[dim] // blocks).reshape((-1,) + (1,) * (len(dims) - 1 - dim))
    return factor_of


def split_up(count, total, reach, skew):
    loads = [(1 << 20) // math.isqrt(rank ** skew) + 1 for rank in range(2, count + 1)]
    surplus, counts = total - reach - (count - 1), [1] * (count - 1)
    while surplus > 0:
        movable = [i for i in range(count - 1) if counts[i] < reach]
        pool, remaining = sum([loads[i] for i in movable]), surplus
        for i in movable:
            addition = min(reach - counts[i], max(1, remaining * loads[i] // pool), surplus)
            counts[i] = counts[i] + addition
            surplus = surplus - addition
    return np.array([reach] + counts)


def uneven(rng, amount, total, most, skew):
    if amount == 2:
        one = jax.random.randint(rng, (), max(1, total - most), min(most, total - 1) + 1)
        return jnp.stack([one, total - one])
    sizes = jnp.asarray(split_up(amount, total, most, skew), jnp.int32)
    pairs = (amount - 1) // 2
    source_of, taker = sizes[1:1 + 2 * pairs:2], sizes[2:2 + 2 * pairs:2]
    room = jnp.minimum(source_of - 1, most - taker)
    shifted = jax.random.randint(jax.random.fold_in(rng, 1), (pairs,), 0, 1 << 20) % (room + 1)
    sizes = sizes.at[1:1 + 2 * pairs:2].set(source_of - shifted).at[2:2 + 2 * pairs:2].set(taker + shifted)
    return sizes[jax.random.permutation(jax.random.fold_in(rng, 2), amount)]


def scatter_about(rng, shape, deviation, bound, cuts=(), held_as=jnp.bfloat16):
    factor_of = block_scale(rng, shape, cuts, -0.22, 0.18) if cuts else 1.0
    entries = jax.random.normal(rng, shape, jnp.float32) * deviation * factor_of
    return jnp.minimum(jnp.maximum(entries, -bound), bound).astype(held_as)


def setup_inputs(seed: int = 0) -> dict:
    streams_of = jax.random.split(jax.random.key(seed), 19)
    return {
        "tokens": scatter_about(streams_of[0], (TOKENS, D), 1.0, 6.0, ((0, 32),)),
        "lengths": jax.vmap(lambda own: uneven(own, DOCS, TOK_DEV, TOK_DEV * 3 // 4, 0))(jax.random.split(streams_of[1], (N_SHARD * N_DP))).reshape((N_SHARD * N_DP, DOCS)).astype(jnp.int32),
        "cotangent": scatter_about(streams_of[2], (TOKENS, D), 1.0, 6.0, ((0, 32),)),
        "heads_master": scatter_about(streams_of[3], (D, 3 * D), D ** -0.5, 0.21875, ((0, 4),), jnp.float32),
        "output_master": scatter_about(streams_of[4], (D, D), (D // 16) ** -0.5, 0.875, ((0, 4),), jnp.float32),
        "expand_master": scatter_about(streams_of[5], (D, FF), D ** -0.5, 0.21875, ((0, 4),), jnp.float32),
        "reduce_master": scatter_about(streams_of[6], (FF, D), FF ** -0.5, 0.109375, ((0, 4),), jnp.float32),
        "vector_master": draw_vector_master(jax.random.fold_in(streams_of[18], 71), 0),
        "heads_moment": scatter_about(streams_of[8], (D, 3 * D), (0.0556 * TOKENS ** 0.5), 64.0, ((0, 4),), jnp.float32),
        "output_moment": scatter_about(streams_of[9], (D, D), (0.0333 * TOKENS ** 0.5), 32.0, ((0, 4),), jnp.float32),
        "expand_moment": scatter_about(streams_of[10], (D, FF), (0.0333 * TOKENS ** 0.5), 32.0, ((0, 4),), jnp.float32),
        "reduce_moment": scatter_about(streams_of[11], (FF, D), (0.0667 * TOKENS ** 0.5), 64.0, ((0, 4),), jnp.float32),
        "vector_moment": scatter_about(streams_of[12], (VEC,), (0.111 * TOKENS ** 0.5), 128.0, ((0, 4),), jnp.float32),
        "heads_square": jnp.clip(jnp.exp(math.log(1723.5968) - 1.3824993 * jax.random.uniform(streams_of[13], (D, 3 * D), jnp.float32) ** block_scale(streams_of[13], (D, 3 * D), ((0, 4),), -0.2, 0.2)), 432.5376, 1723.5968),
        "output_square": jnp.clip(jnp.exp(math.log(622.592) - 1.3884019 * jax.random.uniform(streams_of[14], (D, D), jnp.float32) ** block_scale(streams_of[14], (D, D), ((0, 4),), -0.2, 0.2)), 155.32031, 622.592),
        "expand_square": jnp.clip(jnp.exp(math.log(622.592) - 1.3884019 * jax.random.uniform(streams_of[15], (D, FF), jnp.float32) ** block_scale(streams_of[15], (D, FF), ((0, 4),), -0.2, 0.2)), 155.32031, 622.592),
        "reduce_square": jnp.clip(jnp.exp(math.log(2483.8145) - 1.3889364 * jax.random.uniform(streams_of[16], (FF, D), jnp.float32) ** block_scale(streams_of[16], (FF, D), ((0, 4),), -0.2, 0.2)), 619.3152, 2483.8145),
        "vector_square": jnp.clip(jnp.exp(math.log(6881.28) - 1.3843914 * jax.random.uniform(streams_of[17], (VEC,), jnp.float32) ** block_scale(streams_of[17], (VEC,), ((0, 4),), -0.2, 0.2)), 1723.5968, 6881.28),
    }


first_decay = 0.9
second_decay = 0.95
adam_epsilon = 1e-08
matrix_decay = 0.1
matrix_rate = 0.04
vector_rate = 0.2
norm_epsilon = 1e-05
score_scale = 0.125
rotary_base = 10000.0
masked_score = -1e+30
highest = lax.Precision.HIGHEST

@jax.custom_vjp
def low(v):
    return lax.optimization_barrier(v.astype(jnp.bfloat16)).astype(jnp.float32)

@jax.custom_vjp
def low_back(v):
    return v

def low_keep(v):
    return (low(v), None)

def low_pass(kept, grad):
    return (grad,)

def back_keep(v):
    return (v, None)

def back_low(kept, grad):
    return (low(grad),)
low.defvjp(low_keep, low_pass)
low_back.defvjp(back_keep, back_low)

def layer_norm(values, gain, shift):
    row_mean = lax.optimization_barrier(jnp.mean(values, -1, keepdims=True))
    centred = values - row_mean
    row_var = lax.optimization_barrier(jnp.mean(centred * centred, -1, keepdims=True))
    return centred * lax.rsqrt(row_var + norm_epsilon) * gain + shift

def document_layout(lengths, token_count):
    places = jnp.arange(token_count, dtype=jnp.int32)
    lengths = lengths.astype(jnp.int32)
    bounds = jnp.cumsum(lengths).astype(jnp.int32)
    starts = bounds - lengths
    doc_index = lax.optimization_barrier(jnp.sum((places[:, None] >= bounds[None, :]).astype(jnp.int32), 1)).astype(jnp.int32)
    member = doc_index[:, None] == jnp.arange(lengths.shape[0], dtype=jnp.int32)[None, :]
    offset = lax.optimization_barrier(jnp.sum(jnp.where(member, starts[None, :], 0), 1)).astype(jnp.int32)
    return (doc_index, places - offset)

def rotary_tables(positions):
    steps_float = jnp.arange(ROT // 2, dtype=jnp.float32)
    inverse = rotary_base ** (-2.0 * steps_float / ROT)
    angles = positions.astype(jnp.float32)[:, None] * inverse[None, :]
    return (jnp.cos(angles)[:, None, :], jnp.sin(angles)[:, None, :])

def rotate(values, cosine, sine_table):
    half_width = ROT // 2
    first_half = values[..., :half_width]
    second_half = values[..., half_width:ROT]
    return jnp.concatenate([first_half * cosine - second_half * sine_table, second_half * cosine + first_half * sine_table, values[..., ROT:]], -1)

def device_forward(weights, vectors, source, lengths):
    heads_weight, output_weight, expand_weight, reduce_weight = weights
    token_count = source.shape[0]
    gain_one = vectors[0:D]
    shift_one = vectors[D:2 * D]
    gain_two = vectors[2 * D:3 * D]
    shift_two = vectors[3 * D:4 * D]
    heads_bias = vectors[4 * D:7 * D]
    output_bias = vectors[7 * D:8 * D]
    expand_bias = vectors[8 * D:8 * D + FF]
    reduce_bias = vectors[8 * D + FF:]
    doc_index, positions = document_layout(lengths, token_count)
    cosine, sine_table = rotary_tables(positions)
    normed_one = low(layer_norm(source, gain_one, shift_one))
    joint_rows = low_back(jnp.dot(normed_one, heads_weight, precision=highest) + heads_bias)
    queries = low(rotate(joint_rows[:, 0:D].reshape(token_count, HEADS, HEAD), cosine, sine_table))
    key_rows = low(rotate(joint_rows[:, D:2 * D].reshape(token_count, HEADS, HEAD), cosine, sine_table))
    value_rows = low(joint_rows[:, 2 * D:].reshape(token_count, HEADS, HEAD))
    block_rows = min(512, token_count)
    blocks = token_count // block_rows
    places = jnp.arange(token_count, dtype=jnp.int32)

    def attend(pieces):
        query_block, doc_block, place_block = pieces
        scores = low_back(jnp.einsum('qhe,khe->hqk', query_block, key_rows, precision=highest) * score_scale)
        allowed = (doc_block[:, None] == doc_index[None, :]) & (places[None, :] <= place_block[:, None])
        scores = jnp.where(allowed[None], scores, masked_score)
        row_top = lax.optimization_barrier(jnp.max(scores, -1, keepdims=True))
        exponent = jnp.exp(scores - row_top)
        soft_weights = low(exponent / lax.optimization_barrier(jnp.sum(exponent, -1, keepdims=True)))
        return jnp.einsum('hqk,khe->qhe', soft_weights, value_rows, precision=highest)
    context = lax.map(jax.checkpoint(attend), (queries.reshape(blocks, block_rows, HEADS, HEAD), doc_index.reshape(blocks, block_rows), places.reshape(blocks, block_rows)))
    context = low(low_back(context.reshape(token_count, D)))
    attention = jnp.dot(context, output_weight, precision=highest) + output_bias
    normed_two = low(layer_norm(source, gain_two, shift_two))
    hidden = low_back(jnp.dot(normed_two, expand_weight, precision=highest) + expand_bias)
    active = low(jax.nn.gelu(hidden, approximate=False))
    return source + attention + (jnp.dot(active, reduce_weight, precision=highest) + reduce_bias)

def adam_step(master, moment, square, gradient, rate, decay):
    momentum = first_decay * moment + (1.0 - first_decay) * gradient
    squares = second_decay * square + (1.0 - second_decay) * gradient * gradient
    first_fix = momentum / (1.0 - first_decay ** STEP)
    second_fix = squares / (1.0 - second_decay ** STEP)
    updated = master - rate * (first_fix / (jnp.sqrt(second_fix) + adam_epsilon) + decay * master)
    return (momentum, squares, updated)

def reference(tokens, lengths, cotangent, heads_master, output_master, expand_master, reduce_master, vector_master, heads_moment, output_moment, expand_moment, reduce_moment, vector_moment, heads_square, output_square, expand_square, reduce_square, vector_square):
    device_count = N_SHARD * N_DP
    rounded = (low(heads_master), low(output_master), low(expand_master), low(reduce_master))
    vectors = low(vector_master)
    sources = tokens.astype(jnp.float32).reshape(device_count, TOK_DEV, D)

    def forward(weights, vector_values, inputs):

        def one_device(pieces):
            return device_forward(weights, vector_values, pieces[0], pieces[1])
        return lax.map(jax.checkpoint(one_device), (inputs, lengths))
    outputs, pull = jax.vjp(forward, rounded, vectors, sources)
    weight_grads, vector_grad, input_grad = pull(cotangent.astype(jnp.float32).reshape(device_count, TOK_DEV, D))
    heads_new = adam_step(heads_master, heads_moment, heads_square, weight_grads[0], matrix_rate, matrix_decay)
    output_new = adam_step(output_master, output_moment, output_square, weight_grads[1], matrix_rate, matrix_decay)
    expand_new = adam_step(expand_master, expand_moment, expand_square, weight_grads[2], matrix_rate, matrix_decay)
    reduce_new = adam_step(reduce_master, reduce_moment, reduce_square, weight_grads[3], matrix_rate, matrix_decay)
    vector_new = adam_step(vector_master, vector_moment, vector_square, vector_grad, vector_rate, 0.0)
    block_output = outputs.reshape(TOKENS, D).astype(jnp.bfloat16)
    token_gradient = input_grad.reshape(TOKENS, D).astype(jnp.bfloat16)
    return (block_output, token_gradient, heads_new[0], heads_new[1], heads_new[2], output_new[0], output_new[1], output_new[2], expand_new[0], expand_new[1], expand_new[2], reduce_new[0], reduce_new[1], reduce_new[2], vector_new[0], vector_new[1], vector_new[2])
```

```python
import functools

import jax
import jax.numpy as jnp
from jax import lax
from jax.experimental import pallas as pl
from jax.experimental.pallas import tpu as pltpu
from jax.sharding import PartitionSpec as P

D = 768
HEADS = 12
HEAD = 64
ROT = 16
FF = 3072
STEP = 10
TOK = 1024
LONG = 768
BLK = 256

first_decay = 0.9
second_decay = 0.95
adam_epsilon = 1e-08
matrix_decay = 0.1
matrix_rate = 0.04
vector_rate = 0.2
norm_epsilon = 1e-05
score_scale = 0.125
rotary_base = 10000.0
masked_score = -1e30

f32=jnp.float32; bf16=jnp.bfloat16
LOG2E=1.4426950408889634
NN=(((1,),(0,)),((),())); NT=(((1,),(1,)),((),())); TN=(((0,),(0,)),((),())); TT=(((0,),(1,)),((),()))
def dot(a,b,dims=NN): return lax.dot_general(a,b,dims,preferred_element_type=f32)

def attn_kernel(n1_ref,n1T_ref,dy_ref,wq_ref,wk_ref,wv_ref,wo_ref,bq_ref,bk_ref,bv_ref,cos_ref,sin_ref,mask_ref,
                hh_ref,og_ref,bgq_ref,bgk_ref,bgv_ref,attn_ref,dn1T_ref, qT,kT,vT,oT,cT,gq,gk,gv):
    g=pl.program_id(0)
    heads=BLK//HEAD
    n1=n1_ref[...]
    cos=cos_ref[...]; sin=sin_ref[...]
    def proj(w_ref,b_ref): return dot(w_ref[...],n1,TT)+b_ref[...]
    def rot(x,sgn):
        parts=[]
        for h in range(heads):
            a=x[64*h:64*h+8]; b=x[64*h+8:64*h+16]
            s=sin*sgn
            parts+= [a*cos-b*s, b*cos+a*s, x[64*h+16:64*h+64]]
        return jnp.concatenate(parts,0)
    qT[...]=rot(proj(wq_ref,bq_ref),1.0).astype(bf16)
    kT[...]=rot(proj(wk_ref,bk_ref),1.0).astype(bf16)
    vT[...]=proj(wv_ref,bv_ref).astype(bf16)
    oT[...]=dot(wo_ref[...],dy_ref[...],NT).astype(bf16)
    krow=lax.broadcasted_iota(jnp.int32,(BLK,BLK),0); qcol=lax.broadcasted_iota(jnp.int32,(BLK,BLK),1)
    causal=krow<=qcol
    c=score_scale*LOG2E
    for h in range(heads):
        r=slice(64*h,64*h+64)
        QT=qT[r,:]; KT=kT[r,:]; VT=vT[r,:]; OT=oT[r,:]
        K=KT.T; V=VT.T
        nb=TOK//BLK
        dKT=[None]*nb; dVT=[None]*nb; dQTs=[]; cTs=[]
        for j in range(nb):
            qs=slice(BLK*j,BLK*j+BLK)
            kb0=0 if j<nb-1 else j
            kbs=list(range(kb0,j+1))
            q=QT[:,qs]; o=OT[:,qs]
            S=[dot(K[BLK*b:BLK*b+BLK],q)*c for b in kbs]
            if j<nb-1: S[-1]=jnp.where(causal,S[-1],-1e30)
            else: S[-1]=S[-1]+mask_ref[...]
            m=functools.reduce(jnp.maximum,[jnp.max(s,0,keepdims=True) for s in S])
            E=[jnp.exp2(s-m) for s in S]
            l=functools.reduce(jnp.add,[jnp.sum(e,0,keepdims=True) for e in E])
            inv=1.0/l
            P=[e*inv for e in E]
            Pb=[p.astype(bf16) for p in P]
            ct=functools.reduce(jnp.add,[dot(VT[:,BLK*b:BLK*b+BLK],p) for b,p in zip(kbs,Pb)])
            dP=[dot(V[BLK*b:BLK*b+BLK],o) for b in kbs]
            delta=functools.reduce(jnp.add,[jnp.sum(d*p,0,keepdims=True) for d,p in zip(dP,P)])
            dS=[(p*(d-delta)).astype(bf16) for d,p in zip(dP,P)]
            dq=functools.reduce(jnp.add,[dot(KT[:,BLK*b:BLK*b+BLK],s) for b,s in zip(kbs,dS)])
            cTs.append(ct.astype(bf16)); dQTs.append(dq*score_scale)
            for b,p,s in zip(kbs,Pb,dS):
                dk=dot(q,s,NT); dv=dot(o,p,NT)
                dKT[b]=dk if dKT[b] is None else dKT[b]+dk
                dVT[b]=dv if dVT[b] is None else dVT[b]+dv
        cT[r,:]=jnp.concatenate(cTs,1)
        def unrot(x):
            a=x[0:8]; b=x[8:16]
            return jnp.concatenate([a*cos+b*sin,b*cos-a*sin,x[16:64]],0)
        gq[r,:]=unrot(jnp.concatenate(dQTs,1)).astype(bf16)
        gk[r,:]=unrot(jnp.concatenate(dKT,1)*score_scale).astype(bf16)
        gv[r,:]=jnp.concatenate(dVT,1).astype(bf16)
    n1T=n1T_ref[...]
    dn=None
    for gr,w_ref,h_ref,b_ref in ((gq,wq_ref,hh_ref.at[0],bgq_ref),(gk,wk_ref,hh_ref.at[1],bgk_ref),(gv,wv_ref,hh_ref.at[2],bgv_ref)):
        G=gr[...]
        h_ref[...]=dot(n1T,G,NT)
        b_ref[...]=jnp.sum(G.astype(f32),1,keepdims=True)
        t=dot(w_ref[...],G)
        dn=t if dn is None else dn+t
    ctx=cT[...]
    og_ref[...]=dot(ctx,dy_ref[...])
    at=dot(ctx,wo_ref[...],TN)
    @pl.when(g==0)
    def _():
        attn_ref[...]=at; dn1T_ref[...]=dn
    @pl.when(g>0)
    def _():
        attn_ref[...]+=at; dn1T_ref[...]+=dn

def attention(n1,n1T,dy,W,Wo,bias_col,cos,sin,mask):
    G=D//BLK
    full=lambda s: pl.BlockSpec(s,lambda g:(0,0))
    wspec=lambda k: pl.BlockSpec((D,BLK),lambda g,k=k:(0,k*G+g))
    bspec=lambda k: pl.BlockSpec((BLK,1),lambda g,k=k:(k*G+g,0))
    hspec=pl.BlockSpec((3,D,BLK),lambda g:(0,0,g))
    col=pl.BlockSpec((BLK,1),lambda g:(g,0))
    return pl.pallas_call(attn_kernel,grid=(G,),
        in_specs=[full((TOK,D)),full((D,TOK)),full((TOK,D)),wspec(0),wspec(1),wspec(2),pl.BlockSpec((BLK,D),lambda g:(g,0)),
                  bspec(0),bspec(1),bspec(2),full((8,TOK)),full((8,TOK)),full((BLK,BLK))],
        out_specs=[hspec,pl.BlockSpec((BLK,D),lambda g:(g,0)),col,col,col,full((TOK,D)),full((D,TOK))],
        out_shape=[jax.ShapeDtypeStruct((3,D,D),f32),jax.ShapeDtypeStruct((D,D),f32)]+[jax.ShapeDtypeStruct((D,1),f32)]*3+
                  [jax.ShapeDtypeStruct((TOK,D),f32),jax.ShapeDtypeStruct((D,TOK),f32)],
        scratch_shapes=[pltpu.VMEM((BLK,TOK),bf16)]*8,
        compiler_params=pltpu.CompilerParams(vmem_limit_bytes=60<<20),
        )(n1,n1T,dy,W,W,W,Wo,bias_col,bias_col,bias_col,cos,sin,mask)

def erf_parts(h):
    e=jnp.exp2(h*h*(-0.5*LOG2E))
    return 0.5*(1.0+lax.erf(h*0.7071067811865476)), e*0.3989422804014327

def ffn_kernel(n2_ref,n2T_ref,dy_ref,we_ref,wr_ref,be_ref,eg_ref,rg_ref,bge_ref,out_ref,dn2_ref):
    g=pl.program_id(0)
    we=we_ref[0]; wr=wr_ref[0]
    h=dot(n2_ref[...],we)+be_ref[0]
    Phi,phi=erf_parts(h)
    act=(h*Phi).astype(bf16)
    da=dot(dy_ref[...],wr,NT)
    dh=(da*(Phi+h*phi)).astype(bf16)
    bge_ref[0]=jnp.sum(dh.astype(f32),0,keepdims=True)
    rg_ref[0]=dot(act,dy_ref[...],TN)
    eg_ref[0]=dot(n2T_ref[...],dh)
    o=dot(act,wr); d=dot(dh,we,NT)
    @pl.when(g==0)
    def _():
        out_ref[...]=o; dn2_ref[...]=d
    @pl.when(g>0)
    def _():
        out_ref[...]+=o; dn2_ref[...]+=d

def ffn(n2,n2T,dy,We,Wr,be):
    G,_,FC=We.shape
    full=lambda s: pl.BlockSpec(s,lambda g:(0,0))
    we=pl.BlockSpec((1,D,FC),lambda g:(g,0,0)); wr=pl.BlockSpec((1,FC,D),lambda g:(g,0,0)); b=pl.BlockSpec((1,1,FC),lambda g:(g,0,0))
    S=jax.ShapeDtypeStruct
    return pl.pallas_call(ffn_kernel,grid=(G,),
        in_specs=[full((TOK,D)),full((D,TOK)),full((TOK,D)),we,wr,b],
        out_specs=[we,wr,b,full((TOK,D)),full((TOK,D))],
        out_shape=[S((G,D,FC),f32),S((G,FC,D),f32),S((G,1,FC),f32),S((TOK,D),f32),S((TOK,D),f32)],
        compiler_params=pltpu.CompilerParams(vmem_limit_bytes=60<<20),
        )(n2,n2T,dy,We,Wr,be)


MESH=pl.DeviceIdType.MESH

def place():
    s=lax.axis_index("shard"); d=lax.axis_index("dp")
    c=d%2
    s1=s+1-2*(s%2); s2=s+2-4*(s//2)
    a=(1-c)*s1+c*s2
    b=(1-c)*s2+c*s1
    return s,d,c,a,b

def rcopy(src,dst,ssem,rsem,sh,dp):
    return pltpu.make_async_remote_copy(src_ref=src,dst_ref=dst,send_sem=ssem,recv_sem=rsem,device_id=(sh,dp),device_id_type=MESH)

def greet(peers):
    bar=pltpu.get_barrier_semaphore()
    for sh,dp in peers:
        pl.semaphore_signal(bar,inc=1,device_id=(sh,dp),device_id_type=MESH)
    pl.semaphore_wait(bar,len(peers))

class Gather:
    def __init__(self,own,full,ssem,rsem,lsem,split=True):
        self.own,self.full,self.ss,self.rs,self.ls=own,full,ssem,rsem,lsem
        self.s,self.d,self.c,self.a,self.b=place()
        self.sib=self.d+1-2*self.c
        self.R=own.shape[-2]; self.split=split
        self.h=self.R//2 if split else self.R
    def sl(self,ref,row,n):
        row=pl.multiple_of(row,16)
        if len(ref.shape)==2: return ref.at[pl.ds(row,n)]
        return ref.at[:,pl.ds(row,n)]
    def region(self,sh,core):
        return self.sl(self.full,sh*self.R+(core*self.h if self.split else 0),self.h)
    def mine(self):
        return self.sl(self.own,self.c*self.h if self.split else 0,self.h)
    def cp(self,k,src,reg,sh,dp): return rcopy(src,reg,self.ss.at[k],self.rs.at[k],sh,dp)
    def local(self):
        return pltpu.make_async_copy(self.own,self.sl(self.full,self.s*self.R,self.R),self.ls)
    def start(self):
        r=self.region(self.s,self.c)
        self.cp(0,self.mine(),r,self.a,self.d).start()
        self.cp(1,self.mine(),r,self.b,self.d).start()
        self.local().start()
    def _wait_recv(self,k,sh,core):
        r=self.region(sh,core)
        self.cp(k,r,r,self.s,self.sib).wait_recv()
    def _wait_send(self,k,sh,core):
        r=self.region(sh,core)
        self.cp(k,r,r,self.s,self.sib).wait_send()
    def forward(self):
        ra=self.region(self.a,self.c)
        self._wait_recv(0,self.a,self.c)
        self.cp(2,ra,ra,self.b,self.d).start()
        if self.split: self.cp(3,ra,ra,self.s,self.sib).start()
        self._wait_recv(1,self.b,self.c)
        rb=self.region(self.b,self.c)
        if self.split: self.cp(4,rb,rb,self.s,self.sib).start()
    def diag(self):
        x=3-self.s
        self._wait_recv(2,x,self.c)
        rx=self.region(x,self.c)
        if self.split: self.cp(5,rx,rx,self.s,self.sib).start()
    def finish(self):
        self.local().wait()
        x=3-self.s
        if self.split:
            o=1-self.c
            self._wait_recv(3,self.b,o)
            self._wait_recv(4,self.a,o)
            self._wait_recv(5,x,o)
        self.cp(0,self.mine(),self.region(self.s,self.c),self.a,self.d).wait_send()
        self.cp(1,self.mine(),self.region(self.s,self.c),self.b,self.d).wait_send()
        for k,sh in ((2,self.a),)+(((3,self.a),(4,self.b),(5,x)) if self.split else ()):
            self._wait_send(k,sh,self.c)

def gather_peers():
    s,d,c,a,b=place()
    return [(a,d),(b,d),(s,d+1-2*c)]

def gather_kernel(n,splits,*refs):
    own=refs[:n]; full=refs[n:2*n]; ss,rs,ls=refs[2*n:]
    g=[Gather(own[i],full[i],ss.at[i],rs.at[i],ls.at[i],splits[i]) for i in range(n)]
    greet(gather_peers())
    for t in g: t.start()
    g[0].forward()
    for i in range(1,n):
        g[i].forward()
        g[i-1].diag()
    g[n-1].diag()
    for t in g: t.finish()

def gather(arrs,splits,cid):
    n=len(arrs)
    def fullshape(a):
        sh=list(a.shape); sh[-2]*=4; return jax.ShapeDtypeStruct(tuple(sh),a.dtype)
    anyspec=pl.BlockSpec(memory_space=pl.ANY)
    return pl.pallas_call(functools.partial(gather_kernel,n,splits),
        in_specs=[pl.BlockSpec(memory_space=pltpu.VMEM)]*n,out_specs=[anyspec]*n,out_shape=[fullshape(a) for a in arrs],
        scratch_shapes=[pltpu.SemaphoreType.DMA((n,6)),pltpu.SemaphoreType.DMA((n,6)),pltpu.SemaphoreType.DMA((n,))],
        compiler_params=pltpu.CompilerParams(collective_id=cid,has_side_effects=True,vmem_limit_bytes=40<<20))(*arrs)

def ring_of(dp_size):
    digits=[]; n=dp_size//2; stride=1
    while n>1:
        assert n%4==0
        digits.append(stride); stride*=4; n//=4
    return digits

class Reduce:
    def __init__(self,digits,mine,other,Y,SA,RA,T,SB,RB,SZ,RZ,RM,gout,ss,rs):
        self.digits=digits; self.mine=mine; self.other=other
        self.Y,self.SA,self.RA,self.T,self.SB,self.RB,self.SZ,self.RZ,self.RM,self.gout,self.ss,self.rs=Y,SA,RA,T,SB,RB,SZ,RZ,RM,gout,ss,rs
        self.s,self.d,self.c,self.a,self.b=place()
        self.sib=self.d+1-2*self.c
        self.x=3-self.s
    def cp(self,j,k,src,dst,sh,dp): return rcopy(src,dst,self.ss.at[j,k],self.rs.at[j,k],sh,dp)
    def role(self,i):
        st=self.digits[i]; p=((self.d//2)//st)%4
        end=(p==0)|(p==3)
        mate=self.d+2*st*jnp.where(p==0,1,jnp.where(p==3,-1,jnp.where(p==1,1,-1)))
        tip=self.d+2*st*jnp.where(p==1,-1,1)
        return end,mate,tip
    def stages(self): return 4+3*len(self.digits)+1
    def c0(self,k): return self.cp(0,k,self.other(k),self.Y.at[k],self.s,self.sib)
    def cA(self,k): return self.cp(1,k,self.SA.at[k],self.RA.at[k],self.a,self.d)
    def cB(self,k): return self.cp(2,k,self.SB.at[k],self.RB.at[k],self.b,self.d)
    def nt(self,k): return k%self.T.shape[0]
    def s0(self,k):
        self.c0(k).start()
    def s1(self,k):
        self.c0(k).wait()
        X=self.mine(k)
        def U(p): return X[p]+self.Y[k,p]
        self.SA[k,0]=U(self.a).astype(self.SA.dtype)
        self.SA[k,1]=U(self.x).astype(self.SA.dtype)
        self.cA(k).start()
        t=self.nt(k)
        self.T[t,0]=U(self.s)
        self.T[t,1]=U(self.b)
    def s2(self,k):
        self.cA(k).wait()
        t=self.nt(k)
        self.SB[k]=(self.T[t,1]+self.RA[k,1].astype(f32)).astype(self.SB.dtype)
        self.cB(k).start()
        self.T[t,0]=self.T[t,0]+self.RA[k,0].astype(f32)
    def s3(self,k):
        self.cB(k).wait()
        t=self.nt(k)
        self.T[t,0]=self.T[t,0]+self.RB[k].astype(f32)
        self.za(0,k)
    def g(self,k): return self.gout.at[k,self.c]
    def zcp(self,i,j,k,src,dst,dp): return self.cp(3+4*i+j,k,src,dst,self.s,dp)
    def za(self,i,k):
        t=self.nt(k); end,mate,tip=self.role(i)
        @pl.when(end)
        def _():
            self.SZ[i,k]=self.T[t,0].astype(self.SZ.dtype)
            self.zcp(i,0,k,self.SZ.at[i,k],self.RZ.at[i,k],mate).start()
    def zb(self,i,k):
        t=self.nt(k); end,mate,tip=self.role(i)
        @pl.when(jnp.logical_not(end))
        def _():
            self.zcp(i,0,k,self.SZ.at[i,k],self.RZ.at[i,k],tip).wait_recv()
            self.SZ[i,k]=(self.T[t,0]+self.RZ[i,k].astype(f32)).astype(self.SZ.dtype)
            self.zcp(i,1,k,self.SZ.at[i,k],self.RM.at[i,k],mate).start()
        @pl.when(end)
        def _():
            self.zcp(i,0,k,self.SZ.at[i,k],self.RZ.at[i,k],mate).wait_send()
    def to_sib(self,k):
        return self.cp(3+4*len(self.digits),k,self.g(k),self.g(k),self.s,self.sib)
    def zc(self,i,k):
        end,mate,tip=self.role(i); last=i==len(self.digits)-1
        @pl.when(jnp.logical_not(end))
        def _():
            self.zcp(i,1,k,self.SZ.at[i,k],self.RM.at[i,k],mate).wait()
            self.gout[k,self.c]=(self.SZ[i,k].astype(f32)+self.RM[i,k].astype(f32)).astype(self.gout.dtype)
            self.zcp(i,2,k,self.g(k),self.g(k),tip).start()
            if last: self.to_sib(k).start()
    def zd(self,i,k):
        end,mate,tip=self.role(i); last=i==len(self.digits)-1
        @pl.when(jnp.logical_not(end))
        def _():
            self.zcp(i,2,k,self.g(k),self.g(k),tip).wait_send()
        @pl.when(end)
        def _():
            self.zcp(i,2,k,self.g(k),self.g(k),mate).wait_recv()
            if last: self.to_sib(k).start()
        if not last:
            self.T[self.nt(k),0]=self.gout[k,self.c].astype(f32)
            self.za(i+1,k)
    def fin(self,k):
        self.to_sib(k).wait_send()
        g=self.gout.at[k,1-self.c]
        self.cp(3+4*len(self.digits),k,g,g,self.s,self.sib).wait_recv()
    def stage_list(self):
        out=[self.s0,self.s1,self.s2,self.s3]
        for i in range(len(self.digits)):
            out+=[functools.partial(self.zb,i),functools.partial(self.zc,i),functools.partial(self.zd,i)]
        return out+[self.fin]

def reduce_peers(digits):
    s,d,c,a,b=place()
    peers=[(a,d),(b,d),(s,d+1-2*c)]
    for st in digits:
        p=((d//2)//st)%4
        up=d+2*st*jnp.where(p==3,-3,1); down=d+2*st*jnp.where(p==0,3,-1)
        peers+=[(s,up),(s,down)]
    return peers

def stream_scratch(n,r,w,nd,nt,mt):
    V=pltpu.VMEM; S=pltpu.SemaphoreType.DMA
    return [V((n,4,r,w),f32),V((n,2,r,w),mt),V((n,2,r,w),mt),V((nt,2,r,w),f32),V((n,r,w),mt),V((n,r,w),mt),
            V((nd,n,r,w),mt),V((nd,n,r,w),mt),V((nd,n,r,w),mt),S((4+4*nd,n)),S((4+4*nd,n))]

def reduce_kernel(digits,ns,*refs):
    m=len(ns); srcs=refs[:m]; gouts=refs[m:2*m]; rest=refs[2*m:]
    streams=[]; per=13
    loads=[]
    for i in range(m):
        r=rest[i*per:(i+1)*per]; X,ls=r[11],r[12]
        c=place()[2]
        src=srcs[i]
        def load(k,src=src,X=X,ls=ls,c=c): return pltpu.make_async_copy(src.at[k,:,c],X.at[k%2],ls.at[k])
        loads.append(load)
        def mine(k,X=X): return X.at[k%2]
        def other(k,src=src,c=c): return src.at[k,:,1-c]
        streams.append(Reduce(digits,mine,other,*r[:9],gouts[i],r[9],r[10]))
    greet(reduce_peers(digits))
    nst=len(streams[0].stage_list())
    order=[]
    for t in range(max(ns)):
        for i in range(m):
            if t<ns[i]: order.append((i,t))
    for t in range(len(order)+nst-1):
        for j in range(nst):
            if 0<=t-j<len(order):
                i,k=order[t-j]
                if j==0: loads[i](k).start()
                if j==1: loads[i](k).wait()
                streams[i].stage_list()[j](k)

def reduce(arrs,types,sums,digits,cid):
    ns=[a.shape[0] for a in arrs]; nd=len(digits)
    anyspec=pl.BlockSpec(memory_space=pl.ANY)
    scratch=[]
    for a,mt in zip(arrs,types):
        n,_,_,r,w=a.shape
        scratch+=stream_scratch(n,r,w,nd,n,mt)+[pltpu.VMEM((2,4,r,w),f32),pltpu.SemaphoreType.DMA((n,))]
    return pl.pallas_call(functools.partial(reduce_kernel,digits,ns),
        in_specs=[anyspec]*len(arrs),out_specs=[pl.BlockSpec(memory_space=pltpu.VMEM)]*len(arrs),
        out_shape=[jax.ShapeDtypeStruct((a.shape[0],2)+a.shape[3:],t) for a,t in zip(arrs,sums)],
        scratch_shapes=scratch,
        compiler_params=pltpu.CompilerParams(collective_id=cid,has_side_effects=True,vmem_limit_bytes=60<<20))(*arrs)


def layer_norm(values, gain, shift):
    row_mean = jnp.mean(values, -1, keepdims=True)
    centred = values - row_mean
    row_var = jnp.mean(centred * centred, -1, keepdims=True)
    return centred * lax.rsqrt(row_var + norm_epsilon) * gain + shift


def adam_step(master, moment, square, gradient, rate, decay):
    momentum = first_decay * moment + (1.0 - first_decay) * gradient
    squares = second_decay * square + (1.0 - second_decay) * gradient * gradient
    first_fix = momentum / (1.0 - first_decay**STEP)
    second_fix = squares / (1.0 - second_decay**STEP)
    updated = master - rate * (first_fix / (jnp.sqrt(second_fix) + adam_epsilon) + decay * master)
    return (momentum, squares, updated)


def per_device(
    tokens,
    lengths,
    cotangent,
    heads_master,
    output_master,
    expand_master,
    reduce_master,
    vector_master,
    heads_moment,
    output_moment,
    expand_moment,
    reduce_moment,
    vector_moment,
    heads_square,
    output_square,
    expand_square,
    reduce_square,
    vector_square,
):
    chunks = FF // 4 // 128
    cast = lambda part: part.astype(jnp.bfloat16)
    expand_own = cast(expand_master).reshape(D // 4, 4, chunks, 128).transpose(2, 0, 1, 3).reshape(chunks, D // 4, 512)
    reduce_own = cast(reduce_master).reshape(chunks, 128, D)
    vector_own = jnp.pad(cast(vector_master).reshape(16, 156), ((0, 0), (0, 100)))
    vector_full, heads_weight, output_weight, expand_weight, reduce_weight = gather(
        [vector_own, cast(heads_master), cast(output_master), expand_own, reduce_own], [False, True, True, True, True], 1)
    vectors = vector_full.reshape(4, 16, 256)[:, :, :156].reshape(-1).astype(jnp.float32)
    gain_one = vectors[0:D]
    shift_one = vectors[D : 2 * D]
    gain_two = vectors[2 * D : 3 * D]
    shift_two = vectors[3 * D : 4 * D]
    heads_bias = vectors[4 * D : 7 * D]
    output_bias = vectors[7 * D : 8 * D]
    expand_bias = vectors[8 * D : 8 * D + FF]
    reduce_bias = vectors[8 * D + FF :]
    own = lengths[0]
    ends = jnp.cumsum(own)
    which = jnp.argmax(own)
    start = ends[which] - LONG
    short = own[(which + 1) % 3]
    dy = jnp.roll(cotangent, -start, 0)
    source = jnp.roll(tokens, -start, 0).astype(jnp.float32)
    row = jnp.arange(TOK, dtype=jnp.int32)
    position = jnp.where(row < LONG, row, row - LONG - jnp.where(row - LONG >= short, short, 0))
    inverse = rotary_base ** (-2.0 * jnp.arange(ROT // 2, dtype=jnp.float32) / ROT)
    angles = position.astype(jnp.float32)[None, :] * inverse[:, None]
    small = jnp.arange(BLK, dtype=jnp.int32)
    second = small >= short
    allowed = (second[:, None] == second[None, :]) & (small[:, None] <= small[None, :])
    mask = jnp.where(allowed, 0.0, masked_score).astype(jnp.float32)
    norm_one_out, norm_one_pull = jax.vjp(layer_norm, source, gain_one, shift_one)
    normed_one = norm_one_out.astype(jnp.bfloat16)
    norm_two_out, norm_two_pull = jax.vjp(layer_norm, source, gain_two, shift_two)
    normed_two = norm_two_out.astype(jnp.bfloat16)
    (heads_grad, output_grad, bq, bk, bv, attention_out, norm_one_gradT) = attention(
        normed_one, normed_one.T, dy, heads_weight, output_weight, heads_bias[:, None], jnp.cos(angles), jnp.sin(angles), mask)
    expand_grad, reduce_grad, expand_bias_grad, feed_out, norm_two_grad = ffn(
        normed_two, normed_two.T, dy, expand_weight, reduce_weight,
        expand_bias.reshape(4, chunks, 128).transpose(1, 0, 2).reshape(chunks, 1, 512))
    block_output = jnp.roll((source + (attention_out + output_bias) + (feed_out + reduce_bias)).astype(jnp.bfloat16), start, 0)
    upstream = dy.astype(jnp.float32)
    upstream_sum = jnp.sum(upstream, 0)
    source_one, gain_one_grad, shift_one_grad = norm_one_pull(norm_one_gradT.T)
    source_two, gain_two_grad, shift_two_grad = norm_two_pull(norm_two_grad)
    token_gradient = jnp.roll((upstream + source_one + source_two).astype(jnp.bfloat16), start, 0)
    vector_grad = jnp.concatenate(
        [gain_one_grad, shift_one_grad, gain_two_grad, shift_two_grad, bq[:, 0], bk[:, 0], bv[:, 0], upstream_sum,
         expand_bias_grad.reshape(chunks, 4, 128).transpose(1, 0, 2).reshape(-1), upstream_sum], 0)
    vector_parts = jnp.pad(vector_grad.reshape(4, 2, 1248), ((0, 0), (0, 0), (0, 800))).reshape(1, 4, 2, 16, 128)
    heads_sum, output_sum, expand_sum, reduce_sum, vector_sum = reduce(
        [heads_grad.reshape(3, 4, 2, 96, D), output_grad.reshape(1, 4, 2, 96, D), expand_grad.reshape(chunks, 4, 2, 96, 512),
         reduce_grad.reshape(chunks, 4, 2, 64, D), vector_parts],
        [bf16, bf16, bf16, bf16, f32], [f32, f32, bf16, bf16, f32], ring_of(lax.axis_size("dp")), 2)
    heads_owned = heads_sum.reshape(3, D // 4, D).transpose(1, 0, 2).reshape(D // 4, 3 * D).astype(jnp.float32)
    output_owned = output_sum.reshape(D // 4, D).astype(jnp.float32)
    expand_owned = expand_sum.reshape(chunks, D // 4, 4, 128).transpose(1, 2, 0, 3).reshape(D // 4, FF).astype(jnp.float32)
    reduce_owned = reduce_sum.reshape(FF // 4, D).astype(jnp.float32)
    vector_owned = vector_sum.reshape(2, 2048)[:, :1248].reshape(-1)
    heads_new = adam_step(
        heads_master, heads_moment, heads_square, heads_owned, matrix_rate, matrix_decay
    )
    output_new = adam_step(
        output_master, output_moment, output_square, output_owned, matrix_rate, matrix_decay
    )
    expand_new = adam_step(
        expand_master, expand_moment, expand_square, expand_owned, matrix_rate, matrix_decay
    )
    reduce_new = adam_step(
        reduce_master, reduce_moment, reduce_square, reduce_owned, matrix_rate, matrix_decay
    )
    vector_new = adam_step(
        vector_master, vector_moment, vector_square, vector_owned, vector_rate, 0.0
    )
    return (
        block_output,
        token_gradient,
        heads_new[0],
        heads_new[1],
        heads_new[2],
        output_new[0],
        output_new[1],
        output_new[2],
        expand_new[0],
        expand_new[1],
        expand_new[2],
        reduce_new[0],
        reduce_new[1],
        reduce_new[2],
        vector_new[0],
        vector_new[1],
        vector_new[2],
    )


def solution(mesh):
    placed = (
        P(("shard", "dp"), None),
        P(("shard", "dp"), None),
        P(("shard", "dp"), None),
        P("shard", None),
        P("shard", None),
        P("shard", None),
        P("shard", None),
        P("shard"),
        P("shard", None),
        P("shard", None),
        P("shard", None),
        P("shard", None),
        P("shard"),
        P("shard", None),
        P("shard", None),
        P("shard", None),
        P("shard", None),
        P("shard"),
    )
    return jax.shard_map(
        per_device,
        mesh=mesh,
        in_specs=placed,
        out_specs=(
            P(("shard", "dp"), None),
            P(("shard", "dp"), None),
            P("shard", None),
            P("shard", None),
            P("shard", None),
            P("shard", None),
            P("shard", None),
            P("shard", None),
            P("shard", None),
            P("shard", None),
            P("shard", None),
            P("shard", None),
            P("shard", None),
            P("shard", None),
            P("shard"),
            P("shard"),
            P("shard"),
        ),
        check_vma=False,
    )
```

```python
import functools

import jax
import jax.numpy as jnp
from jax import lax
from jax.experimental import pallas as pl
from jax.experimental.pallas import tpu as pltpu
from jax.sharding import PartitionSpec as P

D = 768
HEADS = 12
HEAD = 64
ROT = 16
FF = 3072
STEP = 10
TOK = 1024
LONG = 768
BLK = 256

first_decay = 0.9
second_decay = 0.95
adam_epsilon = 1e-08
matrix_decay = 0.1
matrix_rate = 0.04
vector_rate = 0.2
norm_epsilon = 1e-05
score_scale = 0.125
rotary_base = 10000.0
masked_score = -1e30

f32=jnp.float32; bf16=jnp.bfloat16
LOG2E=1.4426950408889634
NN=(((1,),(0,)),((),())); NT=(((1,),(1,)),((),())); TN=(((0,),(0,)),((),())); TT=(((0,),(1,)),((),()))
def dot(a,b,dims=NN): return lax.dot_general(a,b,dims,preferred_element_type=f32)

MESH=pl.DeviceIdType.MESH

def place():
    s=lax.axis_index("shard"); d=lax.axis_index("dp")
    c=d%2
    s1=s+1-2*(s%2); s2=s+2-4*(s//2)
    a=(1-c)*s1+c*s2
    b=(1-c)*s2+c*s1
    return s,d,c,a,b

def rcopy(src,dst,ssem,rsem,sh,dp):
    return pltpu.make_async_remote_copy(src_ref=src,dst_ref=dst,send_sem=ssem,recv_sem=rsem,device_id=(sh,dp),device_id_type=MESH)

def greet(peers):
    bar=pltpu.get_barrier_semaphore()
    for sh,dp in peers:
        pl.semaphore_signal(bar,inc=1,device_id=(sh,dp),device_id_type=MESH)
    pl.semaphore_wait(bar,len(peers))

class Gather:
    def __init__(self,own,full,ssem,rsem,lsem,split=True):
        self.own,self.full,self.ss,self.rs,self.ls=own,full,ssem,rsem,lsem
        self.s,self.d,self.c,self.a,self.b=place()
        self.sib=self.d+1-2*self.c
        self.R=own.shape[-2]; self.split=split
        self.h=self.R//2 if split else self.R
    def sl(self,ref,row,n):
        row=pl.multiple_of(row,16)
        if len(ref.shape)==2: return ref.at[pl.ds(row,n)]
        return ref.at[:,pl.ds(row,n)]
    def region(self,sh,core):
        return self.sl(self.full,sh*self.R+(core*self.h if self.split else 0),self.h)
    def mine(self):
        return self.sl(self.own,self.c*self.h if self.split else 0,self.h)
    def cp(self,k,src,reg,sh,dp): return rcopy(src,reg,self.ss.at[k],self.rs.at[k],sh,dp)
    def local(self):
        return pltpu.make_async_copy(self.own,self.sl(self.full,self.s*self.R,self.R),self.ls)
    def start(self):
        r=self.region(self.s,self.c)
        self.cp(0,self.mine(),r,self.a,self.d).start()
        self.cp(1,self.mine(),r,self.b,self.d).start()
        self.local().start()
    def _wait_recv(self,k,sh,core):
        r=self.region(sh,core)
        self.cp(k,r,r,self.s,self.sib).wait_recv()
    def _wait_send(self,k,sh,core):
        r=self.region(sh,core)
        self.cp(k,r,r,self.s,self.sib).wait_send()
    def forward(self):
        ra=self.region(self.a,self.c)
        self._wait_recv(0,self.a,self.c)
        self.cp(2,ra,ra,self.b,self.d).start()
        if self.split: self.cp(3,ra,ra,self.s,self.sib).start()
        self._wait_recv(1,self.b,self.c)
        rb=self.region(self.b,self.c)
        if self.split: self.cp(4,rb,rb,self.s,self.sib).start()
    def diag(self):
        x=3-self.s
        self._wait_recv(2,x,self.c)
        rx=self.region(x,self.c)
        if self.split: self.cp(5,rx,rx,self.s,self.sib).start()
    def finish(self):
        self.local().wait()
        x=3-self.s
        if self.split:
            o=1-self.c
            self._wait_recv(3,self.b,o)
            self._wait_recv(4,self.a,o)
            self._wait_recv(5,x,o)
        self.cp(0,self.mine(),self.region(self.s,self.c),self.a,self.d).wait_send()
        self.cp(1,self.mine(),self.region(self.s,self.c),self.b,self.d).wait_send()
        for k,sh in ((2,self.a),)+(((3,self.a),(4,self.b),(5,x)) if self.split else ()):
            self._wait_send(k,sh,self.c)

def gather_peers():
    s,d,c,a,b=place()
    return [(a,d),(b,d),(s,d+1-2*c)]

def gather_kernel(n,splits,*refs):
    own=refs[:n]; full=refs[n:2*n]; ss,rs,ls=refs[2*n:]
    g=[Gather(own[i],full[i],ss.at[i],rs.at[i],ls.at[i],splits[i]) for i in range(n)]
    greet(gather_peers())
    for t in g: t.start()
    g[0].forward()
    for i in range(1,n):
        g[i].forward()
        g[i-1].diag()
    g[n-1].diag()
    for t in g: t.finish()

def gather(arrs,splits,cid):
    n=len(arrs)
    def fullshape(a):
        sh=list(a.shape); sh[-2]*=4; return jax.ShapeDtypeStruct(tuple(sh),a.dtype)
    anyspec=pl.BlockSpec(memory_space=pl.ANY)
    return pl.pallas_call(functools.partial(gather_kernel,n,splits),
        in_specs=[pl.BlockSpec(memory_space=pltpu.VMEM)]*n,out_specs=[anyspec]*n,out_shape=[fullshape(a) for a in arrs],
        scratch_shapes=[pltpu.SemaphoreType.DMA((n,6)),pltpu.SemaphoreType.DMA((n,6)),pltpu.SemaphoreType.DMA((n,))],
        compiler_params=pltpu.CompilerParams(collective_id=cid,has_side_effects=True,vmem_limit_bytes=40<<20))(*arrs)

def ring_of(dp_size):
    digits=[]; n=dp_size//2; stride=1
    while n>1:
        assert n%4==0
        digits.append(stride); stride*=4; n//=4
    return digits

class Reduce:
    def __init__(self,digits,mine,other,Y,SA,RA,T,SB,RB,SZ,RZ,RM,gout,ss,rs):
        self.digits=digits; self.mine=mine; self.other=other
        self.Y,self.SA,self.RA,self.T,self.SB,self.RB,self.SZ,self.RZ,self.RM,self.gout,self.ss,self.rs=Y,SA,RA,T,SB,RB,SZ,RZ,RM,gout,ss,rs
        self.s,self.d,self.c,self.a,self.b=place()
        self.sib=self.d+1-2*self.c
        self.x=3-self.s
    def cp(self,j,k,src,dst,sh,dp): return rcopy(src,dst,self.ss.at[j,k],self.rs.at[j,k],sh,dp)
    def role(self,i):
        st=self.digits[i]; p=((self.d//2)//st)%4
        end=(p==0)|(p==3)
        mate=self.d+2*st*jnp.where(p==0,1,jnp.where(p==3,-1,jnp.where(p==1,1,-1)))
        tip=self.d+2*st*jnp.where(p==1,-1,1)
        return end,mate,tip
    def stages(self): return 4+3*len(self.digits)+1
    def c0(self,k): return self.cp(0,k,self.other(k),self.Y.at[k],self.s,self.sib)
    def cA(self,k): return self.cp(1,k,self.SA.at[k],self.RA.at[k],self.a,self.d)
    def cB(self,k): return self.cp(2,k,self.SB.at[k],self.RB.at[k],self.b,self.d)
    def nt(self,k): return k%self.T.shape[0]
    def s0(self,k):
        self.c0(k).start()
    def s1(self,k):
        self.c0(k).wait()
        X=self.mine(k)
        def U(p): return X[p]+self.Y[k,p]
        self.SA[k,0]=U(self.a).astype(self.SA.dtype)
        self.SA[k,1]=U(self.x).astype(self.SA.dtype)
        self.cA(k).start()
        t=self.nt(k)
        self.T[t,0]=U(self.s)
        self.T[t,1]=U(self.b)
    def s2(self,k):
        self.cA(k).wait()
        t=self.nt(k)
        self.SB[k]=(self.T[t,1]+self.RA[k,1].astype(f32)).astype(self.SB.dtype)
        self.cB(k).start()
        self.T[t,0]=self.T[t,0]+self.RA[k,0].astype(f32)
    def s3(self,k):
        self.cB(k).wait()
        t=self.nt(k)
        self.T[t,0]=self.T[t,0]+self.RB[k].astype(f32)
        self.za(0,k)
    def g(self,k): return self.gout.at[k,self.c]
    def zcp(self,i,j,k,src,dst,dp): return self.cp(3+4*i+j,k,src,dst,self.s,dp)
    def za(self,i,k):
        t=self.nt(k); end,mate,tip=self.role(i)
        @pl.when(end)
        def _():
            self.SZ[i,k]=self.T[t,0].astype(self.SZ.dtype)
            self.zcp(i,0,k,self.SZ.at[i,k],self.RZ.at[i,k],mate).start()
    def zb(self,i,k):
        t=self.nt(k); end,mate,tip=self.role(i)
        @pl.when(jnp.logical_not(end))
        def _():
            self.zcp(i,0,k,self.SZ.at[i,k],self.RZ.at[i,k],tip).wait_recv()
            self.SZ[i,k]=(self.T[t,0]+self.RZ[i,k].astype(f32)).astype(self.SZ.dtype)
            self.zcp(i,1,k,self.SZ.at[i,k],self.RM.at[i,k],mate).start()
        @pl.when(end)
        def _():
            self.zcp(i,0,k,self.SZ.at[i,k],self.RZ.at[i,k],mate).wait_send()
    def to_sib(self,k):
        return self.cp(3+4*len(self.digits),k,self.g(k),self.g(k),self.s,self.sib)
    def zc(self,i,k):
        end,mate,tip=self.role(i); last=i==len(self.digits)-1
        @pl.when(jnp.logical_not(end))
        def _():
            self.zcp(i,1,k,self.SZ.at[i,k],self.RM.at[i,k],mate).wait()
            self.gout[k,self.c]=(self.SZ[i,k].astype(f32)+self.RM[i,k].astype(f32)).astype(self.gout.dtype)
            self.zcp(i,2,k,self.g(k),self.g(k),tip).start()
            if last: self.to_sib(k).start()
    def zd(self,i,k):
        end,mate,tip=self.role(i); last=i==len(self.digits)-1
        @pl.when(jnp.logical_not(end))
        def _():
            self.zcp(i,2,k,self.g(k),self.g(k),tip).wait_send()
        @pl.when(end)
        def _():
            self.zcp(i,2,k,self.g(k),self.g(k),mate).wait_recv()
            if last: self.to_sib(k).start()
        if not last:
            self.T[self.nt(k),0]=self.gout[k,self.c].astype(f32)
            self.za(i+1,k)
    def fin(self,k):
        self.to_sib(k).wait_send()
        g=self.gout.at[k,1-self.c]
        self.cp(3+4*len(self.digits),k,g,g,self.s,self.sib).wait_recv()
    def stage_list(self):
        out=[self.s0,self.s1,self.s2,self.s3]
        for i in range(len(self.digits)):
            out+=[functools.partial(self.zb,i),functools.partial(self.zc,i),functools.partial(self.zd,i)]
        return out+[self.fin]

def reduce_peers(digits):
    s,d,c,a,b=place()
    peers=[(a,d),(b,d),(s,d+1-2*c)]
    for st in digits:
        p=((d//2)//st)%4
        up=d+2*st*jnp.where(p==3,-3,1); down=d+2*st*jnp.where(p==0,3,-1)
        peers+=[(s,up),(s,down)]
    return peers

def stream_scratch(n,r,w,nd,nt,mt):
    V=pltpu.VMEM; S=pltpu.SemaphoreType.DMA
    return [V((n,4,r,w),f32),V((n,2,r,w),mt),V((n,2,r,w),mt),V((nt,2,r,w),f32),V((n,r,w),mt),V((n,r,w),mt),
            V((nd,n,r,w),mt),V((nd,n,r,w),mt),V((nd,n,r,w),mt),S((4+4*nd,n)),S((4+4*nd,n))]

def reduce_kernel(digits,ns,*refs):
    m=len(ns); srcs=refs[:m]; gouts=refs[m:2*m]; rest=refs[2*m:]
    streams=[]; per=13
    loads=[]
    for i in range(m):
        r=rest[i*per:(i+1)*per]; X,ls=r[11],r[12]
        c=place()[2]
        src=srcs[i]
        def load(k,src=src,X=X,ls=ls,c=c): return pltpu.make_async_copy(src.at[k,:,c],X.at[k%2],ls.at[k])
        loads.append(load)
        def mine(k,X=X): return X.at[k%2]
        def other(k,src=src,c=c): return src.at[k,:,1-c]
        streams.append(Reduce(digits,mine,other,*r[:9],gouts[i],r[9],r[10]))
    greet(reduce_peers(digits))
    nst=len(streams[0].stage_list())
    order=[]
    for t in range(max(ns)):
        for i in range(m):
            if t<ns[i]: order.append((i,t))
    for t in range(len(order)+nst-1):
        for j in range(nst):
            if 0<=t-j<len(order):
                i,k=order[t-j]
                if j==0: loads[i](k).start()
                if j==1: loads[i](k).wait()
                streams[i].stage_list()[j](k)

def reduce(arrs,types,sums,digits,cid):
    ns=[a.shape[0] for a in arrs]; nd=len(digits)
    anyspec=pl.BlockSpec(memory_space=pl.ANY)
    scratch=[]
    for a,mt in zip(arrs,types):
        n,_,_,r,w=a.shape
        scratch+=stream_scratch(n,r,w,nd,n,mt)+[pltpu.VMEM((2,4,r,w),f32),pltpu.SemaphoreType.DMA((n,))]
    return pl.pallas_call(functools.partial(reduce_kernel,digits,ns),
        in_specs=[anyspec]*len(arrs),out_specs=[pl.BlockSpec(memory_space=pltpu.VMEM)]*len(arrs),
        out_shape=[jax.ShapeDtypeStruct((a.shape[0],2)+a.shape[3:],t) for a,t in zip(arrs,sums)],
        scratch_shapes=scratch,
        compiler_params=pltpu.CompilerParams(collective_id=cid,has_side_effects=True,vmem_limit_bytes=60<<20))(*arrs)


def attn_kernel(n1_ref,n1T_ref,dy_ref,wq_ref,wk_ref,wv_ref,wo_ref,bq_ref,bk_ref,bv_ref,cos_ref,sin_ref,mask_ref,eown,rown,
                hh_ref,og_ref,bgq_ref,bgk_ref,bgv_ref,attn_ref,dn1T_ref,efull,rfull,qT,kT,vT,oT,cT,gq,gk,gv,ss,rs,ls):
    g=pl.program_id(0)
    ge=Gather(eown,efull,ss.at[0],rs.at[0],ls.at[0]); gr=Gather(rown,rfull,ss.at[1],rs.at[1],ls.at[1])
    @pl.when(g==0)
    def _():
        greet(gather_peers()); ge.start()
    @pl.when(g==1)
    def _(): ge.forward()
    @pl.when(g==2)
    def _(): ge.diag()
    heads=BLK//HEAD
    n1=n1_ref[...]
    cos=cos_ref[...]; sin=sin_ref[...]
    def proj(w_ref,b_ref): return dot(w_ref[...],n1,TT)+b_ref[...]
    def rot(x,sgn):
        parts=[]
        for h in range(heads):
            a=x[64*h:64*h+8]; b=x[64*h+8:64*h+16]
            s=sin*sgn
            parts+= [a*cos-b*s, b*cos+a*s, x[64*h+16:64*h+64]]
        return jnp.concatenate(parts,0)
    qT[...]=rot(proj(wq_ref,bq_ref),1.0).astype(bf16)
    kT[...]=rot(proj(wk_ref,bk_ref),1.0).astype(bf16)
    vT[...]=proj(wv_ref,bv_ref).astype(bf16)
    oT[...]=dot(wo_ref[...],dy_ref[...],NT).astype(bf16)
    krow=lax.broadcasted_iota(jnp.int32,(BLK,BLK),0); qcol=lax.broadcasted_iota(jnp.int32,(BLK,BLK),1)
    causal=krow<=qcol
    c=score_scale*LOG2E
    for h in range(heads):
        if h==2:
            @pl.when(g==0)
            def _(): gr.start()
            @pl.when(g==1)
            def _(): gr.forward()
            @pl.when(g==2)
            def _(): gr.diag()
        r=slice(64*h,64*h+64)
        QT=qT[r,:]; KT=kT[r,:]; VT=vT[r,:]; OT=oT[r,:]
        K=KT.T; V=VT.T
        nb=TOK//BLK
        dKT=[None]*nb; dVT=[None]*nb; dQTs=[]; cTs=[]
        for j in range(nb):
            qs=slice(BLK*j,BLK*j+BLK)
            kb0=0 if j<nb-1 else j
            kbs=list(range(kb0,j+1))
            q=QT[:,qs]; o=OT[:,qs]
            S=[dot(K[BLK*b:BLK*b+BLK],q)*c for b in kbs]
            if j<nb-1: S[-1]=jnp.where(causal,S[-1],-1e30)
            else: S[-1]=S[-1]+mask_ref[...]
            m=functools.reduce(jnp.maximum,[jnp.max(s,0,keepdims=True) for s in S])
            E=[jnp.exp2(s-m) for s in S]
            l=functools.reduce(jnp.add,[jnp.sum(e,0,keepdims=True) for e in E])
            inv=1.0/l
            P=[e*inv for e in E]
            Pb=[p.astype(bf16) for p in P]
            ct=functools.reduce(jnp.add,[dot(VT[:,BLK*b:BLK*b+BLK],p) for b,p in zip(kbs,Pb)])
            dP=[dot(V[BLK*b:BLK*b+BLK],o) for b in kbs]
            delta=functools.reduce(jnp.add,[jnp.sum(d*p,0,keepdims=True) for d,p in zip(dP,P)])
            dS=[(p*(d-delta)).astype(bf16) for d,p in zip(dP,P)]
            dq=functools.reduce(jnp.add,[dot(KT[:,BLK*b:BLK*b+BLK],s) for b,s in zip(kbs,dS)])
            cTs.append(ct.astype(bf16)); dQTs.append(dq*score_scale)
            for b,p,s in zip(kbs,Pb,dS):
                dk=dot(q,s,NT); dv=dot(o,p,NT)
                dKT[b]=dk if dKT[b] is None else dKT[b]+dk
                dVT[b]=dv if dVT[b] is None else dVT[b]+dv
        cT[r,:]=jnp.concatenate(cTs,1)
        def unrot(x):
            a=x[0:8]; b=x[8:16]
            return jnp.concatenate([a*cos+b*sin,b*cos-a*sin,x[16:64]],0)
        gq[r,:]=unrot(jnp.concatenate(dQTs,1)).astype(bf16)
        gk[r,:]=unrot(jnp.concatenate(dKT,1)*score_scale).astype(bf16)
        gv[r,:]=jnp.concatenate(dVT,1).astype(bf16)
    n1T=n1T_ref[...]
    dn=None
    for gg,w_ref,h_ref,b_ref in ((gq,wq_ref,hh_ref.at[0],bgq_ref),(gk,wk_ref,hh_ref.at[1],bgk_ref),(gv,wv_ref,hh_ref.at[2],bgv_ref)):
        G=gg[...]
        h_ref[...]=dot(n1T,G,NT)
        b_ref[...]=jnp.sum(G.astype(f32),1,keepdims=True)
        t=dot(w_ref[...],G)
        dn=t if dn is None else dn+t
    ctx=cT[...]
    og_ref[...]=dot(ctx,dy_ref[...])
    at=dot(ctx,wo_ref[...],TN)
    @pl.when(g==0)
    def _():
        attn_ref[...]=at; dn1T_ref[...]=dn
    @pl.when(g>0)
    def _():
        attn_ref[...]+=at; dn1T_ref[...]+=dn
    @pl.when(g==2)
    def _():
        ge.finish(); gr.finish()

def attention(n1,n1T,dy,W,Wo,bias_col,cos,sin,mask,eown,rown,cid):
    G=D//BLK
    full=lambda s: pl.BlockSpec(s,lambda g:(0,0))
    wspec=lambda k: pl.BlockSpec((D,BLK),lambda g,k=k:(0,k*G+g))
    bspec=lambda k: pl.BlockSpec((BLK,1),lambda g,k=k:(k*G+g,0))
    hspec=pl.BlockSpec((3,D,BLK),lambda g:(0,0,g))
    col=pl.BlockSpec((BLK,1),lambda g:(g,0))
    return pl.pallas_call(attn_kernel,grid=(G,),
        in_specs=[full((TOK,D)),full((D,TOK)),full((TOK,D)),wspec(0),wspec(1),wspec(2),pl.BlockSpec((BLK,D),lambda g:(g,0)),
                  bspec(0),bspec(1),bspec(2),full((8,TOK)),full((8,TOK)),full((BLK,BLK)),pl.BlockSpec(memory_space=pltpu.VMEM),pl.BlockSpec(memory_space=pltpu.VMEM)],
        out_specs=[hspec,pl.BlockSpec((BLK,D),lambda g:(g,0)),col,col,col,full((TOK,D)),full((D,TOK)),pl.BlockSpec(memory_space=pl.ANY),pl.BlockSpec(memory_space=pl.ANY)],
        out_shape=[jax.ShapeDtypeStruct((3,D,D),f32),jax.ShapeDtypeStruct((D,D),f32)]+[jax.ShapeDtypeStruct((D,1),f32)]*3+
                  [jax.ShapeDtypeStruct((TOK,D),f32),jax.ShapeDtypeStruct((D,TOK),f32),jax.ShapeDtypeStruct((6,D,512),bf16),jax.ShapeDtypeStruct((6,512,D),bf16)],
        scratch_shapes=[pltpu.VMEM((BLK,TOK),bf16)]*8+[pltpu.SemaphoreType.DMA((2,6)),pltpu.SemaphoreType.DMA((2,6)),pltpu.SemaphoreType.DMA((2,))],
        compiler_params=pltpu.CompilerParams(vmem_limit_bytes=60<<20,collective_id=cid,has_side_effects=True),
        )(n1,n1T,dy,W,W,W,Wo,bias_col,bias_col,bias_col,cos,sin,mask,eown,rown)

def erf_parts(h):
    e=jnp.exp2(h*h*(-0.5*LOG2E))
    return 0.5*(1.0+lax.erf(h*0.7071067811865476)), e*0.3989422804014327

def ffn_kernel(n2_ref,n2T_ref,dy_ref,we_ref,wr_ref,be_ref,eg_ref,rg_ref,bge_ref,out_ref,dn2_ref):
    g=pl.program_id(0)
    we=we_ref[0]; wr=wr_ref[0]
    h=dot(n2_ref[...],we)+be_ref[0]
    Phi,phi=erf_parts(h)
    act=(h*Phi).astype(bf16)
    da=dot(dy_ref[...],wr,NT)
    dh=(da*(Phi+h*phi)).astype(bf16)
    bge_ref[0]=jnp.sum(dh.astype(f32),0,keepdims=True)
    rg_ref[0]=dot(act,dy_ref[...],TN)
    eg_ref[0]=dot(n2T_ref[...],dh)
    o=dot(act,wr); d=dot(dh,we,NT)
    @pl.when(g==0)
    def _():
        out_ref[...]=o; dn2_ref[...]=d
    @pl.when(g>0)
    def _():
        out_ref[...]+=o; dn2_ref[...]+=d

def ffn(n2,n2T,dy,We,Wr,be):
    G,_,FC=We.shape
    full=lambda s: pl.BlockSpec(s,lambda g:(0,0))
    we=pl.BlockSpec((1,D,FC),lambda g:(g,0,0)); wr=pl.BlockSpec((1,FC,D),lambda g:(g,0,0)); b=pl.BlockSpec((1,1,FC),lambda g:(g,0,0))
    S=jax.ShapeDtypeStruct
    return pl.pallas_call(ffn_kernel,grid=(G,),
        in_specs=[full((TOK,D)),full((D,TOK)),full((TOK,D)),we,wr,b],
        out_specs=[we,wr,b,full((TOK,D)),full((TOK,D))],
        out_shape=[S((G,D,FC),f32),S((G,FC,D),f32),S((G,1,FC),f32),S((TOK,D),f32),S((TOK,D),f32)],
        compiler_params=pltpu.CompilerParams(vmem_limit_bytes=60<<20),
        )(n2,n2T,dy,We,Wr,be)


def layer_norm(values, gain, shift):
    row_mean = jnp.mean(values, -1, keepdims=True)
    centred = values - row_mean
    row_var = jnp.mean(centred * centred, -1, keepdims=True)
    return centred * lax.rsqrt(row_var + norm_epsilon) * gain + shift


def adam_step(master, moment, square, gradient, rate, decay):
    momentum = first_decay * moment + (1.0 - first_decay) * gradient
    squares = second_decay * square + (1.0 - second_decay) * gradient * gradient
    first_fix = momentum / (1.0 - first_decay**STEP)
    second_fix = squares / (1.0 - second_decay**STEP)
    updated = master - rate * (first_fix / (jnp.sqrt(second_fix) + adam_epsilon) + decay * master)
    return (momentum, squares, updated)


def per_device(
    tokens,
    lengths,
    cotangent,
    heads_master,
    output_master,
    expand_master,
    reduce_master,
    vector_master,
    heads_moment,
    output_moment,
    expand_moment,
    reduce_moment,
    vector_moment,
    heads_square,
    output_square,
    expand_square,
    reduce_square,
    vector_square,
):
    chunks = FF // 4 // 128
    cast = lambda part: part.astype(jnp.bfloat16)
    expand_own = cast(expand_master).reshape(D // 4, 4, chunks, 128).transpose(2, 0, 1, 3).reshape(chunks, D // 4, 512)
    reduce_own = cast(reduce_master).reshape(chunks, 128, D)
    vector_own = jnp.pad(cast(vector_master).reshape(16, 156), ((0, 0), (0, 100)))
    vector_full, heads_weight, output_weight = gather(
        [vector_own, cast(heads_master), cast(output_master)], [False, True, True], 1)
    vectors = vector_full.reshape(4, 16, 256)[:, :, :156].reshape(-1).astype(jnp.float32)
    gain_one = vectors[0:D]
    shift_one = vectors[D : 2 * D]
    gain_two = vectors[2 * D : 3 * D]
    shift_two = vectors[3 * D : 4 * D]
    heads_bias = vectors[4 * D : 7 * D]
    output_bias = vectors[7 * D : 8 * D]
    expand_bias = vectors[8 * D : 8 * D + FF]
    reduce_bias = vectors[8 * D + FF :]
    own = lengths[0]
    ends = jnp.cumsum(own)
    which = jnp.argmax(own)
    start = ends[which] - LONG
    short = own[(which + 1) % 3]
    dy = jnp.roll(cotangent, -start, 0)
    source = jnp.roll(tokens, -start, 0).astype(jnp.float32)
    row = jnp.arange(TOK, dtype=jnp.int32)
    position = jnp.where(row < LONG, row, row - LONG - jnp.where(row - LONG >= short, short, 0))
    inverse = rotary_base ** (-2.0 * jnp.arange(ROT // 2, dtype=jnp.float32) / ROT)
    angles = position.astype(jnp.float32)[None, :] * inverse[:, None]
    small = jnp.arange(BLK, dtype=jnp.int32)
    second = small >= short
    allowed = (second[:, None] == second[None, :]) & (small[:, None] <= small[None, :])
    mask = jnp.where(allowed, 0.0, masked_score).astype(jnp.float32)
    norm_one_out, norm_one_pull = jax.vjp(layer_norm, source, gain_one, shift_one)
    normed_one = norm_one_out.astype(jnp.bfloat16)
    norm_two_out, norm_two_pull = jax.vjp(layer_norm, source, gain_two, shift_two)
    normed_two = norm_two_out.astype(jnp.bfloat16)
    (heads_grad, output_grad, bq, bk, bv, attention_out, norm_one_gradT, expand_weight, reduce_weight) = attention(
        normed_one, normed_one.T, dy, heads_weight, output_weight, heads_bias[:, None], jnp.cos(angles), jnp.sin(angles), mask, expand_own, reduce_own, 3)
    expand_grad, reduce_grad, expand_bias_grad, feed_out, norm_two_grad = ffn(
        normed_two, normed_two.T, dy, expand_weight, reduce_weight,
        expand_bias.reshape(4, chunks, 128).transpose(1, 0, 2).reshape(chunks, 1, 512))
    block_output = jnp.roll((source + (attention_out + output_bias) + (feed_out + reduce_bias)).astype(jnp.bfloat16), start, 0)
    upstream = dy.astype(jnp.float32)
    upstream_sum = jnp.sum(upstream, 0)
    source_one, gain_one_grad, shift_one_grad = norm_one_pull(norm_one_gradT.T)
    source_two, gain_two_grad, shift_two_grad = norm_two_pull(norm_two_grad)
    token_gradient = jnp.roll((upstream + source_one + source_two).astype(jnp.bfloat16), start, 0)
    vector_grad = jnp.concatenate(
        [gain_one_grad, shift_one_grad, gain_two_grad, shift_two_grad, bq[:, 0], bk[:, 0], bv[:, 0], upstream_sum,
         expand_bias_grad.reshape(chunks, 4, 128).transpose(1, 0, 2).reshape(-1), upstream_sum], 0)
    vector_parts = jnp.pad(vector_grad.reshape(4, 2, 1248), ((0, 0), (0, 0), (0, 800))).reshape(1, 4, 2, 16, 128)
    heads_sum, output_sum, expand_sum, reduce_sum, vector_sum = reduce(
        [heads_grad.reshape(3, 4, 2, 96, D), output_grad.reshape(1, 4, 2, 96, D), expand_grad.reshape(chunks, 4, 2, 96, 512),
         reduce_grad.reshape(chunks, 4, 2, 64, D), vector_parts],
        [bf16, bf16, bf16, bf16, f32], [f32, f32, bf16, bf16, f32], ring_of(lax.axis_size("dp")), 2)
    heads_owned = heads_sum.reshape(3, D // 4, D).transpose(1, 0, 2).reshape(D // 4, 3 * D).astype(jnp.float32)
    output_owned = output_sum.reshape(D // 4, D).astype(jnp.float32)
    expand_owned = expand_sum.reshape(chunks, D // 4, 4, 128).transpose(1, 2, 0, 3).reshape(D // 4, FF).astype(jnp.float32)
    reduce_owned = reduce_sum.reshape(FF // 4, D).astype(jnp.float32)
    vector_owned = vector_sum.reshape(2, 2048)[:, :1248].reshape(-1)
    heads_new = adam_step(
        heads_master, heads_moment, heads_square, heads_owned, matrix_rate, matrix_decay
    )
    output_new = adam_step(
        output_master, output_moment, output_square, output_owned, matrix_rate, matrix_decay
    )
    expand_new = adam_step(
        expand_master, expand_moment, expand_square, expand_owned, matrix_rate, matrix_decay
    )
    reduce_new = adam_step(
        reduce_master, reduce_moment, reduce_square, reduce_owned, matrix_rate, matrix_decay
    )
    vector_new = adam_step(
        vector_master, vector_moment, vector_square, vector_owned, vector_rate, 0.0
    )
    return (
        block_output,
        token_gradient,
        heads_new[0],
        heads_new[1],
        heads_new[2],
        output_new[0],
        output_new[1],
        output_new[2],
        expand_new[0],
        expand_new[1],
        expand_new[2],
        reduce_new[0],
        reduce_new[1],
        reduce_new[2],
        vector_new[0],
        vector_new[1],
        vector_new[2],
    )


def solution(mesh):
    placed = (
        P(("shard", "dp"), None),
        P(("shard", "dp"), None),
        P(("shard", "dp"), None),
        P("shard", None),
        P("shard", None),
        P("shard", None),
        P("shard", None),
        P("shard"),
        P("shard", None),
        P("shard", None),
        P("shard", None),
        P("shard", None),
        P("shard"),
        P("shard", None),
        P("shard", None),
        P("shard", None),
        P("shard", None),
        P("shard"),
    )
    return jax.shard_map(
        per_device,
        mesh=mesh,
        in_specs=placed,
        out_specs=(
            P(("shard", "dp"), None),
            P(("shard", "dp"), None),
            P("shard", None),
            P("shard", None),
            P("shard", None),
            P("shard", None),
            P("shard", None),
            P("shard", None),
            P("shard", None),
            P("shard", None),
            P("shard", None),
            P("shard", None),
            P("shard", None),
            P("shard", None),
            P("shard"),
            P("shard"),
            P("shard"),
        ),
        check_vma=False,
    )
```

```python
import functools

import jax
import jax.numpy as jnp
from jax import lax
from jax.experimental import pallas as pl
from jax.experimental.pallas import tpu as pltpu
from jax.sharding import PartitionSpec as P

D = 768
HEADS = 12
HEAD = 64
ROT = 16
FF = 3072
STEP = 10
TOK = 1024
LONG = 768
BLK = 256
CHUNK = 512
CHUNKS = FF // CHUNK
QUARTER = D // 4
SEG = 192

first_decay = 0.9
second_decay = 0.95
adam_epsilon = 1e-08
matrix_decay = 0.1
matrix_rate = 0.04
vector_rate = 0.2
norm_epsilon = 1e-05
score_scale = 0.125
rotary_base = 10000.0
masked_score = -1e30
LOG2E = 1.4426950408889634

f32 = jnp.float32
bf16 = jnp.bfloat16
MESH = pl.DeviceIdType.MESH
NN = (((1,), (0,)), ((), ()))
NT = (((1,), (1,)), ((), ()))
TN = (((0,), (0,)), ((), ()))
TT = (((0,), (1,)), ((), ()))

GAIN_ONE, SHIFT_ONE, GAIN_TWO, SHIFT_TWO, HEADS_BIAS, OUTPUT_BIAS, EXPAND_BIAS, REDUCE_BIAS = 0, 1, 2, 3, 4, 7, 8, 12
VEC_ROWS = 13


def dot(a, b, dims=NN):
    return lax.dot_general(a, b, dims, preferred_element_type=f32)


def total(parts):
    return functools.reduce(jnp.add, parts)


def any_spec():
    return pl.BlockSpec(memory_space=pl.ANY)


def whole(shape):
    return pl.BlockSpec(shape, lambda g: (0,) * len(shape), pipeline_mode=pl.Buffered(1))


def norm_rows(values):
    centred = values - jnp.mean(values, -1, keepdims=True)
    inverse = lax.rsqrt(jnp.mean(centred * centred, -1, keepdims=True) + norm_epsilon)
    return centred * inverse, inverse


def norm_back(values, gain, grad):
    normed, inverse = norm_rows(values)
    scaled = grad * gain
    back = inverse * (
        scaled - jnp.mean(scaled, -1, keepdims=True) - normed * jnp.mean(scaled * normed, -1, keepdims=True)
    )
    return back, jnp.sum(grad * normed, 0, keepdims=True), jnp.sum(grad, 0, keepdims=True)


def place():
    s=lax.axis_index("shard"); d=lax.axis_index("dp")
    c=d%2
    s1=s+1-2*(s%2); s2=s+2-4*(s//2)
    a=(1-c)*s1+c*s2
    b=(1-c)*s2+c*s1
    return s,d,c,a,b

def rcopy(src,dst,ssem,rsem,sh,dp):
    return pltpu.make_async_remote_copy(src_ref=src,dst_ref=dst,send_sem=ssem,recv_sem=rsem,device_id=(sh,dp),device_id_type=MESH)

def greet(peers):
    bar=pltpu.get_barrier_semaphore()
    for sh,dp in peers:
        pl.semaphore_signal(bar,inc=1,device_id=(sh,dp),device_id_type=MESH)
    pl.semaphore_wait(bar,len(peers))

class Gather:
    def __init__(self,own,full,ssem,rsem,lsem,split=True):
        self.own,self.full,self.ss,self.rs,self.ls=own,full,ssem,rsem,lsem
        self.s,self.d,self.c,self.a,self.b=place()
        self.sib=self.d+1-2*self.c
        self.R=own.shape[-2]; self.split=split
        self.h=self.R//2 if split else self.R
    def sl(self,ref,row,n):
        row=pl.multiple_of(row,16)
        if len(ref.shape)==2: return ref.at[pl.ds(row,n)]
        return ref.at[:,pl.ds(row,n)]
    def region(self,sh,core):
        return self.sl(self.full,sh*self.R+(core*self.h if self.split else 0),self.h)
    def mine(self):
        return self.sl(self.own,self.c*self.h if self.split else 0,self.h)
    def cp(self,k,src,reg,sh,dp): return rcopy(src,reg,self.ss.at[k],self.rs.at[k],sh,dp)
    def local(self):
        return pltpu.make_async_copy(self.own,self.sl(self.full,self.s*self.R,self.R),self.ls)
    def start(self):
        r=self.region(self.s,self.c)
        self.cp(0,self.mine(),r,self.a,self.d).start()
        self.cp(1,self.mine(),r,self.b,self.d).start()
        self.local().start()
    def _wait_recv(self,k,sh,core):
        r=self.region(sh,core)
        self.cp(k,r,r,self.s,self.sib).wait_recv()
    def _wait_send(self,k,sh,core):
        r=self.region(sh,core)
        self.cp(k,r,r,self.s,self.sib).wait_send()
    def forward(self):
        ra=self.region(self.a,self.c)
        self._wait_recv(0,self.a,self.c)
        self.cp(2,ra,ra,self.b,self.d).start()
        if self.split: self.cp(3,ra,ra,self.s,self.sib).start()
        self._wait_recv(1,self.b,self.c)
        rb=self.region(self.b,self.c)
        if self.split: self.cp(4,rb,rb,self.s,self.sib).start()
    def diag(self):
        x=3-self.s
        self._wait_recv(2,x,self.c)
        rx=self.region(x,self.c)
        if self.split: self.cp(5,rx,rx,self.s,self.sib).start()
    def finish(self):
        self.local().wait()
        x=3-self.s
        if self.split:
            o=1-self.c
            self._wait_recv(3,self.b,o)
            self._wait_recv(4,self.a,o)
            self._wait_recv(5,x,o)
        self.cp(0,self.mine(),self.region(self.s,self.c),self.a,self.d).wait_send()
        self.cp(1,self.mine(),self.region(self.s,self.c),self.b,self.d).wait_send()
        for k,sh in ((2,self.a),)+(((3,self.a),(4,self.b),(5,x)) if self.split else ()):
            self._wait_send(k,sh,self.c)

def gather_peers():
    s,d,c,a,b=place()
    return [(a,d),(b,d),(s,d+1-2*c)]

def gather_kernel(n,splits,*refs):
    own=refs[:n]; full=refs[n:2*n]; ss,rs,ls=refs[2*n:]
    g=[Gather(own[i],full[i],ss.at[i],rs.at[i],ls.at[i],splits[i]) for i in range(n)]
    greet(gather_peers())
    for t in g: t.start()
    g[0].forward()
    for i in range(1,n):
        g[i].forward()
        g[i-1].diag()
    g[n-1].diag()
    for t in g: t.finish()

def gather(arrs,splits,cid):
    n=len(arrs)
    def fullshape(a):
        sh=list(a.shape); sh[-2]*=4; return jax.ShapeDtypeStruct(tuple(sh),a.dtype)
    anyspec=pl.BlockSpec(memory_space=pl.ANY)
    return pl.pallas_call(functools.partial(gather_kernel,n,splits),
        in_specs=[pl.BlockSpec(memory_space=pltpu.VMEM)]*n,out_specs=[anyspec]*n,out_shape=[fullshape(a) for a in arrs],
        scratch_shapes=[pltpu.SemaphoreType.DMA((n,6)),pltpu.SemaphoreType.DMA((n,6)),pltpu.SemaphoreType.DMA((n,))],
        compiler_params=pltpu.CompilerParams(collective_id=cid,has_side_effects=True,vmem_limit_bytes=40<<20))(*arrs)

def ring_of(dp_size):
    digits=[]; n=dp_size//2; stride=1
    while n>1:
        assert n%4==0
        digits.append(stride); stride*=4; n//=4
    return digits

class Reduce:
    def __init__(self,digits,mine,other,Y,SA,RA,T,SB,RB,SZ,RZ,RM,gout,ss,rs):
        self.digits=digits; self.mine=mine; self.other=other
        self.Y,self.SA,self.RA,self.T,self.SB,self.RB,self.SZ,self.RZ,self.RM,self.gout,self.ss,self.rs=Y,SA,RA,T,SB,RB,SZ,RZ,RM,gout,ss,rs
        self.s,self.d,self.c,self.a,self.b=place()
        self.sib=self.d+1-2*self.c
        self.x=3-self.s
    def cp(self,j,k,src,dst,sh,dp): return rcopy(src,dst,self.ss.at[j,k],self.rs.at[j,k],sh,dp)
    def role(self,i):
        st=self.digits[i]; p=((self.d//2)//st)%4
        end=(p==0)|(p==3)
        mate=self.d+2*st*jnp.where(p==0,1,jnp.where(p==3,-1,jnp.where(p==1,1,-1)))
        tip=self.d+2*st*jnp.where(p==1,-1,1)
        return end,mate,tip
    def stages(self): return 4+3*len(self.digits)+1
    def c0(self,k): return self.cp(0,k,self.other(k),self.Y.at[k%2],self.s,self.sib)
    def cA(self,k): return self.cp(1,k,self.SA.at[k%2],self.RA.at[k%2],self.a,self.d)
    def cB(self,k): return self.cp(2,k,self.SB.at[k%2],self.RB.at[k%2],self.b,self.d)
    def nt(self,k): return k%self.T.shape[0]
    def s0(self,k):
        self.c0(k).start()
    def s1(self,k):
        self.c0(k).wait()
        X=self.mine(k)
        def U(p): return X[p]+self.Y[k%2,p]
        self.SA[k%2,0]=U(self.a).astype(self.SA.dtype)
        self.SA[k%2,1]=U(self.x).astype(self.SA.dtype)
        self.cA(k).start()
        t=self.nt(k)
        self.T[t,0]=U(self.s)
        self.T[t,1]=U(self.b)
    def s2(self,k):
        self.cA(k).wait()
        t=self.nt(k)
        self.SB[k%2]=(self.T[t,1]+self.RA[k%2,1].astype(f32)).astype(self.SB.dtype)
        self.cB(k).start()
        self.T[t,0]=self.T[t,0]+self.RA[k%2,0].astype(f32)
    def s3(self,k):
        self.cB(k).wait()
        t=self.nt(k)
        self.T[t,0]=self.T[t,0]+self.RB[k%2].astype(f32)
        self.za(0,k)
    def g(self,k): return self.gout.at[k,self.c]
    def zcp(self,i,j,k,src,dst,dp): return self.cp(3+4*i+j,k,src,dst,self.s,dp)
    def za(self,i,k):
        t=self.nt(k); end,mate,tip=self.role(i)
        @pl.when(end)
        def _():
            self.SZ[i,k%2]=self.T[t,0].astype(self.SZ.dtype)
            self.zcp(i,0,k,self.SZ.at[i,k%2],self.RZ.at[i,k%3],mate).start()
    def zb(self,i,k):
        t=self.nt(k); end,mate,tip=self.role(i)
        @pl.when(jnp.logical_not(end))
        def _():
            self.zcp(i,0,k,self.SZ.at[i,k%2],self.RZ.at[i,k%3],tip).wait_recv()
            self.SZ[i,k%2]=(self.T[t,0]+self.RZ[i,k%3].astype(f32)).astype(self.SZ.dtype)
            self.zcp(i,1,k,self.SZ.at[i,k%2],self.RM.at[i,k%2],mate).start()
        @pl.when(end)
        def _():
            self.zcp(i,0,k,self.SZ.at[i,k%2],self.RZ.at[i,k%3],mate).wait_send()
    def to_sib(self,k):
        return self.cp(3+4*len(self.digits),k,self.g(k),self.g(k),self.s,self.sib)
    def zc(self,i,k):
        end,mate,tip=self.role(i); last=i==len(self.digits)-1
        @pl.when(jnp.logical_not(end))
        def _():
            self.zcp(i,1,k,self.SZ.at[i,k%2],self.RM.at[i,k%2],mate).wait()
            self.gout[k,self.c]=(self.SZ[i,k%2].astype(f32)+self.RM[i,k%2].astype(f32)).astype(self.gout.dtype)
            self.zcp(i,2,k,self.g(k),self.g(k),tip).start()
            if last: self.to_sib(k).start()
    def zd(self,i,k):
        end,mate,tip=self.role(i); last=i==len(self.digits)-1
        @pl.when(jnp.logical_not(end))
        def _():
            self.zcp(i,2,k,self.g(k),self.g(k),tip).wait_send()
        @pl.when(end)
        def _():
            self.zcp(i,2,k,self.g(k),self.g(k),mate).wait_recv()
            if last: self.to_sib(k).start()
        if not last:
            self.T[self.nt(k),0]=self.gout[k,self.c].astype(f32)
            self.za(i+1,k)
    def fin(self,k):
        self.to_sib(k).wait_send()
        g=self.gout.at[k,1-self.c]
        self.cp(3+4*len(self.digits),k,g,g,self.s,self.sib).wait_recv()
    def stage_list(self):
        out=[self.s0,self.s1,self.s2,self.s3]
        for i in range(len(self.digits)):
            out+=[functools.partial(self.zb,i),functools.partial(self.zc,i),functools.partial(self.zd,i)]
        return out+[self.fin]

def reduce_peers(digits):
    s,d,c,a,b=place()
    peers=[(a,d),(b,d),(s,d+1-2*c)]
    for st in digits:
        p=((d//2)//st)%4
        up=d+2*st*jnp.where(p==3,-3,1); down=d+2*st*jnp.where(p==0,3,-1)
        peers+=[(s,up),(s,down)]
    return peers

def stream_scratch(n, r, w, nd, kind):
    V, S = pltpu.VMEM, pltpu.SemaphoreType.DMA
    ring = min(n, 4 + 3 * (nd - 1))
    return [
        V((2, 4, r, w), f32), V((2, 2, r, w), kind), V((2, 2, r, w), kind), V((ring, 2, r, w), f32),
        V((2, r, w), kind), V((2, r, w), kind), V((nd, 2, r, w), kind), V((nd, 3, r, w), kind), V((nd, 2, r, w), kind),
        S((4 + 4 * nd, n)), S((4 + 4 * nd, n)),
    ]


STREAM = 11


def attention_kernel(
    x_ref, n1_ref, n1T_ref, dy_ref, wq_ref, wk_ref, wv_ref, wo_ref, vec_ref, cos_ref, sin_ref, mask_ref, eown, rown,
    hh_ref, og_ref, base_ref, grad_ref, vgrad_ref, efull, rfull,
    qT, kT, vT, oT, cT, gq, gk, gv, dn1T, ss, rs, ls,
):
    g = pl.program_id(0)
    ge = Gather(eown, efull, ss.at[0], rs.at[0], ls.at[0])
    gr = Gather(rown, rfull, ss.at[1], rs.at[1], ls.at[1])

    @pl.when(g == 0)
    def _():
        greet(gather_peers())
        ge.start()
        vgrad_ref[...] = jnp.zeros_like(vgrad_ref)

    @pl.when(g == 1)
    def _():
        ge.forward()

    @pl.when(g == 2)
    def _():
        ge.diag()

    heads = BLK // HEAD
    n1 = n1_ref[...]
    cos, sin = cos_ref[...], sin_ref[...]
    cols = pl.ds(pl.multiple_of(g * BLK, BLK), BLK)

    def column(row):
        return jnp.transpose(jnp.broadcast_to(vec_ref[row : row + 1, cols], (8, BLK)))[:, 0:1]

    def proj(w_ref, k):
        return dot(w_ref[...], n1, TT) + column(HEADS_BIAS + k)

    def rot(x):
        parts = []
        for h in range(heads):
            a, b = x[64 * h : 64 * h + 8], x[64 * h + 8 : 64 * h + 16]
            parts += [a * cos - b * sin, b * cos + a * sin, x[64 * h + 16 : 64 * h + 64]]
        return jnp.concatenate(parts, 0)

    def unrot(x):
        a, b = x[0:8], x[8:16]
        return jnp.concatenate([a * cos + b * sin, b * cos - a * sin, x[16:64]], 0)

    qT[...] = rot(proj(wq_ref, 0)).astype(bf16)
    kT[...] = rot(proj(wk_ref, 1)).astype(bf16)
    vT[...] = proj(wv_ref, 2).astype(bf16)
    oT[...] = dot(wo_ref[...], dy_ref[...], NT).astype(bf16)
    key = lax.broadcasted_iota(jnp.int32, (BLK, BLK), 0)
    query = lax.broadcasted_iota(jnp.int32, (BLK, BLK), 1)
    causal = key <= query
    scale = score_scale * LOG2E
    nb = TOK // BLK
    for h in range(heads):
        if h == 2:

            @pl.when(g == 0)
            def _():
                gr.start()

            @pl.when(g == 1)
            def _():
                gr.forward()

            @pl.when(g == 2)
            def _():
                gr.diag()

        r = slice(64 * h, 64 * h + 64)
        QT, KT, VT, OT = qT[r, :], kT[r, :], vT[r, :], oT[r, :]
        K, V = KT.T, VT.T
        dKT, dVT, dQT, context = [[] for _ in range(nb)], [[] for _ in range(nb)], [], []
        for j in range(nb):
            blocks = list(range(0 if j < nb - 1 else j, j + 1))
            span = [slice(BLK * b, BLK * b + BLK) for b in blocks]
            q, o = QT[:, BLK * j : BLK * j + BLK], OT[:, BLK * j : BLK * j + BLK]
            S = [dot(K[c], q) * scale for c in span]
            S[-1] = jnp.where(causal, S[-1], masked_score) if j < nb - 1 else S[-1] + mask_ref[...]
            top = functools.reduce(jnp.maximum, [jnp.max(s, 0, keepdims=True) for s in S])
            E = [jnp.exp2(s - top) for s in S]
            inv = 1.0 / total([jnp.sum(e, 0, keepdims=True) for e in E])
            soft = [e * inv for e in E]
            low = [p.astype(bf16) for p in soft]
            context.append(total([dot(VT[:, c], p) for c, p in zip(span, low)]).astype(bf16))
            back = [dot(V[c], o) for c in span]
            row = total([jnp.sum(d * p, 0, keepdims=True) for d, p in zip(back, soft)])
            dS = [(p * (d - row)).astype(bf16) for d, p in zip(back, soft)]
            dQT.append(total([dot(KT[:, c], s) for c, s in zip(span, dS)]) * score_scale)
            for b, p, s in zip(blocks, low, dS):
                dKT[b].append(dot(q, s, NT))
                dVT[b].append(dot(o, p, NT))
        cT[r, :] = jnp.concatenate(context, 1)
        gq[r, :] = unrot(jnp.concatenate(dQT, 1)).astype(bf16)
        gk[r, :] = unrot(jnp.concatenate([total(d) for d in dKT], 1) * score_scale).astype(bf16)
        gv[r, :] = jnp.concatenate([total(d) for d in dVT], 1).astype(bf16)
    n1T = n1T_ref[...]
    ones = jnp.ones((8, TOK), bf16)
    parts = []
    for k, (grads, w_ref) in enumerate(((gq, wq_ref), (gk, wk_ref), (gv, wv_ref))):
        G = grads[...]
        hh_ref[k] = dot(n1T, G, NT)
        vgrad_ref[HEADS_BIAS + k : HEADS_BIAS + k + 1, cols] = dot(ones, G, NT)[0:1]
        parts.append(dot(w_ref[...], G))
    ctx = cT[...]
    og_ref[...] = dot(ctx, dy_ref[...])
    out = dot(ctx, wo_ref[...], TN)

    @pl.when(g == 0)
    def _():
        bias = vec_ref[OUTPUT_BIAS : OUTPUT_BIAS + 1] + vec_ref[REDUCE_BIAS : REDUCE_BIAS + 1]
        base_ref[...] = out + (x_ref[...].astype(f32) + bias)
        dn1T[...] = total(parts)

    @pl.when(g > 0)
    def _():
        base_ref[...] += out
        dn1T[...] += total(parts)

    @pl.when(g == D // BLK - 1)
    def _():
        dy = dy_ref[...].astype(f32)
        back, gain, shift = norm_back(x_ref[...].astype(f32), vec_ref[GAIN_ONE : GAIN_ONE + 1], dn1T[...].T)
        grad_ref[...] = dy + back
        up = jnp.sum(dy, 0, keepdims=True)
        vgrad_ref[GAIN_ONE : GAIN_ONE + 1] = gain
        vgrad_ref[SHIFT_ONE : SHIFT_ONE + 1] = shift
        vgrad_ref[OUTPUT_BIAS : OUTPUT_BIAS + 1] = up
        vgrad_ref[REDUCE_BIAS : REDUCE_BIAS + 1] = up
        ge.finish()
        gr.finish()


def attention(x, n1, n1T, dy, W, Wo, vec, cos, sin, mask, eown, rown, cid):
    G = D // BLK
    S, V = jax.ShapeDtypeStruct, pltpu.VMEM
    block = lambda k: pl.BlockSpec((D, BLK), lambda g: (0, k * G + g))
    rows = pl.BlockSpec((BLK, D), lambda g: (g, 0))
    sem = pltpu.SemaphoreType.DMA
    return pl.pallas_call(
        attention_kernel,
        grid=(G,),
        in_specs=[
            whole((TOK, D)), whole((TOK, D)), whole((D, TOK)), whole((TOK, D)), block(0), block(1), block(2), rows,
            whole((16, D)), whole((8, TOK)), whole((8, TOK)), whole((BLK, BLK)),
            whole(eown.shape), whole(rown.shape),
        ],
        out_specs=[
            pl.BlockSpec((3, D, BLK), lambda g: (0, 0, g)), rows, whole((TOK, D)), whole((TOK, D)), whole((16, D)),
            any_spec(), any_spec(),
        ],
        out_shape=[
            S((3, D, D), f32), S((D, D), f32), S((TOK, D), f32), S((TOK, D), f32), S((16, D), f32),
            S((CHUNKS, D, CHUNK), bf16), S((CHUNKS, CHUNK, D), bf16),
        ],
        scratch_shapes=[V((BLK, TOK), bf16)] * 8 + [V((D, TOK), f32), sem((2, 6)), sem((2, 6)), sem((2,))],
        compiler_params=pltpu.CompilerParams(vmem_limit_bytes=60 << 20, collective_id=cid, has_side_effects=True),
    )(x, n1, n1T, dy, W, W, W, Wo, vec, cos, sin, mask, eown, rown)


def feed_kernel(
    digits, n2_ref, n2T_ref, dy_ref, x_ref, vec_ref, start_ref, we_ref, wr_ref, base_hbm, grad_hbm, hh, og, vg_ref,
    out_ref, token_ref, sum_h, sum_e, sum_r, sum_v,
    gh, gx, gr, gv, os, acc, dn2, bge, ex, rx, vx, hx, ls, bs, *scratch,
):
    t = pl.program_id(0)
    c = place()[2]
    parts = [scratch[STREAM * i : STREAM * i + STREAM] for i in range(4)]

    def stream(i, mine, other, gout):
        return Reduce(digits, mine, other, *parts[i][:9], gout, parts[i][9], parts[i][10])

    def half(k, core, do):
        @pl.when(k < 3)
        def _():
            do(hh.at[k, :, core])

        @pl.when(k == 3)
        def _():
            do(og.at[0, :, core])

    H = stream(0, lambda k: hx.at[k % 2], None, gh)
    E = stream(1, lambda k: ex.at[:, c], lambda k: ex.at[:, 1 - c], gx)
    R = stream(2, lambda k: rx.at[:, c], lambda k: rx.at[:, 1 - c], gr)
    Z = stream(3, lambda k: vx.at[:, c], lambda k: vx.at[:, 1 - c], gv)

    sums = ((gh, sum_h), (gx, sum_e), (gr, sum_r), (gv, sum_v))

    def hand(i, k):
        return pltpu.make_async_copy(sums[i][0].at[k], sums[i][1].at[k], os.at[i, k])

    def load_base():
        return pltpu.make_async_copy(base_hbm, acc, bs.at[0])

    def load_grad():
        return pltpu.make_async_copy(grad_hbm, acc, bs.at[1])

    @pl.when(t == 0)
    def _():
        greet(reduce_peers(digits))
        load_base().start()

    last = len(E.stage_list()) - 1
    for j in range(last, 0, -1):
        for i, (s, n, first) in enumerate(((H, 4, 0), (E, CHUNKS, 0), (R, CHUNKS, 0), (Z, 1, CHUNKS - 1))):

            @pl.when((t >= j + first) & (t < j + first + n))
            def _():
                k = t - j - first
                if s is H and j == 1:
                    pltpu.make_async_copy(hh.at[0, :, c], hx.at[k % 2], ls.at[k]).wait()
                    s.other = lambda k: hx.at[k % 2]
                s.stage_list()[j](k)
                if j == last:
                    hand(i, k).start()

    @pl.when(t < 4)
    def _():
        half(t, c, lambda src: pltpu.make_async_copy(src, hx.at[t % 2], ls.at[t]).start())
        half(t, 1 - c, lambda src: H.cp(0, t, src, H.Y.at[t % 2], H.s, H.sib).start())

    @pl.when(t < CHUNKS)
    def _():
        n2, dy, we, wr = n2_ref[...], dy_ref[...], we_ref[0], wr_ref[0]
        bias = jnp.concatenate(
            [vec_ref[EXPAND_BIAS + s : EXPAND_BIAS + s + 1, pl.ds(pl.multiple_of(t * 128, 128), 128)] for s in range(4)], 1
        )
        h = dot(n2, we) + bias
        cdf = 0.5 * (1.0 + lax.erf(h * 0.7071067811865476))
        pdf = jnp.exp2(h * h * (-0.5 * LOG2E)) * 0.3989422804014327
        active = (h * cdf).astype(bf16)
        hidden = (dot(dy, wr, NT) * (cdf + h * pdf)).astype(bf16)
        bge[pl.ds(t, 1)] = jnp.sum(hidden.astype(f32), 0, keepdims=True)[None]
        rx[...] = dot(active, dy, TN).reshape(rx.shape)
        R.s0(t)
        ex[...] = dot(n2T_ref[...], hidden).reshape(ex.shape)
        E.s0(t)
        out = dot(active, wr)
        back = dot(hidden, we, NT)

        @pl.when(t == 0)
        def _():
            load_base().wait()
            dn2[...] = back

        @pl.when(t > 0)
        def _():
            dn2[...] += back

        acc[...] += out

    @pl.when(t == CHUNKS - 1)
    def _():
        block = acc[...].astype(bf16)
        load_grad().start()
        back, gain, shift = norm_back(x_ref[...].astype(f32), vec_ref[GAIN_TWO : GAIN_TWO + 1], dn2[...])
        rows = {k: vg_ref[k : k + 1] for k in range(VEC_ROWS) if k not in (2, 3, 8, 9, 10, 11)}
        rows[GAIN_TWO], rows[SHIFT_TWO] = gain, shift
        for s in range(4):
            rows[EXPAND_BIAS + s] = jnp.concatenate([bge[g, :, 128 * s : 128 * s + 128] for g in range(CHUNKS)], 1)
        vx[...] = jnp.zeros_like(vx)
        for i in range(VEC_ROWS * 4):
            s, row = i // VEC_ROWS, i % VEC_ROWS
            vx[s, row // 8, row % 8 : row % 8 + 1, 0:SEG] = rows[i // 4][:, SEG * (i % 4) : SEG * (i % 4) + SEG]
        Z.s0(0)
        load_grad().wait()
        token = (acc[...] + back).astype(bf16)
        place_of = lax.broadcasted_iota(jnp.int32, (BLK, TOK), 1)
        for i in range(TOK // BLK):
            want = lax.broadcasted_iota(jnp.int32, (BLK, TOK), 0) + (i * BLK - start_ref[0:1, 0:1])
            want = jnp.where(want < 0, want + TOK, want)
            turn = (want == place_of).astype(bf16)
            out_ref[BLK * i : BLK * i + BLK] = dot(turn, block).astype(bf16)
            token_ref[BLK * i : BLK * i + BLK] = dot(turn, token).astype(bf16)

    @pl.when(t == pl.num_programs(0) - 1)
    def _():
        for i, n in enumerate((4, CHUNKS, CHUNKS, 1)):
            for k in range(n):
                hand(i, k).wait()


def feed(n2, n2T, dy, x, vec, start, We, Wr, base, grad, hh, og, vgrad, digits, cid):
    S, V, sem = jax.ShapeDtypeStruct, pltpu.VMEM, pltpu.SemaphoreType.DMA
    nd = len(digits)
    steps = CHUNKS + 4 + 3 * nd
    at = lambda t: jnp.minimum(t, CHUNKS - 1)
    vmem = pl.BlockSpec(memory_space=pltpu.VMEM)
    shapes = [((4, 2, 96, D), f32), ((CHUNKS, 2, 96, CHUNK), bf16), ((CHUNKS, 2, 64, D), bf16), ((1, 2, 8, BLK), f32)]
    return pl.pallas_call(
        functools.partial(feed_kernel, digits),
        grid=(steps,),
        in_specs=[
            whole((TOK, D)), whole((D, TOK)), whole((TOK, D)), whole((TOK, D)), whole((16, D)), whole((1, 128)),
            pl.BlockSpec((1, D, CHUNK), lambda t: (at(t), 0, 0)), pl.BlockSpec((1, CHUNK, D), lambda t: (at(t), 0, 0)),
            any_spec(), any_spec(), any_spec(), any_spec(), whole((16, D)),
        ],
        out_specs=[whole((TOK, D)), whole((TOK, D))] + [any_spec() for _ in shapes],
        out_shape=[S((TOK, D), bf16), S((TOK, D), bf16)] + [S(s, k) for s, k in shapes],
        scratch_shapes=[V(s, k) for s, k in shapes] + [
            sem((4, CHUNKS)), V((TOK, D), f32), V((TOK, D), f32), V((CHUNKS, 1, CHUNK), f32), V((4, 2, 96, CHUNK), f32),
            V((4, 2, 64, D), f32), V((4, 2, 8, BLK), f32), V((2, 4, 96, D), f32), sem((4,)), sem((2,)),
        ]
        + stream_scratch(4, 96, D, nd, bf16) + stream_scratch(CHUNKS, 96, CHUNK, nd, bf16)
        + stream_scratch(CHUNKS, 64, D, nd, bf16) + stream_scratch(1, 8, BLK, nd, f32),
        compiler_params=pltpu.CompilerParams(vmem_limit_bytes=63 << 20, collective_id=cid, has_side_effects=True),
    )(n2, n2T, dy, x, vec, start, We, Wr, base, grad, hh, og, vgrad)


def adam_step(master, moment, square, gradient, rate, decay):
    momentum = first_decay * moment + (1.0 - first_decay) * gradient
    squares = second_decay * square + (1.0 - second_decay) * gradient * gradient
    first_fix = momentum / (1.0 - first_decay**STEP)
    second_fix = squares / (1.0 - second_decay**STEP)
    updated = master - rate * (first_fix / (jnp.sqrt(second_fix) + adam_epsilon) + decay * master)
    return (momentum, squares, updated)


def per_device(
    tokens,
    lengths,
    cotangent,
    heads_master,
    output_master,
    expand_master,
    reduce_master,
    vector_master,
    heads_moment,
    output_moment,
    expand_moment,
    reduce_moment,
    vector_moment,
    heads_square,
    output_square,
    expand_square,
    reduce_square,
    vector_square,
):
    cast = lambda part: part.astype(jnp.bfloat16)
    expand_own = cast(expand_master).reshape(QUARTER, 4, CHUNKS, 128).transpose(2, 0, 1, 3).reshape(CHUNKS, QUARTER, CHUNK)
    reduce_own = cast(reduce_master).reshape(CHUNKS, 128, D)
    vector_own = jnp.pad(cast(vector_master).reshape(VEC_ROWS, SEG), ((0, 3), (0, 64)))
    vector_full, heads_weight, output_weight = gather(
        [vector_own, cast(heads_master), cast(output_master)], [False, True, True], 1)
    vectors = jnp.pad(vector_full.reshape(4, 16, BLK)[:, :VEC_ROWS, :SEG].reshape(VEC_ROWS, D).astype(f32), ((0, 3), (0, 0)))
    own = lengths[0]
    ends = jnp.cumsum(own)
    which = jnp.argmax(own)
    start = ends[which] - LONG
    short = own[(which + 1) % 3]
    dy = jnp.roll(cotangent, -start, 0)
    tokens_r = jnp.roll(tokens, -start, 0)
    source = tokens_r.astype(f32)
    row = jnp.arange(TOK, dtype=jnp.int32)
    position = jnp.where(row < LONG, row, row - LONG - jnp.where(row - LONG >= short, short, 0))
    inverse = rotary_base ** (-2.0 * jnp.arange(ROT // 2, dtype=f32) / ROT)
    angles = position.astype(f32)[None, :] * inverse[:, None]
    small = jnp.arange(BLK, dtype=jnp.int32)
    second = small >= short
    allowed = (second[:, None] == second[None, :]) & (small[:, None] <= small[None, :])
    mask = jnp.where(allowed, 0.0, masked_score).astype(f32)
    normed = norm_rows(source)[0]
    normed_one = (normed * vectors[GAIN_ONE] + vectors[SHIFT_ONE]).astype(bf16)
    normed_two = (normed * vectors[GAIN_TWO] + vectors[SHIFT_TWO]).astype(bf16)
    heads_grad, output_grad, base, grad, vector_grad, expand_weight, reduce_weight = attention(
        tokens_r, normed_one, normed_one.T, dy, heads_weight, output_weight, vectors, jnp.cos(angles), jnp.sin(angles),
        mask, expand_own, reduce_own, 2)
    block_output, token_gradient, heads_sum, expand_sum, reduce_sum, vector_sum = feed(
        normed_two, normed_two.T, dy, tokens_r, vectors, jnp.full((1, 128), start, jnp.int32), expand_weight,
        reduce_weight, base, grad, heads_grad.reshape(3, 4, 2, 96, D), output_grad.reshape(1, 4, 2, 96, D), vector_grad,
        ring_of(lax.axis_size("dp")), 3)
    heads_owned = heads_sum[:3].reshape(3, QUARTER, D).transpose(1, 0, 2).reshape(QUARTER, 3 * D)
    output_owned = heads_sum[3].reshape(QUARTER, D)
    expand_owned = expand_sum.reshape(CHUNKS, QUARTER, 4, 128).transpose(1, 2, 0, 3).reshape(QUARTER, FF).astype(f32)
    reduce_owned = reduce_sum.reshape(FF // 4, D).astype(f32)
    vector_owned = vector_sum.reshape(16, BLK)[:VEC_ROWS, :SEG].reshape(-1)
    heads_new = adam_step(
        heads_master, heads_moment, heads_square, heads_owned, matrix_rate, matrix_decay
    )
    output_new = adam_step(
        output_master, output_moment, output_square, output_owned, matrix_rate, matrix_decay
    )
    expand_new = adam_step(
        expand_master, expand_moment, expand_square, expand_owned, matrix_rate, matrix_decay
    )
    reduce_new = adam_step(
        reduce_master, reduce_moment, reduce_square, reduce_owned, matrix_rate, matrix_decay
    )
    vector_new = adam_step(
        vector_master, vector_moment, vector_square, vector_owned, vector_rate, 0.0
    )
    return (
        block_output,
        token_gradient,
        heads_new[0],
        heads_new[1],
        heads_new[2],
        output_new[0],
        output_new[1],
        output_new[2],
        expand_new[0],
        expand_new[1],
        expand_new[2],
        reduce_new[0],
        reduce_new[1],
        reduce_new[2],
        vector_new[0],
        vector_new[1],
        vector_new[2],
    )


def solution(mesh):
    placed = (
        P(("shard", "dp"), None),
        P(("shard", "dp"), None),
        P(("shard", "dp"), None),
        P("shard", None),
        P("shard", None),
        P("shard", None),
        P("shard", None),
        P("shard"),
        P("shard", None),
        P("shard", None),
        P("shard", None),
        P("shard", None),
        P("shard"),
        P("shard", None),
        P("shard", None),
        P("shard", None),
        P("shard", None),
        P("shard"),
    )
    return jax.shard_map(
        per_device,
        mesh=mesh,
        in_specs=placed,
        out_specs=(
            P(("shard", "dp"), None),
            P(("shard", "dp"), None),
            P("shard", None),
            P("shard", None),
            P("shard", None),
            P("shard", None),
            P("shard", None),
            P("shard", None),
            P("shard", None),
            P("shard", None),
            P("shard", None),
            P("shard", None),
            P("shard", None),
            P("shard", None),
            P("shard"),
            P("shard"),
            P("shard"),
        ),
        check_vma=False,
    )
```

```python
import functools

import jax
import jax.numpy as jnp
from jax import lax
from jax.experimental import pallas as pl
from jax.experimental.pallas import tpu as pltpu
from jax.sharding import PartitionSpec as P

D = 768
HEADS = 12
HEAD = 64
ROT = 16
FF = 3072
STEP = 10
TOK = 1024
LONG = 768
BLK = 256
CHUNK = 512
CHUNKS = FF // CHUNK
QUARTER = D // 4
SEG = 192

first_decay = 0.9
second_decay = 0.95
adam_epsilon = 1e-08
matrix_decay = 0.1
matrix_rate = 0.04
vector_rate = 0.2
norm_epsilon = 1e-05
score_scale = 0.125
rotary_base = 10000.0
masked_score = -1e30
LOG2E = 1.4426950408889634

f32 = jnp.float32
bf16 = jnp.bfloat16
MESH = pl.DeviceIdType.MESH
NN = (((1,), (0,)), ((), ()))
NT = (((1,), (1,)), ((), ()))
TN = (((0,), (0,)), ((), ()))
TT = (((0,), (1,)), ((), ()))

GAIN_ONE, SHIFT_ONE, GAIN_TWO, SHIFT_TWO, HEADS_BIAS, OUTPUT_BIAS, EXPAND_BIAS, REDUCE_BIAS = 0, 1, 2, 3, 4, 7, 8, 12
VEC_ROWS = 13


def dot(a, b, dims=NN):
    return lax.dot_general(a, b, dims, preferred_element_type=f32)


def total(parts):
    return functools.reduce(jnp.add, parts)


def any_spec():
    return pl.BlockSpec(memory_space=pl.ANY)


def whole(shape):
    return pl.BlockSpec(shape, lambda g: (0,) * len(shape), pipeline_mode=pl.Buffered(1))


def norm_rows(values):
    centred = values - jnp.mean(values, -1, keepdims=True)
    inverse = lax.rsqrt(jnp.mean(centred * centred, -1, keepdims=True) + norm_epsilon)
    return centred * inverse, inverse


def norm_back(values, gain, grad):
    normed, inverse = norm_rows(values)
    scaled = grad * gain
    back = inverse * (
        scaled - jnp.mean(scaled, -1, keepdims=True) - normed * jnp.mean(scaled * normed, -1, keepdims=True)
    )
    return back, jnp.sum(grad * normed, 0, keepdims=True), jnp.sum(grad, 0, keepdims=True)


def place():
    s=lax.axis_index("shard"); d=lax.axis_index("dp")
    c=d%2
    s1=s+1-2*(s%2); s2=s+2-4*(s//2)
    a=(1-c)*s1+c*s2
    b=(1-c)*s2+c*s1
    return s,d,c,a,b

def rcopy(src,dst,ssem,rsem,sh,dp):
    return pltpu.make_async_remote_copy(src_ref=src,dst_ref=dst,send_sem=ssem,recv_sem=rsem,device_id=(sh,dp),device_id_type=MESH)

def greet(peers):
    bar=pltpu.get_barrier_semaphore()
    for sh,dp in peers:
        pl.semaphore_signal(bar,inc=1,device_id=(sh,dp),device_id_type=MESH)
    pl.semaphore_wait(bar,len(peers))

class Gather:
    def __init__(self,own,full,ssem,rsem,lsem,split=True):
        self.own,self.full,self.ss,self.rs,self.ls=own,full,ssem,rsem,lsem
        self.s,self.d,self.c,self.a,self.b=place()
        self.sib=self.d+1-2*self.c
        self.R=own.shape[-2]; self.split=split
        self.h=self.R//2 if split else self.R
    def sl(self,ref,row,n):
        row=pl.multiple_of(row,16)
        if len(ref.shape)==2: return ref.at[pl.ds(row,n)]
        return ref.at[:,pl.ds(row,n)]
    def region(self,sh,core):
        return self.sl(self.full,sh*self.R+(core*self.h if self.split else 0),self.h)
    def mine(self):
        return self.sl(self.own,self.c*self.h if self.split else 0,self.h)
    def cp(self,k,src,reg,sh,dp): return rcopy(src,reg,self.ss.at[k],self.rs.at[k],sh,dp)
    def local(self):
        return pltpu.make_async_copy(self.own,self.sl(self.full,self.s*self.R,self.R),self.ls)
    def start(self):
        r=self.region(self.s,self.c)
        self.cp(0,self.mine(),r,self.a,self.d).start()
        self.cp(1,self.mine(),r,self.b,self.d).start()
        self.local().start()
    def _wait_recv(self,k,sh,core):
        r=self.region(sh,core)
        self.cp(k,r,r,self.s,self.sib).wait_recv()
    def _wait_send(self,k,sh,core):
        r=self.region(sh,core)
        self.cp(k,r,r,self.s,self.sib).wait_send()
    def forward(self):
        ra=self.region(self.a,self.c)
        self._wait_recv(0,self.a,self.c)
        self.cp(2,ra,ra,self.b,self.d).start()
        if self.split: self.cp(3,ra,ra,self.s,self.sib).start()
        self._wait_recv(1,self.b,self.c)
        rb=self.region(self.b,self.c)
        if self.split: self.cp(4,rb,rb,self.s,self.sib).start()
    def diag(self):
        x=3-self.s
        self._wait_recv(2,x,self.c)
        rx=self.region(x,self.c)
        if self.split: self.cp(5,rx,rx,self.s,self.sib).start()
    def finish(self):
        self.local().wait()
        x=3-self.s
        if self.split:
            o=1-self.c
            self._wait_recv(3,self.b,o)
            self._wait_recv(4,self.a,o)
            self._wait_recv(5,x,o)
        self.cp(0,self.mine(),self.region(self.s,self.c),self.a,self.d).wait_send()
        self.cp(1,self.mine(),self.region(self.s,self.c),self.b,self.d).wait_send()
        for k,sh in ((2,self.a),)+(((3,self.a),(4,self.b),(5,x)) if self.split else ()):
            self._wait_send(k,sh,self.c)

def gather_peers():
    s,d,c,a,b=place()
    return [(a,d),(b,d),(s,d+1-2*c)]

def ring_of(dp_size):
    digits=[]; n=dp_size//2; stride=1
    while n>1:
        assert n%4==0
        digits.append(stride); stride*=4; n//=4
    return digits

class Reduce:
    def __init__(self,digits,mine,other,Y,SA,RA,T,SB,RB,SZ,RZ,RM,gout,ss,rs):
        self.digits=digits; self.mine=mine; self.other=other
        self.Y,self.SA,self.RA,self.T,self.SB,self.RB,self.SZ,self.RZ,self.RM,self.gout,self.ss,self.rs=Y,SA,RA,T,SB,RB,SZ,RZ,RM,gout,ss,rs
        self.s,self.d,self.c,self.a,self.b=place()
        self.sib=self.d+1-2*self.c
        self.x=3-self.s
    def cp(self,j,k,src,dst,sh,dp): return rcopy(src,dst,self.ss.at[j,k],self.rs.at[j,k],sh,dp)
    def role(self,i):
        st=self.digits[i]; p=((self.d//2)//st)%4
        end=(p==0)|(p==3)
        mate=self.d+2*st*jnp.where(p==0,1,jnp.where(p==3,-1,jnp.where(p==1,1,-1)))
        tip=self.d+2*st*jnp.where(p==1,-1,1)
        return end,mate,tip
    def stages(self): return 4+3*len(self.digits)+1
    def c0(self,k): return self.cp(0,k,self.other(k),self.Y.at[k%2],self.s,self.sib)
    def cA(self,k): return self.cp(1,k,self.SA.at[k%2],self.RA.at[k%2],self.a,self.d)
    def cB(self,k): return self.cp(2,k,self.SB.at[k%2],self.RB.at[k%2],self.b,self.d)
    def nt(self,k): return k%self.T.shape[0]
    def s0(self,k):
        self.c0(k).start()
    def s1(self,k):
        self.c0(k).wait()
        X=self.mine(k)
        def U(p): return X[p]+self.Y[k%2,p]
        self.SA[k%2,0]=U(self.a).astype(self.SA.dtype)
        self.SA[k%2,1]=U(self.x).astype(self.SA.dtype)
        self.cA(k).start()
        t=self.nt(k)
        self.T[t,0]=U(self.s)
        self.T[t,1]=U(self.b)
    def s2(self,k):
        self.cA(k).wait()
        t=self.nt(k)
        self.SB[k%2]=(self.T[t,1]+self.RA[k%2,1].astype(f32)).astype(self.SB.dtype)
        self.cB(k).start()
        self.T[t,0]=self.T[t,0]+self.RA[k%2,0].astype(f32)
    def s3(self,k):
        self.cB(k).wait()
        t=self.nt(k)
        self.T[t,0]=self.T[t,0]+self.RB[k%2].astype(f32)
        self.za(0,k)
    def g(self,k): return self.gout.at[k,self.c]
    def zcp(self,i,j,k,src,dst,dp): return self.cp(3+4*i+j,k,src,dst,self.s,dp)
    def za(self,i,k):
        t=self.nt(k); end,mate,tip=self.role(i)
        @pl.when(end)
        def _():
            self.SZ[i,k%2]=self.T[t,0].astype(self.SZ.dtype)
            self.zcp(i,0,k,self.SZ.at[i,k%2],self.RZ.at[i,k%3],mate).start()
    def zb(self,i,k):
        t=self.nt(k); end,mate,tip=self.role(i)
        @pl.when(jnp.logical_not(end))
        def _():
            self.zcp(i,0,k,self.SZ.at[i,k%2],self.RZ.at[i,k%3],tip).wait_recv()
            self.SZ[i,k%2]=(self.T[t,0]+self.RZ[i,k%3].astype(f32)).astype(self.SZ.dtype)
            self.zcp(i,1,k,self.SZ.at[i,k%2],self.RM.at[i,k%2],mate).start()
        @pl.when(end)
        def _():
            self.zcp(i,0,k,self.SZ.at[i,k%2],self.RZ.at[i,k%3],mate).wait_send()
    def to_sib(self,k):
        return self.cp(3+4*len(self.digits),k,self.g(k),self.g(k),self.s,self.sib)
    def zc(self,i,k):
        end,mate,tip=self.role(i); last=i==len(self.digits)-1
        @pl.when(jnp.logical_not(end))
        def _():
            self.zcp(i,1,k,self.SZ.at[i,k%2],self.RM.at[i,k%2],mate).wait()
            self.gout[k,self.c]=(self.SZ[i,k%2].astype(f32)+self.RM[i,k%2].astype(f32)).astype(self.gout.dtype)
            self.zcp(i,2,k,self.g(k),self.g(k),tip).start()
            if last: self.to_sib(k).start()
    def zd(self,i,k):
        end,mate,tip=self.role(i); last=i==len(self.digits)-1
        @pl.when(jnp.logical_not(end))
        def _():
            self.zcp(i,2,k,self.g(k),self.g(k),tip).wait_send()
        @pl.when(end)
        def _():
            self.zcp(i,2,k,self.g(k),self.g(k),mate).wait_recv()
            if last: self.to_sib(k).start()
        if not last:
            self.T[self.nt(k),0]=self.gout[k,self.c].astype(f32)
            self.za(i+1,k)
    def fin(self,k):
        self.to_sib(k).wait_send()
        g=self.gout.at[k,1-self.c]
        self.cp(3+4*len(self.digits),k,g,g,self.s,self.sib).wait_recv()
    def stage_list(self):
        out=[self.s0,self.s1,self.s2,self.s3]
        for i in range(len(self.digits)):
            out+=[functools.partial(self.zb,i),functools.partial(self.zc,i),functools.partial(self.zd,i)]
        return out+[self.fin]

def reduce_peers(digits):
    s,d,c,a,b=place()
    peers=[(a,d),(b,d),(s,d+1-2*c)]
    for st in digits:
        p=((d//2)//st)%4
        up=d+2*st*jnp.where(p==3,-3,1); down=d+2*st*jnp.where(p==0,3,-1)
        peers+=[(s,up),(s,down)]
    return peers

def stream_scratch(n, r, w, nd, kind):
    V, S = pltpu.VMEM, pltpu.SemaphoreType.DMA
    ring = min(n, 4 + 3 * (nd - 1))
    return [
        V((2, 4, r, w), f32), V((2, 2, r, w), kind), V((2, 2, r, w), kind), V((ring, 2, r, w), f32),
        V((2, r, w), kind), V((2, r, w), kind), V((nd, 2, r, w), kind), V((nd, 3, r, w), kind), V((nd, 2, r, w), kind),
        S((4 + 4 * nd, n)), S((4 + 4 * nd, n)),
    ]


STREAM = 11


def enter_kernel(
    lens, x_hbm, dy_hbm, vec_own, heads_hbm, output_hbm, expand_hbm, reduce_hbm,
    x_out, dy_out, n1_out, n1T_out, n2_out, n2T_out, vec_ref, cos_ref, sin_ref, mask_ref, heads_full, output_full, e_out, r_out,
    vec_full, vec_low, xs, ds, normed, n1, n1T, n2, n2T, heads_in, output_in, expand_in, reduce_in, heads_own, output_own,
    eown, rown, ss, rs, ls, ins, outs,
):
    loads = [
        pltpu.make_async_copy(src, dst, ins.at[i])
        for i, (src, dst) in enumerate((
            (heads_hbm, heads_in), (output_hbm, output_in), (x_hbm, xs), (dy_hbm, ds), (expand_hbm, expand_in),
            (reduce_hbm, reduce_in),
        ))
    ]
    stores = [
        pltpu.make_async_copy(src, dst, outs.at[i])
        for i, (src, dst) in enumerate((
            (xs, x_out), (ds, dy_out), (n1, n1_out), (n1T, n1T_out), (n2, n2_out), (n2T, n2T_out), (eown, e_out),
            (rown, r_out),
        ))
    ]
    for copy in loads:
        copy.start()
    gv = Gather(vec_low, vec_full, ss.at[0], rs.at[0], ls.at[0], False)
    gh = Gather(heads_own, heads_full, ss.at[1], rs.at[1], ls.at[1])
    go = Gather(output_own, output_full, ss.at[2], rs.at[2], ls.at[2])
    vec_low[...] = jnp.zeros_like(vec_low)
    vec_low[0:VEC_ROWS, 0:SEG] = vec_own[...].astype(bf16)
    greet(gather_peers())
    gv.start()
    loads[0].wait()
    heads_own[...] = heads_in[...].astype(bf16)
    gh.start()
    loads[1].wait()
    output_own[...] = output_in[...].astype(bf16)
    go.start()
    first, second, third = lens[0, 0], lens[0, 1], lens[0, 2]
    start = jnp.where(first == LONG, 0, jnp.where(second == LONG, first, first + second))
    short = jnp.where(first == LONG, second, jnp.where(second == LONG, third, first))
    from_row = lax.broadcasted_iota(jnp.int32, (BLK, TOK), 1)

    def turn(ref):
        values, parts = ref[...], []
        for i in range(TOK // BLK):
            want = lax.broadcasted_iota(jnp.int32, (BLK, TOK), 0) + (i * BLK + start)
            want = jnp.where(want >= TOK, want - TOK, want)
            parts.append(dot((want == from_row).astype(bf16), values).astype(bf16))
        for i, part in enumerate(parts):
            ref[BLK * i : BLK * i + BLK] = part

    loads[2].wait()
    turn(xs)
    stores[0].start()
    for i in range(TOK // BLK):
        normed[BLK * i : BLK * i + BLK] = norm_rows(xs[BLK * i : BLK * i + BLK].astype(f32))[0]
    gv.forward()
    loads[3].wait()
    turn(ds)
    stores[1].start()
    gv.diag()
    row = lax.broadcasted_iota(jnp.int32, (8, TOK), 1)
    late = row - LONG
    position = jnp.where(late < 0, row, jnp.where(late >= short, late - short, late)).astype(f32)
    step = lax.broadcasted_iota(jnp.int32, (8, TOK), 0).astype(f32)
    angles = position * jnp.exp2(step * (-2.0 / ROT * 13.287712379549449))
    cos_ref[...] = jnp.cos(angles)
    sin_ref[...] = jnp.sin(angles)
    key = lax.broadcasted_iota(jnp.int32, (BLK, BLK), 0)
    query = lax.broadcasted_iota(jnp.int32, (BLK, BLK), 1)
    allowed = ((key >= short) == (query >= short)) & (key <= query)
    mask_ref[...] = jnp.where(allowed, 0.0, masked_score)
    gv.finish()
    vec_ref[...] = jnp.zeros_like(vec_ref)
    for i in range(4 * VEC_ROWS):
        s, r = i // VEC_ROWS, i % VEC_ROWS
        piece = vec_full[16 * s : 16 * s + 16].astype(f32)[r : r + 1, 0:SEG]
        vec_ref[i // 4 : i // 4 + 1, SEG * (i % 4) : SEG * (i % 4) + SEG] = piece
    gh.forward()
    for out, outT, gain, shift, k in ((n1, n1T, GAIN_ONE, SHIFT_ONE, 2), (n2, n2T, GAIN_TWO, SHIFT_TWO, 4)):
        for i in range(TOK // BLK):
            rows = slice(BLK * i, BLK * i + BLK)
            low = (normed[rows] * vec_ref[gain : gain + 1] + vec_ref[shift : shift + 1]).astype(bf16)
            out[rows] = low
            outT[:, rows] = low.T
        stores[k].start()
        stores[k + 1].start()
        if k == 2:
            go.forward()
            gh.diag()
    loads[4].wait()
    for g in range(CHUNKS):
        for s in range(4):
            eown[g, :, 128 * s : 128 * s + 128] = expand_in[:, D * s + 128 * g : D * s + 128 * g + 128].astype(bf16)
    stores[6].start()
    loads[5].wait()
    rown[...] = reduce_in[...].astype(bf16).reshape(rown.shape)
    stores[7].start()
    go.diag()
    gh.finish()
    go.finish()
    for copy in stores:
        copy.wait()


def enter(lens, x, dy, vec, heads, output, expand, reduce, cid):
    S, V, sem = jax.ShapeDtypeStruct, pltpu.VMEM, pltpu.SemaphoreType.DMA
    vmem = pl.BlockSpec(memory_space=pltpu.VMEM)
    tall, wide = (TOK, D), (D, TOK)
    return pl.pallas_call(
        enter_kernel,
        in_specs=[pl.BlockSpec(memory_space=pltpu.SMEM), any_spec(), any_spec(), vmem] + [any_spec()] * 4,
        out_specs=[any_spec()] * 6 + [vmem] * 4 + [any_spec()] * 4,
        out_shape=[S(tall, bf16), S(tall, bf16), S(tall, bf16), S(wide, bf16), S(tall, bf16), S(wide, bf16)]
        + [S((16, D), f32), S((8, TOK), f32), S((8, TOK), f32), S((BLK, BLK), f32)]
        + [S((D, 3 * D), bf16), S((D, D), bf16), S((CHUNKS, QUARTER, CHUNK), bf16), S((CHUNKS, 128, D), bf16)],
        scratch_shapes=[
            V((64, BLK), bf16), V((16, BLK), bf16), V(tall, bf16), V(tall, bf16), V(tall, f32), V(tall, bf16),
            V(wide, bf16), V(tall, bf16), V(wide, bf16), V((QUARTER, 3 * D), f32), V((QUARTER, D), f32),
            V((QUARTER, FF), f32), V((D, D), f32), V((QUARTER, 3 * D), bf16), V((QUARTER, D), bf16),
            V((CHUNKS, QUARTER, CHUNK), bf16), V((CHUNKS, 128, D), bf16), sem((3, 6)), sem((3, 6)), sem((3,)), sem((6,)),
            sem((8,)),
        ],
        compiler_params=pltpu.CompilerParams(vmem_limit_bytes=60 << 20, collective_id=cid, has_side_effects=True),
    )(lens, x, dy, vec, heads, output, expand, reduce)


def attention_kernel(
    x_ref, n1_ref, n1T_ref, dy_ref, wq_ref, wk_ref, wv_ref, wo_ref, vec_ref, cos_ref, sin_ref, mask_ref, eown, rown,
    hh_ref, og_ref, base_ref, grad_ref, vgrad_ref, efull, rfull,
    qT, kT, vT, oT, cT, gq, gk, gv, dn1T, ss, rs, ls,
):
    g = pl.program_id(0)
    ge = Gather(eown, efull, ss.at[0], rs.at[0], ls.at[0])
    gr = Gather(rown, rfull, ss.at[1], rs.at[1], ls.at[1])

    @pl.when(g == 0)
    def _():
        greet(gather_peers())
        ge.start()
        vgrad_ref[...] = jnp.zeros_like(vgrad_ref)

    @pl.when(g == 1)
    def _():
        ge.forward()

    @pl.when(g == 2)
    def _():
        ge.diag()

    heads = BLK // HEAD
    n1 = n1_ref[...]
    cos, sin = cos_ref[...], sin_ref[...]
    cols = pl.ds(pl.multiple_of(g * BLK, BLK), BLK)

    def column(row):
        return jnp.transpose(jnp.broadcast_to(vec_ref[row : row + 1, cols], (8, BLK)))[:, 0:1]

    def proj(w_ref, k):
        return dot(w_ref[...], n1, TT) + column(HEADS_BIAS + k)

    def rot(x):
        parts = []
        for h in range(heads):
            a, b = x[64 * h : 64 * h + 8], x[64 * h + 8 : 64 * h + 16]
            parts += [a * cos - b * sin, b * cos + a * sin, x[64 * h + 16 : 64 * h + 64]]
        return jnp.concatenate(parts, 0)

    def unrot(x):
        a, b = x[0:8], x[8:16]
        return jnp.concatenate([a * cos + b * sin, b * cos - a * sin, x[16:64]], 0)

    qT[...] = rot(proj(wq_ref, 0)).astype(bf16)
    kT[...] = rot(proj(wk_ref, 1)).astype(bf16)
    vT[...] = proj(wv_ref, 2).astype(bf16)
    oT[...] = dot(wo_ref[...], dy_ref[...], NT).astype(bf16)
    key = lax.broadcasted_iota(jnp.int32, (BLK, BLK), 0)
    query = lax.broadcasted_iota(jnp.int32, (BLK, BLK), 1)
    causal = key <= query
    scale = score_scale * LOG2E
    nb = TOK // BLK
    for h in range(heads):
        if h == 2:

            @pl.when(g == 0)
            def _():
                gr.start()

            @pl.when(g == 1)
            def _():
                gr.forward()

            @pl.when(g == 2)
            def _():
                gr.diag()

        r = slice(64 * h, 64 * h + 64)
        QT, KT, VT, OT = qT[r, :], kT[r, :], vT[r, :], oT[r, :]
        K, V = KT.T, VT.T
        dKT, dVT, dQT, context = [[] for _ in range(nb)], [[] for _ in range(nb)], [], []
        for j in range(nb):
            blocks = list(range(0 if j < nb - 1 else j, j + 1))
            span = [slice(BLK * b, BLK * b + BLK) for b in blocks]
            q, o = QT[:, BLK * j : BLK * j + BLK], OT[:, BLK * j : BLK * j + BLK]
            S = [dot(K[c], q) * scale for c in span]
            S[-1] = jnp.where(causal, S[-1], masked_score) if j < nb - 1 else S[-1] + mask_ref[...]
            top = functools.reduce(jnp.maximum, [jnp.max(s, 0, keepdims=True) for s in S])
            E = [jnp.exp2(s - top) for s in S]
            inv = 1.0 / total([jnp.sum(e, 0, keepdims=True) for e in E])
            soft = [e * inv for e in E]
            low = [p.astype(bf16) for p in soft]
            context.append(total([dot(VT[:, c], p) for c, p in zip(span, low)]).astype(bf16))
            back = [dot(V[c], o) for c in span]
            row = total([jnp.sum(d * p, 0, keepdims=True) for d, p in zip(back, soft)])
            dS = [(p * (d - row)).astype(bf16) for d, p in zip(back, soft)]
            dQT.append(total([dot(KT[:, c], s) for c, s in zip(span, dS)]) * score_scale)
            for b, p, s in zip(blocks, low, dS):
                dKT[b].append(dot(q, s, NT))
                dVT[b].append(dot(o, p, NT))
        cT[r, :] = jnp.concatenate(context, 1)
        gq[r, :] = unrot(jnp.concatenate(dQT, 1)).astype(bf16)
        gk[r, :] = unrot(jnp.concatenate([total(d) for d in dKT], 1) * score_scale).astype(bf16)
        gv[r, :] = jnp.concatenate([total(d) for d in dVT], 1).astype(bf16)
    n1T = n1T_ref[...]
    ones = jnp.ones((8, TOK), bf16)
    parts = []
    for k, (grads, w_ref) in enumerate(((gq, wq_ref), (gk, wk_ref), (gv, wv_ref))):
        G = grads[...]
        hh_ref[k] = dot(n1T, G, NT)
        vgrad_ref[HEADS_BIAS + k : HEADS_BIAS + k + 1, cols] = dot(ones, G, NT)[0:1]
        parts.append(dot(w_ref[...], G))
    ctx = cT[...]
    og_ref[...] = dot(ctx, dy_ref[...])
    out = dot(ctx, wo_ref[...], TN)

    @pl.when(g == 0)
    def _():
        bias = vec_ref[OUTPUT_BIAS : OUTPUT_BIAS + 1] + vec_ref[REDUCE_BIAS : REDUCE_BIAS + 1]
        base_ref[...] = out + (x_ref[...].astype(f32) + bias)
        dn1T[...] = total(parts)

    @pl.when(g > 0)
    def _():
        base_ref[...] += out
        dn1T[...] += total(parts)

    @pl.when(g == D // BLK - 1)
    def _():
        dy = dy_ref[...].astype(f32)
        back, gain, shift = norm_back(x_ref[...].astype(f32), vec_ref[GAIN_ONE : GAIN_ONE + 1], dn1T[...].T)
        grad_ref[...] = dy + back
        up = jnp.sum(dy, 0, keepdims=True)
        vgrad_ref[GAIN_ONE : GAIN_ONE + 1] = gain
        vgrad_ref[SHIFT_ONE : SHIFT_ONE + 1] = shift
        vgrad_ref[OUTPUT_BIAS : OUTPUT_BIAS + 1] = up
        vgrad_ref[REDUCE_BIAS : REDUCE_BIAS + 1] = up
        ge.finish()
        gr.finish()


def attention(x, n1, n1T, dy, W, Wo, vec, cos, sin, mask, eown, rown, cid):
    G = D // BLK
    S, V = jax.ShapeDtypeStruct, pltpu.VMEM
    block = lambda k: pl.BlockSpec((D, BLK), lambda g: (0, k * G + g))
    rows = pl.BlockSpec((BLK, D), lambda g: (g, 0))
    sem = pltpu.SemaphoreType.DMA
    return pl.pallas_call(
        attention_kernel,
        grid=(G,),
        in_specs=[
            whole((TOK, D)), whole((TOK, D)), whole((D, TOK)), whole((TOK, D)), block(0), block(1), block(2), rows,
            whole((16, D)), whole((8, TOK)), whole((8, TOK)), whole((BLK, BLK)),
            whole(eown.shape), whole(rown.shape),
        ],
        out_specs=[
            pl.BlockSpec((3, D, BLK), lambda g: (0, 0, g)), rows, whole((TOK, D)), whole((TOK, D)), whole((16, D)),
            any_spec(), any_spec(),
        ],
        out_shape=[
            S((3, D, D), f32), S((D, D), f32), S((TOK, D), f32), S((TOK, D), f32), S((16, D), f32),
            S((CHUNKS, D, CHUNK), bf16), S((CHUNKS, CHUNK, D), bf16),
        ],
        scratch_shapes=[V((BLK, TOK), bf16)] * 8 + [V((D, TOK), f32), sem((2, 6)), sem((2, 6)), sem((2,))],
        compiler_params=pltpu.CompilerParams(vmem_limit_bytes=60 << 20, collective_id=cid, has_side_effects=True),
    )(x, n1, n1T, dy, W, W, W, Wo, vec, cos, sin, mask, eown, rown)


def feed_kernel(
    digits, n2_ref, n2T_ref, dy_ref, x_ref, vec_ref, we_ref, wr_ref, base_hbm, grad_hbm, hh, og, vg_ref,
    out_ref, token_ref, sum_h, sum_e, sum_r, sum_v,
    gh, gx, gr, gv, os, acc, dn2, act_ref, hid_ref, bge, ex, rx, vx, hx, ls, bs, *scratch,
):
    t = pl.program_id(0)
    c = place()[2]
    parts = [scratch[STREAM * i : STREAM * i + STREAM] for i in range(4)]

    def stream(i, mine, other, gout):
        return Reduce(digits, mine, other, *parts[i][:9], gout, parts[i][9], parts[i][10])

    def half(k, core, do):
        @pl.when(k < 3)
        def _():
            do(hh.at[k, :, core])

        @pl.when(k == 3)
        def _():
            do(og.at[0, :, core])

    H = stream(0, lambda k: hx.at[k % 2], None, gh)
    E = stream(1, lambda k: ex.at[:, c], lambda k: ex.at[:, 1 - c], gx)
    R = stream(2, lambda k: rx.at[:, c], lambda k: rx.at[:, 1 - c], gr)
    Z = stream(3, lambda k: vx.at[:, c], lambda k: vx.at[:, 1 - c], gv)

    sums = ((gh, sum_h), (gx, sum_e), (gr, sum_r), (gv, sum_v))

    def hand(i, k):
        return pltpu.make_async_copy(sums[i][0].at[k], sums[i][1].at[k], os.at[i, k])

    def load_base():
        return pltpu.make_async_copy(base_hbm, acc, bs.at[0])

    def load_grad():
        return pltpu.make_async_copy(grad_hbm, acc, bs.at[1])

    @pl.when(t == 0)
    def _():
        greet(reduce_peers(digits))
        load_base().start()

    last = len(E.stage_list()) - 1
    streams = ((H, 4, 0), (E, CHUNKS, 0), (R, CHUNKS, 0), (Z, 1, CHUNKS - 1))

    def advance(i):
        s, n, first = streams[i]
        for j in range(last, 0, -1):

            @pl.when((t >= j + first) & (t < j + first + n))
            def _():
                k = t - j - first
                if i == 0 and j == 1:
                    pltpu.make_async_copy(hh.at[0, :, c], hx.at[k % 2], ls.at[k]).wait()
                    s.other = lambda k: hx.at[k % 2]
                s.stage_list()[j](k)
                if j == last:
                    hand(i, k).start()

    advance(0)

    @pl.when(t < 4)
    def _():
        half(t, c, lambda src: pltpu.make_async_copy(src, hx.at[t % 2], ls.at[t]).start())
        half(t, 1 - c, lambda src: H.cp(0, t, src, H.Y.at[t % 2], H.s, H.sib).start())

    @pl.when(t < CHUNKS)
    def _():
        n2, dy, we, wr = n2_ref[...], dy_ref[...], we_ref[0], wr_ref[0]
        bias = jnp.concatenate(
            [vec_ref[EXPAND_BIAS + s : EXPAND_BIAS + s + 1, pl.ds(pl.multiple_of(t * 128, 128), 128)] for s in range(4)], 1
        )
        h = dot(n2, we) + bias
        cdf = 0.5 * (1.0 + lax.erf(h * 0.7071067811865476))
        pdf = jnp.exp2(h * h * (-0.5 * LOG2E)) * 0.3989422804014327
        act_ref[...] = (h * cdf).astype(bf16)
        hid_ref[...] = hidden = (dot(dy, wr, NT) * (cdf + h * pdf)).astype(bf16)
        bge[pl.ds(t, 1)] = jnp.sum(hidden.astype(f32), 0, keepdims=True)[None]

    advance(2)

    @pl.when(t < CHUNKS)
    def _():
        rx[...] = dot(act_ref[...], dy_ref[...], TN).reshape(rx.shape)
        R.s0(t)

    advance(1)

    @pl.when(t < CHUNKS)
    def _():
        hidden = hid_ref[...]
        ex[...] = dot(n2T_ref[...], hidden).reshape(ex.shape)
        E.s0(t)
        out = dot(act_ref[...], wr_ref[0])
        back = dot(hidden, we_ref[0], NT)

        @pl.when(t == 0)
        def _():
            load_base().wait()
            dn2[...] = back

        @pl.when(t > 0)
        def _():
            dn2[...] += back

        acc[...] += out

    advance(3)

    @pl.when(t == CHUNKS - 1)
    def _():
        block = acc[...].astype(bf16)
        load_grad().start()
        back, gain, shift = norm_back(x_ref[...].astype(f32), vec_ref[GAIN_TWO : GAIN_TWO + 1], dn2[...])
        rows = {k: vg_ref[k : k + 1] for k in range(VEC_ROWS) if k not in (2, 3, 8, 9, 10, 11)}
        rows[GAIN_TWO], rows[SHIFT_TWO] = gain, shift
        for s in range(4):
            rows[EXPAND_BIAS + s] = jnp.concatenate([bge[g, :, 128 * s : 128 * s + 128] for g in range(CHUNKS)], 1)
        vx[...] = jnp.zeros_like(vx)
        for i in range(VEC_ROWS * 4):
            s, row = i // VEC_ROWS, i % VEC_ROWS
            vx[s, row // 8, row % 8 : row % 8 + 1, 0:SEG] = rows[i // 4][:, SEG * (i % 4) : SEG * (i % 4) + SEG]
        Z.s0(0)
        load_grad().wait()
        token = (acc[...] + back).astype(bf16)
        out_ref[...] = block
        token_ref[...] = token

    @pl.when(t == pl.num_programs(0) - 1)
    def _():
        for i, n in enumerate((4, CHUNKS, CHUNKS, 1)):
            for k in range(n):
                hand(i, k).wait()


def feed(n2, n2T, dy, x, vec, We, Wr, base, grad, hh, og, vgrad, digits, cid):
    S, V, sem = jax.ShapeDtypeStruct, pltpu.VMEM, pltpu.SemaphoreType.DMA
    nd = len(digits)
    steps = CHUNKS + 4 + 3 * nd
    at = lambda t: jnp.minimum(t, CHUNKS - 1)
    vmem = pl.BlockSpec(memory_space=pltpu.VMEM)
    shapes = [((4, 2, 96, D), f32), ((CHUNKS, 2, 96, CHUNK), bf16), ((CHUNKS, 2, 64, D), bf16), ((1, 2, 8, BLK), f32)]
    return pl.pallas_call(
        functools.partial(feed_kernel, digits),
        grid=(steps,),
        in_specs=[
            whole((TOK, D)), whole((D, TOK)), whole((TOK, D)), whole((TOK, D)), whole((16, D)),
            pl.BlockSpec((1, D, CHUNK), lambda t: (at(t), 0, 0)), pl.BlockSpec((1, CHUNK, D), lambda t: (at(t), 0, 0)),
            any_spec(), any_spec(), any_spec(), any_spec(), whole((16, D)),
        ],
        out_specs=[whole((TOK, D)), whole((TOK, D))] + [any_spec() for _ in shapes],
        out_shape=[S((TOK, D), bf16), S((TOK, D), bf16)] + [S(s, k) for s, k in shapes],
        scratch_shapes=[V(s, k) for s, k in shapes] + [
            sem((4, CHUNKS)), V((TOK, D), f32), V((TOK, D), f32), V((TOK, CHUNK), bf16), V((TOK, CHUNK), bf16), V((CHUNKS, 1, CHUNK), f32), V((4, 2, 96, CHUNK), f32),
            V((4, 2, 64, D), f32), V((4, 2, 8, BLK), f32), V((2, 4, 96, D), f32), sem((4,)), sem((2,)),
        ]
        + stream_scratch(4, 96, D, nd, bf16) + stream_scratch(CHUNKS, 96, CHUNK, nd, bf16)
        + stream_scratch(CHUNKS, 64, D, nd, bf16) + stream_scratch(1, 8, BLK, nd, f32),
        compiler_params=pltpu.CompilerParams(vmem_limit_bytes=63 << 20, collective_id=cid, has_side_effects=True),
    )(n2, n2T, dy, x, vec, We, Wr, base, grad, hh, og, vgrad)


def adam_step(master, moment, square, gradient, rate, decay):
    momentum = first_decay * moment + (1.0 - first_decay) * gradient
    squares = second_decay * square + (1.0 - second_decay) * gradient * gradient
    first_fix = momentum / (1.0 - first_decay**STEP)
    second_fix = squares / (1.0 - second_decay**STEP)
    updated = master - rate * (first_fix / (jnp.sqrt(second_fix) + adam_epsilon) + decay * master)
    return (momentum, squares, updated)


def leave_kernel(lens, block, token, sh, so, se, sr, sv, *refs):
    ins, outs = refs[:15], refs[15:]
    g = pl.program_id(0)

    @pl.when(g < TOK // BLK)
    def _():
        first, second = lens[0, 0], lens[0, 1]
        start = jnp.where(first == LONG, 0, jnp.where(second == LONG, first, first + second))
        want = lax.broadcasted_iota(jnp.int32, (BLK, TOK), 0) + (g * BLK - start)
        want = jnp.where(want < 0, want + TOK, want)
        turn = (want == lax.broadcasted_iota(jnp.int32, (BLK, TOK), 1)).astype(bf16)
        rows = pl.ds(pl.multiple_of(g * BLK, BLK), BLK)
        outs[0][rows] = dot(turn, block[...]).astype(bf16)
        outs[1][rows] = dot(turn, token[...]).astype(bf16)

    def step(i, gradient, rate, decay):
        new = adam_step(*(ins[3 * i + j][...] for j in range(3)), gradient, rate, decay)
        for j in range(3):
            outs[2 + 3 * i + j][...] = new[j]

    step(0, sh[0].reshape(QUARTER, -1), matrix_rate, matrix_decay)
    step(1, so[0].reshape(QUARTER, -1), matrix_rate, matrix_decay)
    pieces = []
    for i in range(4):
        b = 4 * g + i
        at = pl.ds(pl.multiple_of(b // CHUNKS * 128, 128), 128)
        pieces.append(se[b % CHUNKS, :, :, at].astype(f32).reshape(QUARTER, 128))
    step(2, jnp.concatenate(pieces, 1), matrix_rate, matrix_decay)
    step(3, sr[...].astype(f32), matrix_rate, matrix_decay)

    @pl.when(g == 0)
    def _():
        step(4, sv[...], vector_rate, 0.0)


def leave(lens, block, token, sums, state):
    S = jax.ShapeDtypeStruct
    sh, se, sr, sv = sums
    still = lambda shape: pl.BlockSpec(shape, lambda g: (0,) * len(shape))
    specs = [
        pl.BlockSpec((QUARTER, D // 2), lambda g: (0, g)), pl.BlockSpec((QUARTER, 128), lambda g: (0, g)),
        pl.BlockSpec((QUARTER, CHUNK), lambda g: (0, g)), pl.BlockSpec((128, D), lambda g: (g, 0)),
        still((VEC_ROWS, SEG)),
    ]
    sums_specs = [
        pl.BlockSpec((1, 2, 96, D // 2), lambda g: (g // 2, 0, 0, g % 2)),
        pl.BlockSpec((1, 2, 96, 128), lambda g: (3, 0, 0, g)),
        still(se.shape), pl.BlockSpec((128, D), lambda g: (g, 0)), still((VEC_ROWS, SEG)),
    ]
    shapes = [S((QUARTER, 3 * D), f32), S((QUARTER, D), f32), S((QUARTER, FF), f32), S((D, D), f32), S((VEC_ROWS, SEG), f32)]
    return pl.pallas_call(
        leave_kernel,
        grid=(CHUNKS,),
        in_specs=[pl.BlockSpec(memory_space=pltpu.SMEM), whole((TOK, D)), whole((TOK, D))] + sums_specs
        + [s for s in specs for _ in range(3)],
        out_specs=[whole((TOK, D))] * 2 + [s for s in specs for _ in range(3)],
        out_shape=[S((TOK, D), bf16)] * 2 + [s for s in shapes for _ in range(3)],
        compiler_params=pltpu.CompilerParams(vmem_limit_bytes=60 << 20),
    )(lens, block, token, sh, sh, se, sr.reshape(D, D), sv.reshape(16, BLK)[:VEC_ROWS, :SEG], *state)


def per_device(
    tokens,
    lengths,
    cotangent,
    heads_master,
    output_master,
    expand_master,
    reduce_master,
    vector_master,
    heads_moment,
    output_moment,
    expand_moment,
    reduce_moment,
    vector_moment,
    heads_square,
    output_square,
    expand_square,
    reduce_square,
    vector_square,
):
    digits = ring_of(lax.axis_size("dp"))
    (x, dy, n1, n1T, n2, n2T, vectors, cos, sin, mask, heads_weight, output_weight, expand_own, reduce_own) = enter(
        lengths, tokens, cotangent, vector_master.reshape(VEC_ROWS, SEG), heads_master, output_master, expand_master,
        reduce_master, 1)
    heads_grad, output_grad, base, grad, vector_grad, expand_weight, reduce_weight = attention(
        x, n1, n1T, dy, heads_weight, output_weight, vectors, cos, sin, mask, expand_own, reduce_own, 2)
    block, token, *sums = feed(
        n2, n2T, dy, x, vectors, expand_weight, reduce_weight, base, grad, heads_grad.reshape(3, 4, 2, 96, D),
        output_grad.reshape(1, 4, 2, 96, D), vector_grad, digits, 3)
    state = [
        heads_master, heads_moment, heads_square, output_master, output_moment, output_square,
        expand_master, expand_moment, expand_square, reduce_master, reduce_moment, reduce_square,
    ] + [v.reshape(VEC_ROWS, SEG) for v in (vector_master, vector_moment, vector_square)]
    out = leave(lengths, block, token, sums, state)
    return tuple(out[:14]) + tuple(v.reshape(-1) for v in out[14:])


def solution(mesh):
    placed = (
        P(("shard", "dp"), None),
        P(("shard", "dp"), None),
        P(("shard", "dp"), None),
        P("shard", None),
        P("shard", None),
        P("shard", None),
        P("shard", None),
        P("shard"),
        P("shard", None),
        P("shard", None),
        P("shard", None),
        P("shard", None),
        P("shard"),
        P("shard", None),
        P("shard", None),
        P("shard", None),
        P("shard", None),
        P("shard"),
    )
    return jax.shard_map(
        per_device,
        mesh=mesh,
        in_specs=placed,
        out_specs=(
            P(("shard", "dp"), None),
            P(("shard", "dp"), None),
            P("shard", None),
            P("shard", None),
            P("shard", None),
            P("shard", None),
            P("shard", None),
            P("shard", None),
            P("shard", None),
            P("shard", None),
            P("shard", None),
            P("shard", None),
            P("shard", None),
            P("shard", None),
            P("shard"),
            P("shard"),
            P("shard"),
        ),
        check_vma=False,
    )
```

```python
import functools

import jax
import jax.numpy as jnp
from jax import lax
from jax.experimental import pallas as pl
from jax.experimental.pallas import tpu as pltpu
from jax.sharding import PartitionSpec as P

D = 768
HEADS = 12
HEAD = 64
ROT = 16
FF = 3072
STEP = 10
TOK = 1024
LONG = 768
BLK = 256
CHUNK = 512
BW = CHUNK // 4
HPART = 48
HPARTS = 3 * 96 // HPART
CHUNKS = FF // CHUNK
QUARTER = D // 4
SEG = 192
TILE = 128
ATILE = 256
AROWS = 48
FTILE = 512

first_decay = 0.9
second_decay = 0.95
adam_epsilon = 1e-08
matrix_decay = 0.1
matrix_rate = 0.04
vector_rate = 0.2
norm_epsilon = 1e-05
score_scale = 0.125
rotary_base = 10000.0
masked_score = -1e30
LOG2E = 1.4426950408889634

f32 = jnp.float32
bf16 = jnp.bfloat16
MESH = pl.DeviceIdType.MESH
NN = (((1,), (0,)), ((), ()))
NT = (((1,), (1,)), ((), ()))
TN = (((0,), (0,)), ((), ()))
TT = (((0,), (1,)), ((), ()))

GAIN_ONE, SHIFT_ONE, GAIN_TWO, SHIFT_TWO, HEADS_BIAS, OUTPUT_BIAS, EXPAND_BIAS, REDUCE_BIAS = 0, 1, 2, 3, 4, 7, 8, 12
VEC_ROWS = 13


def dot(a, b, dims=NN):
    return lax.dot_general(a, b, dims, preferred_element_type=f32)


def total(parts):
    return functools.reduce(jnp.add, parts)


def any_spec():
    return pl.BlockSpec(memory_space=pl.ANY)


def whole(shape):
    return pl.BlockSpec(shape, lambda g: (0,) * len(shape), pipeline_mode=pl.Buffered(1))


def norm_rows(values):
    centred = values - jnp.mean(values, -1, keepdims=True)
    inverse = lax.rsqrt(jnp.mean(centred * centred, -1, keepdims=True) + norm_epsilon)
    return centred * inverse, inverse


def norm_back(values, gain, grad):
    normed, inverse = norm_rows(values)
    scaled = grad * gain
    back = inverse * (
        scaled - jnp.mean(scaled, -1, keepdims=True) - normed * jnp.mean(scaled * normed, -1, keepdims=True)
    )
    return back, jnp.sum(grad * normed, 0, keepdims=True), jnp.sum(grad, 0, keepdims=True)


def place():
    s=lax.axis_index("shard"); d=lax.axis_index("dp")
    c=d%2
    s1=s+1-2*(s%2); s2=s+2-4*(s//2)
    a=(1-c)*s1+c*s2
    b=(1-c)*s2+c*s1
    return s,d,c,a,b

def rcopy(src,dst,ssem,rsem,sh,dp):
    return pltpu.make_async_remote_copy(src_ref=src,dst_ref=dst,send_sem=ssem,recv_sem=rsem,device_id=(sh,dp),device_id_type=MESH)

def greet(peers):
    bar=pltpu.get_barrier_semaphore()
    for sh,dp in peers:
        pl.semaphore_signal(bar,inc=1,device_id=(sh,dp),device_id_type=MESH)
    pl.semaphore_wait(bar,len(peers))

class Gather:
    def __init__(self,own,full,ssem,rsem,lsem,split=True):
        self.own,self.full,self.ss,self.rs,self.ls=own,full,ssem,rsem,lsem
        self.s,self.d,self.c,self.a,self.b=place()
        self.sib=self.d+1-2*self.c
        self.R=own.shape[-2]; self.split=split
        self.h=self.R//2 if split else self.R
    def sl(self,ref,row,n):
        row=pl.multiple_of(row,16)
        if len(ref.shape)==2: return ref.at[pl.ds(row,n)]
        return ref.at[:,pl.ds(row,n)]
    def region(self,sh,core):
        return self.sl(self.full,sh*self.R+(core*self.h if self.split else 0),self.h)
    def mine(self):
        return self.sl(self.own,self.c*self.h if self.split else 0,self.h)
    def cp(self,k,src,reg,sh,dp): return rcopy(src,reg,self.ss.at[k],self.rs.at[k],sh,dp)
    def local(self):
        return pltpu.make_async_copy(self.own,self.sl(self.full,self.s*self.R,self.R),self.ls)
    def start(self):
        r=self.region(self.s,self.c)
        self.cp(0,self.mine(),r,self.a,self.d).start()
        self.cp(1,self.mine(),r,self.b,self.d).start()
        self.local().start()
    def _wait_recv(self,k,sh,core):
        r=self.region(sh,core)
        self.cp(k,r,r,self.s,self.sib).wait_recv()
    def _wait_send(self,k,sh,core):
        r=self.region(sh,core)
        self.cp(k,r,r,self.s,self.sib).wait_send()
    def forward(self):
        ra=self.region(self.a,self.c)
        self._wait_recv(0,self.a,self.c)
        self.cp(2,ra,ra,self.b,self.d).start()
        if self.split: self.cp(3,ra,ra,self.s,self.sib).start()
        self._wait_recv(1,self.b,self.c)
        rb=self.region(self.b,self.c)
        if self.split: self.cp(4,rb,rb,self.s,self.sib).start()
    def diag(self):
        x=3-self.s
        self._wait_recv(2,x,self.c)
        rx=self.region(x,self.c)
        if self.split: self.cp(5,rx,rx,self.s,self.sib).start()
    def finish(self):
        self.local().wait()
        x=3-self.s
        if self.split:
            o=1-self.c
            self._wait_recv(3,self.b,o)
            self._wait_recv(4,self.a,o)
            self._wait_recv(5,x,o)
        self.cp(0,self.mine(),self.region(self.s,self.c),self.a,self.d).wait_send()
        self.cp(1,self.mine(),self.region(self.s,self.c),self.b,self.d).wait_send()
        for k,sh in ((2,self.a),)+(((3,self.a),(4,self.b),(5,x)) if self.split else ()):
            self._wait_send(k,sh,self.c)

def gather_peers():
    s,d,c,a,b=place()
    return [(a,d),(b,d),(s,d+1-2*c)]

def ring_of(dp_size):
    digits=[]; n=dp_size//2; stride=1
    while n>1:
        assert n%4==0
        digits.append(stride); stride*=4; n//=4
    return digits

class Reduce:
    def __init__(self,digits,mine,other,Y,SA,RA,T,SB,RB,SZ,RZ,RM,gout,ss,rs):
        self.digits=digits; self.mine=mine; self.other=other
        self.Y,self.SA,self.RA,self.T,self.SB,self.RB,self.SZ,self.RZ,self.RM,self.gout,self.ss,self.rs=Y,SA,RA,T,SB,RB,SZ,RZ,RM,gout,ss,rs
        self.s,self.d,self.c,self.a,self.b=place()
        self.sib=self.d+1-2*self.c
        self.x=3-self.s
    def cp(self,j,k,src,dst,sh,dp): return rcopy(src,dst,self.ss.at[j,k],self.rs.at[j,k],sh,dp)
    def role(self,i):
        st=self.digits[i]; p=((self.d//2)//st)%4
        end=(p==0)|(p==3)
        mate=self.d+2*st*jnp.where(p==0,1,jnp.where(p==3,-1,jnp.where(p==1,1,-1)))
        tip=self.d+2*st*jnp.where(p==1,-1,1)
        return end,mate,tip
    def stages(self): return 4+3*len(self.digits)+1
    def c0(self,k): return self.cp(0,k,self.other(k),self.Y.at[k%2],self.s,self.sib)
    def cA(self,k): return self.cp(1,k,self.SA.at[k%2],self.RA.at[k%2],self.a,self.d)
    def cB(self,k): return self.cp(2,k,self.SB.at[k%2],self.RB.at[k%2],self.b,self.d)
    def nt(self,k): return k%self.T.shape[0]
    def s0(self,k):
        self.c0(k).start()
    def s1(self,k):
        self.c0(k).wait()
        X=self.mine(k)
        def U(p): return X[p]+self.Y[k%2,p]
        self.SA[k%2,0]=U(self.a).astype(self.SA.dtype)
        self.SA[k%2,1]=U(self.x).astype(self.SA.dtype)
        self.cA(k).start()
        t=self.nt(k)
        self.T[t,0]=U(self.s)
        self.T[t,1]=U(self.b)
    def s2(self,k):
        self.cA(k).wait()
        t=self.nt(k)
        self.SB[k%2]=(self.T[t,1]+self.RA[k%2,1].astype(f32)).astype(self.SB.dtype)
        self.cB(k).start()
        self.T[t,0]=self.T[t,0]+self.RA[k%2,0].astype(f32)
    def s3(self,k):
        self.cB(k).wait()
        t=self.nt(k)
        self.T[t,0]=self.T[t,0]+self.RB[k%2].astype(f32)
        self.za(0,k)
    def g(self,k): return self.gout.at[k,self.c]
    def zcp(self,i,j,k,src,dst,dp): return self.cp(3+4*i+j,k,src,dst,self.s,dp)
    def za(self,i,k):
        t=self.nt(k); end,mate,tip=self.role(i)
        @pl.when(end)
        def _():
            self.SZ[i,k%2]=self.T[t,0].astype(self.SZ.dtype)
            self.zcp(i,0,k,self.SZ.at[i,k%2],self.RZ.at[i,k%3],mate).start()
    def zb(self,i,k):
        t=self.nt(k); end,mate,tip=self.role(i)
        @pl.when(jnp.logical_not(end))
        def _():
            self.zcp(i,0,k,self.SZ.at[i,k%2],self.RZ.at[i,k%3],tip).wait_recv()
            self.SZ[i,k%2]=(self.T[t,0]+self.RZ[i,k%3].astype(f32)).astype(self.SZ.dtype)
            self.zcp(i,1,k,self.SZ.at[i,k%2],self.RM.at[i,k%2],mate).start()
        @pl.when(end)
        def _():
            self.zcp(i,0,k,self.SZ.at[i,k%2],self.RZ.at[i,k%3],mate).wait_send()
    def to_sib(self,k):
        return self.cp(3+4*len(self.digits),k,self.g(k),self.g(k),self.s,self.sib)
    def zc(self,i,k):
        end,mate,tip=self.role(i); last=i==len(self.digits)-1
        @pl.when(jnp.logical_not(end))
        def _():
            self.zcp(i,1,k,self.SZ.at[i,k%2],self.RM.at[i,k%2],mate).wait()
            self.gout[k,self.c]=(self.SZ[i,k%2].astype(f32)+self.RM[i,k%2].astype(f32)).astype(self.gout.dtype)
            self.zcp(i,2,k,self.g(k),self.g(k),tip).start()
            if last: self.to_sib(k).start()
    def zd(self,i,k):
        end,mate,tip=self.role(i); last=i==len(self.digits)-1
        @pl.when(jnp.logical_not(end))
        def _():
            self.zcp(i,2,k,self.g(k),self.g(k),tip).wait_send()
        @pl.when(end)
        def _():
            self.zcp(i,2,k,self.g(k),self.g(k),mate).wait_recv()
            if last: self.to_sib(k).start()
        if not last:
            self.T[self.nt(k),0]=self.gout[k,self.c].astype(f32)
            self.za(i+1,k)
    def fin(self,k):
        self.to_sib(k).wait_send()
        g=self.gout.at[k,1-self.c]
        self.cp(3+4*len(self.digits),k,g,g,self.s,self.sib).wait_recv()
    def stage_list(self):
        out=[self.s0,self.s1,self.s2,self.s3]
        for i in range(len(self.digits)):
            out+=[functools.partial(self.zb,i),functools.partial(self.zc,i),functools.partial(self.zd,i)]
        return out+[self.fin]

def reduce_peers(digits):
    s,d,c,a,b=place()
    peers=[(a,d),(b,d),(s,d+1-2*c)]
    for st in digits:
        p=((d//2)//st)%4
        up=d+2*st*jnp.where(p==3,-3,1); down=d+2*st*jnp.where(p==0,3,-1)
        peers+=[(s,up),(s,down)]
    return peers

def stream_scratch(n, r, w, nd, kind):
    V, S = pltpu.VMEM, pltpu.SemaphoreType.DMA
    ring = min(n, 4 + 3 * (nd - 1))
    return [
        V((2, 4, r, w), f32), V((2, 2, r, w), kind), V((2, 2, r, w), kind), V((ring, 2, r, w), f32),
        V((2, r, w), kind), V((2, r, w), kind), V((nd, 2, r, w), kind), V((nd, 3, r, w), kind), V((nd, 2, r, w), kind),
        S((4 + 4 * nd, n)), S((4 + 4 * nd, n)),
    ]


STREAM = 11


def enter_kernel(
    lens, x_hbm, dy_hbm, vec_own, heads_hbm, output_hbm, expand_hbm, reduce_hbm,
    x_out, dy_out, n1_out, n1T_out, n2_out, n2T_out, vec_ref, bias_ref, cos_ref, sin_ref, mask_ref, heads_full, output_full, e_out, r_out,
    vec_full, vec_low, xs, ds, normed, n1, n1T, n2, n2T, heads_in, output_in, expand_in, reduce_in, heads_own, output_own,
    eown, rown, ss, rs, ls, ins, outs,
):
    loads = [
        pltpu.make_async_copy(src, dst, ins.at[i])
        for i, (src, dst) in enumerate((
            (heads_hbm, heads_in), (output_hbm, output_in), (x_hbm, xs), (dy_hbm, ds), (expand_hbm, expand_in),
            (reduce_hbm, reduce_in),
        ))
    ]
    stores = [
        pltpu.make_async_copy(src, dst, outs.at[i])
        for i, (src, dst) in enumerate((
            (xs, x_out), (ds, dy_out), (n1, n1_out), (n1T, n1T_out), (n2, n2_out), (n2T, n2T_out), (eown, e_out),
            (rown, r_out),
        ))
    ]
    for copy in loads:
        copy.start()
    gv = Gather(vec_low, vec_full, ss.at[0], rs.at[0], ls.at[0], False)
    gh = Gather(heads_own, heads_full, ss.at[1], rs.at[1], ls.at[1])
    go = Gather(output_own, output_full, ss.at[2], rs.at[2], ls.at[2])
    vec_low[...] = jnp.zeros_like(vec_low)
    vec_low[0:VEC_ROWS, 0:SEG] = vec_own[...].astype(bf16)
    greet(gather_peers())
    gv.start()
    loads[0].wait()
    heads_own[...] = heads_in[...].astype(bf16)
    gh.start()
    loads[1].wait()
    output_own[...] = output_in[...].astype(bf16)
    go.start()
    first, second, third = lens[0, 0], lens[0, 1], lens[0, 2]
    start = jnp.where(first == LONG, 0, jnp.where(second == LONG, first, first + second))
    short = jnp.where(first == LONG, second, jnp.where(second == LONG, third, first))
    from_row = lax.broadcasted_iota(jnp.int32, (BLK, TOK), 1)

    def turn(ref):
        values, parts = ref[...], []
        for i in range(TOK // BLK):
            want = lax.broadcasted_iota(jnp.int32, (BLK, TOK), 0) + (i * BLK + start)
            want = jnp.where(want >= TOK, want - TOK, want)
            parts.append(dot((want == from_row).astype(bf16), values).astype(bf16))
        for i, part in enumerate(parts):
            ref[BLK * i : BLK * i + BLK] = part

    loads[2].wait()
    turn(xs)
    stores[0].start()
    for i in range(TOK // BLK):
        normed[BLK * i : BLK * i + BLK] = norm_rows(xs[BLK * i : BLK * i + BLK].astype(f32))[0]
    gv.forward()
    loads[3].wait()
    turn(ds)
    stores[1].start()
    gv.diag()
    row = lax.broadcasted_iota(jnp.int32, (8, TOK), 1)
    late = row - LONG
    position = jnp.where(late < 0, row, jnp.where(late >= short, late - short, late)).astype(f32)
    step = lax.broadcasted_iota(jnp.int32, (8, TOK), 0).astype(f32)
    angles = position * jnp.exp2(step * (-2.0 / ROT * 13.287712379549449))
    cos_ref[...] = jnp.cos(angles)
    sin_ref[...] = jnp.sin(angles)
    key = lax.broadcasted_iota(jnp.int32, (BLK, BLK), 0)
    query = lax.broadcasted_iota(jnp.int32, (BLK, BLK), 1)
    allowed = ((key >= short) == (query >= short)) & (key <= query)
    mask_ref[...] = jnp.where(allowed, 0.0, masked_score)
    gv.finish()
    vec_ref[...] = jnp.zeros_like(vec_ref)
    for i in range(4 * VEC_ROWS):
        s, r = i // VEC_ROWS, i % VEC_ROWS
        piece = vec_full[16 * s : 16 * s + 16].astype(f32)[r : r + 1, 0:SEG]
        vec_ref[i // 4 : i // 4 + 1, SEG * (i % 4) : SEG * (i % 4) + SEG] = piece
    for g in range(CHUNKS):
        for s in range(4):
            bias_ref[g, :, BW * s : BW * s + BW] = vec_ref[EXPAND_BIAS + s : EXPAND_BIAS + s + 1, BW * g : BW * g + BW]
    gh.forward()
    for out, outT, gain, shift, k in ((n1, n1T, GAIN_ONE, SHIFT_ONE, 2), (n2, n2T, GAIN_TWO, SHIFT_TWO, 4)):
        for i in range(TOK // BLK):
            rows = slice(BLK * i, BLK * i + BLK)
            low = (normed[rows] * vec_ref[gain : gain + 1] + vec_ref[shift : shift + 1]).astype(bf16)
            out[rows] = low
            outT[:, rows] = low.T
        stores[k].start()
        stores[k + 1].start()
        if k == 2:
            go.forward()
            gh.diag()
    loads[4].wait()
    for g in range(CHUNKS):
        for s in range(4):
            eown[g, :, BW * s : BW * s + BW] = expand_in[:, D * s + BW * g : D * s + BW * g + BW].astype(bf16)
    stores[6].start()
    loads[5].wait()
    rown[...] = reduce_in[...].astype(bf16).reshape(rown.shape)
    stores[7].start()
    go.diag()
    gh.finish()
    go.finish()
    for copy in stores:
        copy.wait()


def enter(lens, x, dy, vec, heads, output, expand, reduce, cid):
    S, V, sem = jax.ShapeDtypeStruct, pltpu.VMEM, pltpu.SemaphoreType.DMA
    vmem = pl.BlockSpec(memory_space=pltpu.VMEM)
    tall, wide = (TOK, D), (D, TOK)
    return pl.pallas_call(
        enter_kernel,
        in_specs=[pl.BlockSpec(memory_space=pltpu.SMEM), any_spec(), any_spec(), vmem] + [any_spec()] * 4,
        out_specs=[any_spec()] * 6 + [vmem] * 5 + [any_spec()] * 4,
        out_shape=[S(tall, bf16), S(tall, bf16), S(tall, bf16), S(wide, bf16), S(tall, bf16), S(wide, bf16)]
        + [S((16, D), f32), S((CHUNKS, 1, CHUNK), f32), S((8, TOK), f32), S((8, TOK), f32), S((BLK, BLK), f32)]
        + [S((D, 3 * D), bf16), S((D, D), bf16), S((CHUNKS, QUARTER, CHUNK), bf16), S((CHUNKS, BW, D), bf16)],
        scratch_shapes=[
            V((64, BLK), bf16), V((16, BLK), bf16), V(tall, bf16), V(tall, bf16), V(tall, f32), V(tall, bf16),
            V(wide, bf16), V(tall, bf16), V(wide, bf16), V((QUARTER, 3 * D), f32), V((QUARTER, D), f32),
            V((QUARTER, FF), f32), V((D, D), f32), V((QUARTER, 3 * D), bf16), V((QUARTER, D), bf16),
            V((CHUNKS, QUARTER, CHUNK), bf16), V((CHUNKS, BW, D), bf16), sem((3, 6)), sem((3, 6)), sem((3,)), sem((6,)),
            sem((8,)),
        ],
        compiler_params=pltpu.CompilerParams(vmem_limit_bytes=60 << 20, collective_id=cid, has_side_effects=True),
    )(lens, x, dy, vec, heads, output, expand, reduce)


def attention_kernel(
    x_ref, n1_ref, n1T_ref, dy_ref, wq_ref, wk_ref, wv_ref, wo_ref, vec_ref, cos_ref, sin_ref, mask_ref, eown, rown,
    hh_ref, og_ref, base_ref, grad_ref, vgrad_ref, efull, rfull,
    qT, kT, vT, oT, cT, gq, gk, gv, dn1T, ss, rs, ls,
):
    g = pl.program_id(0)
    ge = Gather(eown, efull, ss.at[0], rs.at[0], ls.at[0])
    gr = Gather(rown, rfull, ss.at[1], rs.at[1], ls.at[1])

    @pl.when(g == 0)
    def _():
        greet(gather_peers())
        ge.start()
        vgrad_ref[...] = jnp.zeros_like(vgrad_ref)

    @pl.when(g == 1)
    def _():
        ge.forward()

    @pl.when(g == 2)
    def _():
        ge.diag()

    heads = BLK // HEAD
    n1 = n1_ref[...]
    cos, sin = cos_ref[...], sin_ref[...]
    cols = pl.ds(pl.multiple_of(g * BLK, BLK), BLK)

    def column(row):
        return jnp.transpose(jnp.broadcast_to(vec_ref[row : row + 1, cols], (8, BLK)))[:, 0:1]

    def proj(w_ref, k):
        return dot(w_ref[...], n1, TT) + column(HEADS_BIAS + k)

    def rot(x):
        parts = []
        for h in range(heads):
            a, b = x[64 * h : 64 * h + 8], x[64 * h + 8 : 64 * h + 16]
            parts += [a * cos - b * sin, b * cos + a * sin, x[64 * h + 16 : 64 * h + 64]]
        return jnp.concatenate(parts, 0)

    def unrot(x):
        a, b = x[0:8], x[8:16]
        return jnp.concatenate([a * cos + b * sin, b * cos - a * sin, x[16:64]], 0)

    qT[...] = rot(proj(wq_ref, 0)).astype(bf16)
    kT[...] = rot(proj(wk_ref, 1)).astype(bf16)
    vT[...] = proj(wv_ref, 2).astype(bf16)
    oT[...] = dot(wo_ref[...], dy_ref[...], NT).astype(bf16)
    key = lax.broadcasted_iota(jnp.int32, (BLK, BLK), 0)
    query = lax.broadcasted_iota(jnp.int32, (BLK, BLK), 1)
    causal = key <= query
    scale = score_scale * LOG2E
    nb = TOK // BLK
    @pl.loop(0, heads // 2)
    def _(pair):
        @pl.when((g == 0) & (pair == 1))
        def _():
            gr.start()

        @pl.when((g == 1) & (pair == 1))
        def _():
            gr.forward()

        @pl.when((g == 2) & (pair == 1))
        def _():
            gr.diag()

        for h in (2 * pair, 2 * pair + 1):
            r = pl.ds(pl.multiple_of(HEAD * h, HEAD), HEAD)
            QT, KT, VT, OT = qT[r, :], kT[r, :], vT[r, :], oT[r, :]
            K, V = KT.T, VT.T
            dKT, dVT, dQT, context = [[] for _ in range(nb)], [[] for _ in range(nb)], [], []
            for j in range(nb):
                blocks = list(range(0 if j < nb - 1 else j, j + 1))
                span = [slice(BLK * b, BLK * b + BLK) for b in blocks]
                q, o = QT[:, BLK * j : BLK * j + BLK], OT[:, BLK * j : BLK * j + BLK]
                S = [dot(K[c], q) * scale for c in span]
                S[-1] = jnp.where(causal, S[-1], masked_score) if j < nb - 1 else S[-1] + mask_ref[...]
                top = functools.reduce(jnp.maximum, [jnp.max(s, 0, keepdims=True) for s in S])
                E = [jnp.exp2(s - top) for s in S]
                inv = 1.0 / total([jnp.sum(e, 0, keepdims=True) for e in E])
                soft = [e * inv for e in E]
                low = [p.astype(bf16) for p in soft]
                context.append(total([dot(VT[:, c], p) for c, p in zip(span, low)]).astype(bf16))
                back = [dot(V[c], o) for c in span]
                row = total([jnp.sum(d * p, 0, keepdims=True) for d, p in zip(back, soft)])
                dS = [(p * (d - row)).astype(bf16) for d, p in zip(back, soft)]
                dQT.append(total([dot(KT[:, c], s) for c, s in zip(span, dS)]) * score_scale)
                for b, p, s in zip(blocks, low, dS):
                    dKT[b].append(dot(q, s, NT))
                    dVT[b].append(dot(o, p, NT))
            cT[r, :] = jnp.concatenate(context, 1)
            gq[r, :] = unrot(jnp.concatenate(dQT, 1)).astype(bf16)
            gk[r, :] = unrot(jnp.concatenate([total(d) for d in dKT], 1) * score_scale).astype(bf16)
            gv[r, :] = jnp.concatenate([total(d) for d in dVT], 1).astype(bf16)
    n1T = n1T_ref[...]
    ones = jnp.ones((8, TOK), bf16)
    parts = []
    for k, (grads, w_ref) in enumerate(((gq, wq_ref), (gk, wk_ref), (gv, wv_ref))):
        G = grads[...]
        hh_ref[k] = dot(n1T, G, NT)
        vgrad_ref[HEADS_BIAS + k : HEADS_BIAS + k + 1, cols] = dot(ones, G, NT)[0:1]
        parts.append(dot(w_ref[...], G))
    ctx = cT[...]
    og_ref[...] = dot(ctx, dy_ref[...])
    out = dot(ctx, wo_ref[...], TN)

    @pl.when(g == 0)
    def _():
        bias = vec_ref[OUTPUT_BIAS : OUTPUT_BIAS + 1] + vec_ref[REDUCE_BIAS : REDUCE_BIAS + 1]
        base_ref[...] = out + (x_ref[...].astype(f32) + bias)
        dn1T[...] = total(parts)

    @pl.when(g > 0)
    def _():
        base_ref[...] += out
        dn1T[...] += total(parts)

    @pl.when(g == D // BLK - 1)
    def _():
        vgrad_ref[GAIN_ONE : SHIFT_ONE + 1] = jnp.zeros((2, D), f32)
        vgrad_ref[OUTPUT_BIAS : OUTPUT_BIAS + 1] = jnp.zeros((1, D), f32)

        @pl.loop(0, TOK // TILE)
        def _(i):
            rows = pl.ds(pl.multiple_of(TILE * i, TILE), TILE)
            dy = dy_ref[rows].astype(f32)
            back, gain, shift = norm_back(
                x_ref[rows].astype(f32), vec_ref[GAIN_ONE : GAIN_ONE + 1], dn1T[:, rows].T
            )
            grad_ref[rows] = dy + back
            vgrad_ref[GAIN_ONE : GAIN_ONE + 1] += gain
            vgrad_ref[SHIFT_ONE : SHIFT_ONE + 1] += shift
            vgrad_ref[OUTPUT_BIAS : OUTPUT_BIAS + 1] += jnp.sum(dy, 0, keepdims=True)

        vgrad_ref[REDUCE_BIAS : REDUCE_BIAS + 1] = vgrad_ref[OUTPUT_BIAS : OUTPUT_BIAS + 1]
        ge.finish()
        gr.finish()


def attention(x, n1, n1T, dy, W, Wo, vec, cos, sin, mask, eown, rown, cid):
    G = D // BLK
    S, V = jax.ShapeDtypeStruct, pltpu.VMEM
    block = lambda k: pl.BlockSpec((D, BLK), lambda g: (0, k * G + g))
    rows = pl.BlockSpec((BLK, D), lambda g: (g, 0))
    sem = pltpu.SemaphoreType.DMA
    return pl.pallas_call(
        attention_kernel,
        grid=(G,),
        in_specs=[
            whole((TOK, D)), whole((TOK, D)), whole((D, TOK)), whole((TOK, D)), block(0), block(1), block(2), rows,
            whole((16, D)), whole((8, TOK)), whole((8, TOK)), whole((BLK, BLK)),
            whole(eown.shape), whole(rown.shape),
        ],
        out_specs=[
            pl.BlockSpec((3, D, BLK), lambda g: (0, 0, g)), rows, whole((TOK, D)), whole((TOK, D)), whole((16, D)),
            any_spec(), any_spec(),
        ],
        out_shape=[
            S((3, D, D), f32), S((D, D), f32), S((TOK, D), f32), S((TOK, D), f32), S((16, D), f32),
            S((CHUNKS, D, CHUNK), bf16), S((CHUNKS, CHUNK, D), bf16),
        ],
        scratch_shapes=[V((BLK, TOK), bf16)] * 8 + [V((D, TOK), f32), sem((2, 6)), sem((2, 6)), sem((2,))],
        compiler_params=pltpu.CompilerParams(vmem_limit_bytes=60 << 20, collective_id=cid, has_side_effects=True),
    )(x, n1, n1T, dy, W, W, W, Wo, vec, cos, sin, mask, eown, rown)


def feed_kernel(
    digits, n2_ref, n2T_ref, dy_ref, x_ref, vec_ref, bias_ref, we_ref, wr_ref, base_hbm, grad_hbm, hh, og, vg_ref,
    out_ref, token_ref, sum_h, sum_e, sum_r, sum_v, sum_o,
    gh, gx, gr, gv, go, os, acc, dn2, act_ref, hid_ref, sums, bge, ex, rx, vx, hx, ox, ls, bs, *scratch,
):
    t = pl.program_id(0)
    c = place()[2]
    parts = [scratch[STREAM * i : STREAM * i + STREAM] for i in range(5)]

    def stream(i, mine, other, gout):
        return Reduce(digits, mine, other, *parts[i][:9], gout, parts[i][9], parts[i][10])

    def heads_part(k, core):
        return hh.at[k // 2, :, core, pl.ds(pl.multiple_of(HPART * (k % 2), 16), HPART)]

    H = stream(0, lambda k: hx.at[k % 2], lambda k: heads_part(k, 1 - c), gh)
    O = stream(4, lambda k: ox, lambda k: og.at[0, :, 1 - c], go)
    E = stream(1, lambda k: ex.at[:, c], lambda k: ex.at[:, 1 - c], gx)
    R = stream(2, lambda k: rx.at[:, c], lambda k: rx.at[:, 1 - c], gr)
    Z = stream(3, lambda k: vx.at[:, c], lambda k: vx.at[:, 1 - c], gv)

    ways = ((gh, sum_h), (gx, sum_e), (gr, sum_r), (gv, sum_v), (go, sum_o))

    def hand(i, k):
        return pltpu.make_async_copy(ways[i][0].at[k], ways[i][1].at[k], os.at[i, k])

    def load_part(i, k):
        if i == 4:
            return pltpu.make_async_copy(og.at[0, :, c], ox, ls.at[HPARTS])
        return pltpu.make_async_copy(heads_part(k, c), hx.at[k % 2], ls.at[k])

    def load_base():
        return pltpu.make_async_copy(base_hbm, acc, bs.at[0])

    def load_grad():
        return pltpu.make_async_copy(grad_hbm, acc, bs.at[1])

    @pl.when(t == 0)
    def _():
        greet(reduce_peers(digits))
        load_base().start()

    last = len(E.stage_list()) - 1
    streams = ((H, HPARTS, 0), (E, CHUNKS, 0), (R, CHUNKS, 0), (Z, 1, CHUNKS - 1), (O, 1, 0))

    def advance(i):
        s, n, first = streams[i]
        for j in range(last, 0, -1):

            @pl.when((t >= j + first) & (t < j + first + n))
            def _():
                k = t - j - first
                if j == 1 and i in (0, 4):
                    load_part(i, k).wait()
                s.stage_list()[j](k)
                if j == last:
                    hand(i, k).start()

    advance(0)
    advance(4)

    @pl.when(t < HPARTS)
    def _():
        load_part(0, t).start()
        H.s0(t)

    @pl.when(t == 0)
    def _():
        load_part(4, 0).start()
        O.s0(0)

    @pl.when(t < CHUNKS)
    def _():
        we, wr = we_ref[0], wr_ref[0]
        bias = bias_ref[pl.ds(t, 1)][0]

        @pl.when(t == 0)
        def _():
            load_base().wait()
            dn2[...] = jnp.zeros_like(dn2)

        bge[pl.ds(t, 1)] = jnp.zeros((1, 1, CHUNK), f32)

        @pl.loop(0, TOK // FTILE)
        def _(i):
            rows = pl.ds(pl.multiple_of(FTILE * i, FTILE), FTILE)
            h = dot(n2_ref[rows], we) + bias
            cdf = 0.5 * (1.0 + lax.erf(h * 0.7071067811865476))
            pdf = jnp.exp2(h * h * (-0.5 * LOG2E)) * 0.3989422804014327
            active = (h * cdf).astype(bf16)
            hidden = (dot(dy_ref[rows], wr, NT) * (cdf + h * pdf)).astype(bf16)
            act_ref[rows] = active
            hid_ref[rows] = hidden
            bge[pl.ds(t, 1)] += jnp.sum(hidden.astype(f32), 0, keepdims=True)[None]
            acc[rows] += dot(active, wr)
            dn2[rows] += dot(hidden, we, NT)

    advance(2)

    @pl.when(t < CHUNKS)
    def _():
        rx[...] = dot(act_ref[...], dy_ref[...], TN).reshape(rx.shape)
        R.s0(t)

    advance(1)

    @pl.when(t < CHUNKS)
    def _():
        ex[...] = dot(n2T_ref[...], hid_ref[...]).reshape(ex.shape)
        E.s0(t)

    advance(3)

    @pl.when(t == CHUNKS - 1)
    def _():
        out_ref[...] = acc[...].astype(bf16)
        load_grad().start()
        sums[...] = jnp.zeros_like(sums)
        load_grad().wait()

        @pl.loop(0, TOK // TILE)
        def _(i):
            rows = pl.ds(pl.multiple_of(TILE * i, TILE), TILE)
            back, gain, shift = norm_back(x_ref[rows].astype(f32), vec_ref[GAIN_TWO : GAIN_TWO + 1], dn2[rows])
            token_ref[rows] = (acc[rows] + back).astype(bf16)
            sums[0:1] += gain
            sums[1:2] += shift

        rows = {k: vg_ref[k : k + 1] for k in range(VEC_ROWS) if k not in (2, 3, 8, 9, 10, 11)}
        rows[GAIN_TWO], rows[SHIFT_TWO] = sums[0:1], sums[1:2]
        for s in range(4):
            rows[EXPAND_BIAS + s] = jnp.concatenate([bge[g, :, BW * s : BW * s + BW] for g in range(CHUNKS)], 1)
        vx[...] = jnp.zeros_like(vx)
        for i in range(VEC_ROWS * 4):
            s, row = i // VEC_ROWS, i % VEC_ROWS
            vx[s, row // 8, row % 8 : row % 8 + 1, 0:SEG] = rows[i // 4][:, SEG * (i % 4) : SEG * (i % 4) + SEG]
        Z.s0(0)

    @pl.when(t == pl.num_programs(0) - 1)
    def _():
        for i, n in enumerate((HPARTS, CHUNKS, CHUNKS, 1, 1)):
            for k in range(n):
                hand(i, k).wait()


def feed(n2, n2T, dy, x, vec, bias, We, Wr, base, grad, hh, og, vgrad, digits, cid):
    S, V, sem = jax.ShapeDtypeStruct, pltpu.VMEM, pltpu.SemaphoreType.DMA
    nd = len(digits)
    steps = CHUNKS + 4 + 3 * nd
    at = lambda t: jnp.minimum(t, CHUNKS - 1)
    vmem = pl.BlockSpec(memory_space=pltpu.VMEM)
    shapes = [((HPARTS, 2, HPART, D), f32), ((CHUNKS, 2, 96, CHUNK), bf16), ((CHUNKS, 2, BW // 2, D), bf16), ((1, 2, 8, BLK), f32), ((1, 2, 96, D), f32)]
    return pl.pallas_call(
        functools.partial(feed_kernel, digits),
        grid=(steps,),
        in_specs=[
            whole((TOK, D)), whole((D, TOK)), whole((TOK, D)), whole((TOK, D)), whole((16, D)), whole((CHUNKS, 1, CHUNK)),
            pl.BlockSpec((1, D, CHUNK), lambda t: (at(t), 0, 0)), pl.BlockSpec((1, CHUNK, D), lambda t: (at(t), 0, 0)),
            any_spec(), any_spec(), any_spec(), any_spec(), whole((16, D)),
        ],
        out_specs=[whole((TOK, D)), whole((TOK, D))] + [any_spec() for _ in shapes],
        out_shape=[S((TOK, D), bf16), S((TOK, D), bf16)] + [S(s, k) for s, k in shapes],
        scratch_shapes=[V(s, k) for s, k in shapes] + [
            sem((5, CHUNKS)), V((TOK, D), f32), V((TOK, D), f32), V((TOK, CHUNK), bf16), V((TOK, CHUNK), bf16), V((8, D), f32), V((CHUNKS, 1, CHUNK), f32), V((4, 2, 96, CHUNK), f32),
            V((4, 2, BW // 2, D), f32), V((4, 2, 8, BLK), f32), V((2, 4, HPART, D), f32), V((4, 96, D), f32), sem((HPARTS + 1,)), sem((2,)),
        ]
        + stream_scratch(HPARTS, HPART, D, nd, bf16) + stream_scratch(CHUNKS, 96, CHUNK, nd, bf16)
        + stream_scratch(CHUNKS, BW // 2, D, nd, bf16) + stream_scratch(1, 8, BLK, nd, f32) + stream_scratch(1, 96, D, nd, bf16),
        compiler_params=pltpu.CompilerParams(vmem_limit_bytes=63 << 20, collective_id=cid, has_side_effects=True),
    )(n2, n2T, dy, x, vec, bias, We, Wr, base, grad, hh, og, vgrad)


def adam_step(master, moment, square, gradient, rate, decay):
    momentum = first_decay * moment + (1.0 - first_decay) * gradient
    squares = second_decay * square + (1.0 - second_decay) * gradient * gradient
    first_fix = momentum * (rate / (1.0 - first_decay**STEP))
    second_fix = squares * (1.0 / (1.0 - second_decay**STEP))
    updated = master - first_fix / (jnp.sqrt(second_fix) + adam_epsilon)
    if decay:
        updated = updated - (rate * decay) * master
    return (momentum, squares, updated)


def leave_kernel(lens, block, token, sh, so, se, sr, *refs):
    ins, outs = refs[:12], refs[12:]
    g = pl.program_id(0)

    @pl.when(g < TOK // ATILE)
    def _():
        first, second = lens[0, 0], lens[0, 1]
        start = jnp.where(first == LONG, 0, jnp.where(second == LONG, first, first + second))
        want = lax.broadcasted_iota(jnp.int32, (ATILE, TOK), 0) + (g * ATILE - start)
        want = jnp.where(want < 0, want + TOK, want)
        turn = (want == lax.broadcasted_iota(jnp.int32, (ATILE, TOK), 1)).astype(bf16)
        outs[0][...] = dot(turn, block[...]).astype(bf16)
        outs[1][...] = dot(turn, token[...]).astype(bf16)

    def step(i, gradient):
        new = adam_step(*(ins[3 * i + j][...] for j in range(3)), gradient, matrix_rate, matrix_decay)
        for j in range(3):
            outs[2 + 3 * i + j][...] = new[j]

    step(0, jnp.concatenate([sh[q, 0, 0] for q in range(3)], 1))
    step(1, so[0, 0])
    blocks = [se[k, 0, :, 128 * s : 128 * s + 128] for s in range(4) for k in range(CHUNKS)]
    step(2, jnp.concatenate(blocks, 1).astype(f32))
    step(3, sr[...].astype(f32))


def leave(lens, block, token, sums, state):
    S = jax.ShapeDtypeStruct
    sh, se, sr, so = sums
    steps, per = QUARTER // AROWS, HPART // AROWS
    still = lambda *shape: pl.BlockSpec(shape, lambda g: (g, 0))
    specs = [still(AROWS, 3 * D), still(AROWS, D), still(AROWS, FF), still(D // steps, D)]
    turned = pl.BlockSpec((ATILE, D), lambda g: (jnp.minimum(g, TOK // ATILE - 1), 0))
    sums_specs = [
        pl.BlockSpec((3, 1, 1, AROWS, D), lambda g: (0, g // per % 2, g // per // 2, g % per, 0)),
        pl.BlockSpec((1, 1, AROWS, D), lambda g: (0, g // per // 2, g % (2 * per), 0)),
        pl.BlockSpec((CHUNKS, 1, AROWS, CHUNK), lambda g: (0, g // per // 2, g % (2 * per), 0)),
        still(D // steps, D),
    ]
    shapes = [S((QUARTER, 3 * D), f32), S((QUARTER, D), f32), S((QUARTER, FF), f32), S((D, D), f32)]
    return pl.pallas_call(
        leave_kernel,
        grid=(steps,),
        in_specs=[pl.BlockSpec(memory_space=pltpu.SMEM), whole((TOK, D)), whole((TOK, D))] + sums_specs
        + [s for s in specs for _ in range(3)],
        out_specs=[turned] * 2 + [s for s in specs for _ in range(3)],
        out_shape=[S((TOK, D), bf16)] * 2 + [s for s in shapes for _ in range(3)],
        compiler_params=pltpu.CompilerParams(vmem_limit_bytes=60 << 20),
    )(lens, block, token, sh.reshape(3, 2, 2, HPART, D), so, se, sr.reshape(D, D), *state)


def per_device(
    tokens,
    lengths,
    cotangent,
    heads_master,
    output_master,
    expand_master,
    reduce_master,
    vector_master,
    heads_moment,
    output_moment,
    expand_moment,
    reduce_moment,
    vector_moment,
    heads_square,
    output_square,
    expand_square,
    reduce_square,
    vector_square,
):
    digits = ring_of(lax.axis_size("dp"))
    (x, dy, n1, n1T, n2, n2T, vectors, bias, cos, sin, mask, heads_weight, output_weight, expand_own, reduce_own) = enter(
        lengths, tokens, cotangent, vector_master.reshape(VEC_ROWS, SEG), heads_master, output_master, expand_master,
        reduce_master, 1)
    heads_grad, output_grad, base, grad, vector_grad, expand_weight, reduce_weight = attention(
        x, n1, n1T, dy, heads_weight, output_weight, vectors, cos, sin, mask, expand_own, reduce_own, 2)
    block, token, *sums = feed(
        n2, n2T, dy, x, vectors, bias, expand_weight, reduce_weight, base, grad, heads_grad.reshape(3, 4, 2, 96, D),
        output_grad.reshape(1, 4, 2, 96, D), vector_grad, digits, 3)
    state = [
        heads_master, heads_moment, heads_square, output_master, output_moment, output_square,
        expand_master, expand_moment, expand_square, reduce_master, reduce_moment, reduce_square,
    ]
    sum_h, sum_e, sum_r, sum_v, sum_o = sums
    vector_new = adam_step(
        vector_master, vector_moment, vector_square, sum_v.reshape(16, BLK)[:VEC_ROWS, :SEG].reshape(-1), vector_rate, 0.0)
    return (*leave(lengths, block, token, (sum_h, sum_e, sum_r, sum_o), state), *vector_new)


def solution(mesh):
    placed = (
        P(("shard", "dp"), None),
        P(("shard", "dp"), None),
        P(("shard", "dp"), None),
        P("shard", None),
        P("shard", None),
        P("shard", None),
        P("shard", None),
        P("shard"),
        P("shard", None),
        P("shard", None),
        P("shard", None),
        P("shard", None),
        P("shard"),
        P("shard", None),
        P("shard", None),
        P("shard", None),
        P("shard", None),
        P("shard"),
    )
    return jax.shard_map(
        per_device,
        mesh=mesh,
        in_specs=placed,
        out_specs=(
            P(("shard", "dp"), None),
            P(("shard", "dp"), None),
            P("shard", None),
            P("shard", None),
            P("shard", None),
            P("shard", None),
            P("shard", None),
            P("shard", None),
            P("shard", None),
            P("shard", None),
            P("shard", None),
            P("shard", None),
            P("shard", None),
            P("shard", None),
            P("shard"),
            P("shard"),
            P("shard"),
        ),
        check_vma=False,
    )
```

```python
import functools

import jax
import jax.numpy as jnp
from jax import lax
from jax.experimental import pallas as pl
from jax.experimental.pallas import tpu as pltpu
from jax.sharding import PartitionSpec as P

D = 768
HEADS = 12
HEAD = 64
ROT = 16
FF = 3072
STEP = 10
TOK = 1024
LONG = 768
BLK = 256
CHUNK = 512
BW = CHUNK // 4
HROWS = 3 * 96
CHUNKS = FF // CHUNK
QUARTER = D // 4
SEG = 192
TILE = 128
ATILE = 512
AROWS = 96
FTILE = 512

first_decay = 0.9
second_decay = 0.95
adam_epsilon = 1e-08
matrix_decay = 0.1
matrix_rate = 0.04
vector_rate = 0.2
norm_epsilon = 1e-05
score_scale = 0.125
rotary_base = 10000.0
masked_score = -1e30
LOG2E = 1.4426950408889634

f32 = jnp.float32
bf16 = jnp.bfloat16
MESH = pl.DeviceIdType.MESH
NN = (((1,), (0,)), ((), ()))
NT = (((1,), (1,)), ((), ()))
TN = (((0,), (0,)), ((), ()))
TT = (((0,), (1,)), ((), ()))

GAIN_ONE, SHIFT_ONE, GAIN_TWO, SHIFT_TWO, HEADS_BIAS, OUTPUT_BIAS, EXPAND_BIAS, REDUCE_BIAS = 0, 1, 2, 3, 4, 7, 8, 12
VEC_ROWS = 13


def dot(a, b, dims=NN):
    return lax.dot_general(a, b, dims, preferred_element_type=f32)


def total(parts):
    return functools.reduce(jnp.add, parts)


def any_spec():
    return pl.BlockSpec(memory_space=pl.ANY)


def whole(shape):
    return pl.BlockSpec(shape, lambda g: (0,) * len(shape), pipeline_mode=pl.Buffered(1))


def norm_rows(values):
    centred = values - jnp.mean(values, -1, keepdims=True)
    inverse = lax.rsqrt(jnp.mean(centred * centred, -1, keepdims=True) + norm_epsilon)
    return centred * inverse, inverse


def norm_back(values, gain, grad):
    normed, inverse = norm_rows(values)
    scaled = grad * gain
    back = inverse * (
        scaled - jnp.mean(scaled, -1, keepdims=True) - normed * jnp.mean(scaled * normed, -1, keepdims=True)
    )
    return back, jnp.sum(grad * normed, 0, keepdims=True), jnp.sum(grad, 0, keepdims=True)


def place():
    s=lax.axis_index("shard"); d=lax.axis_index("dp")
    c=d%2
    s1=s+1-2*(s%2); s2=s+2-4*(s//2)
    a=(1-c)*s1+c*s2
    b=(1-c)*s2+c*s1
    return s,d,c,a,b

def rcopy(src,dst,ssem,rsem,sh,dp):
    return pltpu.make_async_remote_copy(src_ref=src,dst_ref=dst,send_sem=ssem,recv_sem=rsem,device_id=(sh,dp),device_id_type=MESH)

def greet(peers):
    bar=pltpu.get_barrier_semaphore()
    for sh,dp in peers:
        pl.semaphore_signal(bar,inc=1,device_id=(sh,dp),device_id_type=MESH)
    pl.semaphore_wait(bar,len(peers))

class Gather:
    def __init__(self,own,full,ssem,rsem,lsem,split=True,lo=0,n=None):
        self.own,self.full,self.ss,self.rs,self.ls=own,full,ssem,rsem,lsem
        self.s,self.d,self.c,self.a,self.b=place()
        self.sib=self.d+1-2*self.c
        self.R=own.shape[-2]; self.split=split
        self.h=self.R//2 if split else self.R
        self.lo=lo; self.n=n or self.h
    def sl(self,ref,row,n):
        row=pl.multiple_of(row,16)
        if len(ref.shape)==2: return ref.at[pl.ds(row,n)]
        return ref.at[:,pl.ds(row,n)]
    def region(self,sh,core):
        return self.sl(self.full,sh*self.R+(core*self.h if self.split else 0)+self.lo,self.n)
    def mine(self):
        return self.sl(self.own,(self.c*self.h if self.split else 0)+self.lo,self.n)
    def cp(self,k,src,reg,sh,dp): return rcopy(src,reg,self.ss.at[k],self.rs.at[k],sh,dp)
    def local(self):
        return pltpu.make_async_copy(self.own,self.sl(self.full,self.s*self.R,self.R),self.ls)
    def start(self):
        r=self.region(self.s,self.c)
        self.cp(0,self.mine(),r,self.a,self.d).start()
        self.cp(1,self.mine(),r,self.b,self.d).start()
        if self.lo==0: self.local().start()
    def _wait_recv(self,k,sh,core):
        r=self.region(sh,core)
        self.cp(k,r,r,self.s,self.sib).wait_recv()
    def _wait_send(self,k,sh,core):
        r=self.region(sh,core)
        self.cp(k,r,r,self.s,self.sib).wait_send()
    def forward(self):
        ra=self.region(self.a,self.c)
        self._wait_recv(0,self.a,self.c)
        self.cp(2,ra,ra,self.b,self.d).start()
        if self.split: self.cp(3,ra,ra,self.s,self.sib).start()
        self._wait_recv(1,self.b,self.c)
        rb=self.region(self.b,self.c)
        if self.split: self.cp(4,rb,rb,self.s,self.sib).start()
    def diag(self):
        x=3-self.s
        self._wait_recv(2,x,self.c)
        rx=self.region(x,self.c)
        if self.split: self.cp(5,rx,rx,self.s,self.sib).start()
    def finish(self):
        if self.lo==0: self.local().wait()
        x=3-self.s
        if self.split:
            o=1-self.c
            self._wait_recv(3,self.b,o)
            self._wait_recv(4,self.a,o)
            self._wait_recv(5,x,o)
        self.cp(0,self.mine(),self.region(self.s,self.c),self.a,self.d).wait_send()
        self.cp(1,self.mine(),self.region(self.s,self.c),self.b,self.d).wait_send()
        for k,sh in ((2,self.a),)+(((3,self.a),(4,self.b),(5,x)) if self.split else ()):
            self._wait_send(k,sh,self.c)

def gather_peers():
    s,d,c,a,b=place()
    return [(a,d),(b,d),(s,d+1-2*c)]

def ring_of(dp_size):
    digits=[]; n=dp_size//2; stride=1
    while n>1:
        assert n%4==0
        digits.append(stride); stride*=4; n//=4
    return digits

class Reduce:
    def __init__(self,digits,mine,other,Y,SA,RA,T,SB,RB,SZ,RZ,RM,gout,ss,rs):
        self.digits=digits; self.mine=mine; self.other=other
        self.Y,self.SA,self.RA,self.T,self.SB,self.RB,self.SZ,self.RZ,self.RM,self.gout,self.ss,self.rs=Y,SA,RA,T,SB,RB,SZ,RZ,RM,gout,ss,rs
        self.s,self.d,self.c,self.a,self.b=place()
        self.sib=self.d+1-2*self.c
        self.x=3-self.s
    def cp(self,j,k,src,dst,sh,dp): return rcopy(src,dst,self.ss.at[j,k],self.rs.at[j,k],sh,dp)
    def role(self,i):
        st=self.digits[i]; p=((self.d//2)//st)%4
        end=(p==0)|(p==3)
        mate=self.d+2*st*jnp.where(p==0,1,jnp.where(p==3,-1,jnp.where(p==1,1,-1)))
        tip=self.d+2*st*jnp.where(p==1,-1,1)
        return end,mate,tip
    def stages(self): return 4+3*len(self.digits)+1
    def c0(self,k): return self.cp(0,k,self.other(k),self.Y.at[k%2],self.s,self.sib)
    def cA(self,k): return self.cp(1,k,self.SA.at[k%2],self.RA.at[k%2],self.a,self.d)
    def cB(self,k): return self.cp(2,k,self.SB.at[k%2],self.RB.at[k%2],self.b,self.d)
    def nt(self,k): return k%self.T.shape[0]
    def s0(self,k):
        self.c0(k).start()
    def s1(self,k):
        self.c0(k).wait()
        X=self.mine(k)
        def U(p): return X[p]+self.Y[k%2,p]
        self.SA[k%2,0]=U(self.a).astype(self.SA.dtype)
        self.SA[k%2,1]=U(self.x).astype(self.SA.dtype)
        self.cA(k).start()
        t=self.nt(k)
        self.T[t,0]=U(self.s)
        self.T[t,1]=U(self.b)
    def s2(self,k):
        self.cA(k).wait()
        t=self.nt(k)
        self.SB[k%2]=(self.T[t,1]+self.RA[k%2,1].astype(f32)).astype(self.SB.dtype)
        self.cB(k).start()
        self.T[t,0]=self.T[t,0]+self.RA[k%2,0].astype(f32)
    def plane(self,k):
        self.cB(k).wait()
        t=self.nt(k)
        self.T[t,0]=self.T[t,0]+self.RB[k%2].astype(f32)
    def s3(self,k):
        self.plane(k)
        self.za(0,k)
    def g(self,k): return self.gout.at[k,self.c]
    def zcp(self,i,j,k,src,dst,dp): return self.cp(3+4*i+j,k,src,dst,self.s,dp)
    def za(self,i,k):
        t=self.nt(k); end,mate,tip=self.role(i)
        @pl.when(end)
        def _():
            self.SZ[i,k%2]=self.T[t,0].astype(self.SZ.dtype)
            self.zcp(i,0,k,self.SZ.at[i,k%2],self.RZ.at[i,k%3],mate).start()
    def zb(self,i,k):
        t=self.nt(k); end,mate,tip=self.role(i)
        @pl.when(jnp.logical_not(end))
        def _():
            self.zcp(i,0,k,self.SZ.at[i,k%2],self.RZ.at[i,k%3],tip).wait_recv()
            self.SZ[i,k%2]=(self.T[t,0]+self.RZ[i,k%3].astype(f32)).astype(self.SZ.dtype)
            self.zcp(i,1,k,self.SZ.at[i,k%2],self.RM.at[i,k%2],mate).start()
        @pl.when(end)
        def _():
            self.zcp(i,0,k,self.SZ.at[i,k%2],self.RZ.at[i,k%3],mate).wait_send()
    def to_sib(self,k):
        return self.cp(3+4*len(self.digits),k,self.g(k),self.g(k),self.s,self.sib)
    def zc(self,i,k):
        end,mate,tip=self.role(i); last=i==len(self.digits)-1
        @pl.when(jnp.logical_not(end))
        def _():
            self.zcp(i,1,k,self.SZ.at[i,k%2],self.RM.at[i,k%2],mate).wait()
            self.gout[k,self.c]=(self.SZ[i,k%2].astype(f32)+self.RM[i,k%2].astype(f32)).astype(self.gout.dtype)
            self.zcp(i,2,k,self.g(k),self.g(k),tip).start()
            if last: self.to_sib(k).start()
    def zd(self,i,k):
        end,mate,tip=self.role(i); last=i==len(self.digits)-1
        @pl.when(jnp.logical_not(end))
        def _():
            self.zcp(i,2,k,self.g(k),self.g(k),tip).wait_send()
        @pl.when(end)
        def _():
            self.zcp(i,2,k,self.g(k),self.g(k),mate).wait_recv()
            if last: self.to_sib(k).start()
        if not last:
            self.T[self.nt(k),0]=self.gout[k,self.c].astype(f32)
            self.za(i+1,k)
    def fin(self,k):
        self.to_sib(k).wait_send()
        g=self.gout.at[k,1-self.c]
        self.cp(3+4*len(self.digits),k,g,g,self.s,self.sib).wait_recv()
    def stage_list(self):
        return [self.s0,self.s1,self.s2,self.s3]+self.chain()
    def chain(self):
        out=[]
        for i in range(len(self.digits)):
            out+=[functools.partial(self.zb,i),functools.partial(self.zc,i),functools.partial(self.zd,i)]
        return out+[self.fin]

def reduce_peers(digits):
    s,d,c,a,b=place()
    peers=[(a,d),(b,d),(s,d+1-2*c)]
    for st in digits:
        p=((d//2)//st)%4
        up=d+2*st*jnp.where(p==3,-3,1); down=d+2*st*jnp.where(p==0,3,-1)
        peers+=[(s,up),(s,down)]
    return peers

def stream_scratch(n, r, w, nd, kind):
    V, S = pltpu.VMEM, pltpu.SemaphoreType.DMA
    ring = min(n, 4 + 3 * (nd - 1))
    return [
        V((2, 4, r, w), f32), V((2, 2, r, w), kind), V((2, 2, r, w), kind), V((ring, 2, r, w), f32),
        V((2, r, w), kind), V((2, r, w), kind), V((nd, 2, r, w), kind), V((nd, 3, r, w), kind), V((nd, 2, r, w), kind),
        S((4 + 4 * nd, n)), S((4 + 4 * nd, n)),
    ]


STREAM = 11


def enter_kernel(
    lens, x_hbm, dy_hbm, vec_own, heads_hbm, output_hbm, expand_hbm, reduce_hbm,
    x_out, dy_out, n1_out, n1T_out, n2_out, n2T_out, vec_ref, bias_ref, cos_ref, sin_ref, mask_ref, heads_full, output_full, e_out, r_out,
    vec_full, vec_low, xs, ds, normed, n1, n1T, n2, n2T, heads_in, output_in, expand_in, reduce_in, heads_own, output_own,
    eown, rown, ss, rs, ls, ins, outs,
):
    loads = [
        pltpu.make_async_copy(src, dst, ins.at[i])
        for i, (src, dst) in enumerate((
            (heads_hbm, heads_in), (output_hbm, output_in), (x_hbm, xs), (dy_hbm, ds), (expand_hbm, expand_in),
            (reduce_hbm, reduce_in),
        ))
    ]
    stores = [
        pltpu.make_async_copy(src, dst, outs.at[i])
        for i, (src, dst) in enumerate((
            (xs, x_out), (ds, dy_out), (n1, n1_out), (n1T, n1T_out), (n2, n2_out), (n2T, n2T_out), (eown, e_out),
            (rown, r_out),
        ))
    ]
    for copy in loads:
        copy.start()
    gv = Gather(vec_low, vec_full, ss.at[0], rs.at[0], ls.at[0], False)
    gh = Gather(heads_own, heads_full, ss.at[1], rs.at[1], ls.at[1])
    go = Gather(output_own, output_full, ss.at[2], rs.at[2], ls.at[2])
    vec_low[...] = jnp.zeros_like(vec_low)
    vec_low[0:VEC_ROWS, 0:SEG] = vec_own[...].astype(bf16)
    greet(gather_peers())
    gv.start()
    loads[0].wait()
    heads_own[...] = heads_in[...].astype(bf16)
    gh.start()
    loads[1].wait()
    output_own[...] = output_in[...].astype(bf16)
    go.start()
    first, second, third = lens[0, 0], lens[0, 1], lens[0, 2]
    start = jnp.where(first == LONG, 0, jnp.where(second == LONG, first, first + second))
    short = jnp.where(first == LONG, second, jnp.where(second == LONG, third, first))
    from_row = lax.broadcasted_iota(jnp.int32, (BLK, TOK), 1)

    def turn(ref):
        values, parts = ref[...], []
        for i in range(TOK // BLK):
            want = lax.broadcasted_iota(jnp.int32, (BLK, TOK), 0) + (i * BLK + start)
            want = jnp.where(want >= TOK, want - TOK, want)
            parts.append(dot((want == from_row).astype(bf16), values).astype(bf16))
        for i, part in enumerate(parts):
            ref[BLK * i : BLK * i + BLK] = part

    loads[2].wait()
    turn(xs)
    stores[0].start()
    for i in range(TOK // BLK):
        normed[BLK * i : BLK * i + BLK] = norm_rows(xs[BLK * i : BLK * i + BLK].astype(f32))[0]
    gv.forward()
    loads[3].wait()
    turn(ds)
    stores[1].start()
    gv.diag()
    row = lax.broadcasted_iota(jnp.int32, (8, TOK), 1)
    late = row - LONG
    position = jnp.where(late < 0, row, jnp.where(late >= short, late - short, late)).astype(f32)
    step = lax.broadcasted_iota(jnp.int32, (8, TOK), 0).astype(f32)
    angles = position * jnp.exp2(step * (-2.0 / ROT * 13.287712379549449))
    cos_ref[...] = jnp.cos(angles)
    sin_ref[...] = jnp.sin(angles)
    key = lax.broadcasted_iota(jnp.int32, (BLK, BLK), 0)
    query = lax.broadcasted_iota(jnp.int32, (BLK, BLK), 1)
    allowed = ((key >= short) == (query >= short)) & (key <= query)
    mask_ref[...] = jnp.where(allowed, 0.0, masked_score)
    gv.finish()
    vec_ref[...] = jnp.zeros_like(vec_ref)
    for i in range(4 * VEC_ROWS):
        s, r = i // VEC_ROWS, i % VEC_ROWS
        piece = vec_full[16 * s : 16 * s + 16].astype(f32)[r : r + 1, 0:SEG]
        vec_ref[i // 4 : i // 4 + 1, SEG * (i % 4) : SEG * (i % 4) + SEG] = piece
    for g in range(CHUNKS):
        for s in range(4):
            bias_ref[g, :, BW * s : BW * s + BW] = vec_ref[EXPAND_BIAS + s : EXPAND_BIAS + s + 1, BW * g : BW * g + BW]
    gh.forward()
    go.forward()
    for out, outT, gain, shift, k in ((n1, n1T, GAIN_ONE, SHIFT_ONE, 2), (n2, n2T, GAIN_TWO, SHIFT_TWO, 4)):
        for i in range(TOK // BLK):
            rows = slice(BLK * i, BLK * i + BLK)
            low = (normed[rows] * vec_ref[gain : gain + 1] + vec_ref[shift : shift + 1]).astype(bf16)
            out[rows] = low
            outT[:, rows] = low.T
        stores[k].start()
        stores[k + 1].start()
        if k == 2:
            gh.diag()
    loads[4].wait()
    for g in range(CHUNKS):
        for s in range(4):
            eown[g, :, BW * s : BW * s + BW] = expand_in[:, D * s + BW * g : D * s + BW * g + BW].astype(bf16)
    stores[6].start()
    loads[5].wait()
    rown[...] = reduce_in[...].astype(bf16).reshape(rown.shape)
    stores[7].start()
    go.diag()
    gh.finish()
    go.finish()
    for copy in stores:
        copy.wait()


def enter(lens, x, dy, vec, heads, output, expand, reduce, cid):
    S, V, sem = jax.ShapeDtypeStruct, pltpu.VMEM, pltpu.SemaphoreType.DMA
    vmem = pl.BlockSpec(memory_space=pltpu.VMEM)
    tall, wide = (TOK, D), (D, TOK)
    return pl.pallas_call(
        enter_kernel,
        in_specs=[pl.BlockSpec(memory_space=pltpu.SMEM), any_spec(), any_spec(), vmem] + [any_spec()] * 4,
        out_specs=[any_spec()] * 6 + [vmem] * 5 + [any_spec()] * 4,
        out_shape=[S(tall, bf16), S(tall, bf16), S(tall, bf16), S(wide, bf16), S(tall, bf16), S(wide, bf16)]
        + [S((16, D), f32), S((CHUNKS, 1, CHUNK), f32), S((8, TOK), f32), S((8, TOK), f32), S((BLK, BLK), f32)]
        + [S((D, 3 * D), bf16), S((D, D), bf16), S((CHUNKS, QUARTER, CHUNK), bf16), S((CHUNKS, BW, D), bf16)],
        scratch_shapes=[
            V((64, BLK), bf16), V((16, BLK), bf16), V(tall, bf16), V(tall, bf16), V(tall, f32), V(tall, bf16),
            V(wide, bf16), V(tall, bf16), V(wide, bf16), V((QUARTER, 3 * D), f32), V((QUARTER, D), f32),
            V((QUARTER, FF), f32), V((D, D), f32), V((QUARTER, 3 * D), bf16), V((QUARTER, D), bf16),
            V((CHUNKS, QUARTER, CHUNK), bf16), V((CHUNKS, BW, D), bf16), sem((3, 6)), sem((3, 6)), sem((3,)), sem((6,)),
            sem((8,)),
        ],
        compiler_params=pltpu.CompilerParams(vmem_limit_bytes=60 << 20, collective_id=cid, has_side_effects=True),
    )(lens, x, dy, vec, heads, output, expand, reduce)


def attention_kernel(
    x_hbm, n1_ref, n1T_hbm, dy_ref, wq_ref, wk_ref, wv_ref, wo_ref, vec_ref, cos_ref, sin_ref, mask_ref, e_hbm, r_hbm,
    hh_out, og_ref, base_out, grad_ref, vgrad_ref, efull, rfull, part_out,
    qT, kT, vT, oT, cT, gq, gk, gv, dn1T, ss, rs, ls, x2, Y, SA, RA, T, SB, RB, ps, pr, os,
    x_ref, n1T_ref, eown, rown, base_ref, ins,
):
    g = pl.program_id(0)
    ge = Gather(eown, efull, ss.at[0], rs.at[0], ls.at[0])
    gr = Gather(rown, rfull, ss.at[1], rs.at[1], ls.at[1])
    c = place()[2]
    part = Reduce((), lambda k: x2.at[:, c], lambda k: x2.at[:, 1 - c], Y, SA, RA, T, SB, RB, None, None, None, None, ps, pr)

    loads = [
        pltpu.make_async_copy(src, dst, ins.at[i])
        for i, (src, dst) in enumerate(((e_hbm, eown), (r_hbm, rown), (n1T_hbm, n1T_ref), (x_hbm, x_ref)))
    ]
    base_copy = pltpu.make_async_copy(base_ref, base_out, os.at[3])

    @pl.when(g == 0)
    def _():
        for copy in loads:
            copy.start()
        greet(gather_peers())
        loads[0].wait()
        ge.start()
        vgrad_ref[...] = jnp.zeros_like(vgrad_ref)

    @pl.when(g == 1)
    def _():
        ge.forward()

    @pl.when(g == 2)
    def _():
        ge.diag()

    heads = BLK // HEAD
    n1 = n1_ref[...]
    cos, sin = cos_ref[...], sin_ref[...]
    cols = pl.ds(pl.multiple_of(g * BLK, BLK), BLK)

    def column(row):
        return jnp.transpose(jnp.broadcast_to(vec_ref[row : row + 1, cols], (8, BLK)))[:, 0:1]

    def proj(w_ref, k):
        return dot(w_ref[...], n1, TT) + column(HEADS_BIAS + k)

    def rot(x):
        parts = []
        for h in range(heads):
            a, b = x[64 * h : 64 * h + 8], x[64 * h + 8 : 64 * h + 16]
            parts += [a * cos - b * sin, b * cos + a * sin, x[64 * h + 16 : 64 * h + 64]]
        return jnp.concatenate(parts, 0)

    def unrot(x):
        a, b = x[0:8], x[8:16]
        return jnp.concatenate([a * cos + b * sin, b * cos - a * sin, x[16:64]], 0)

    qT[...] = rot(proj(wq_ref, 0)).astype(bf16)
    kT[...] = rot(proj(wk_ref, 1)).astype(bf16)
    vT[...] = proj(wv_ref, 2).astype(bf16)
    oT[...] = dot(wo_ref[...], dy_ref[...], NT).astype(bf16)
    key = lax.broadcasted_iota(jnp.int32, (BLK, BLK), 0)
    query = lax.broadcasted_iota(jnp.int32, (BLK, BLK), 1)
    causal = key <= query
    scale = score_scale * LOG2E
    nb = TOK // BLK
    @pl.loop(0, heads // 2)
    def _(pair):
        @pl.when((g == 0) & (pair == 1))
        def _():
            loads[1].wait()
            gr.start()

        @pl.when((g == 1) & (pair == 0))
        def _():
            part.s1(0)

        @pl.when((g == 1) & (pair == 1))
        def _():
            gr.forward()

        @pl.when((g == 2) & (pair == 0))
        def _():
            part.plane(0)
            part.s1(1)

        @pl.when((g == 2) & (pair == 1))
        def _():
            gr.diag()

        for h in (2 * pair, 2 * pair + 1):
            r = pl.ds(pl.multiple_of(HEAD * h, HEAD), HEAD)
            QT, KT, VT, OT = qT[r, :], kT[r, :], vT[r, :], oT[r, :]
            K, V, Q, O = KT.T, VT.T, QT.T, OT.T
            dK, dV, dQT, context = [[] for _ in range(nb)], [[] for _ in range(nb)], [], []
            for j in range(nb):
                blocks = list(range(0 if j < nb - 1 else j, j + 1))
                span = [slice(BLK * b, BLK * b + BLK) for b in blocks]
                q, o = QT[:, BLK * j : BLK * j + BLK], OT[:, BLK * j : BLK * j + BLK]
                S = [dot(K[c], q) * scale for c in span]
                S[-1] = jnp.where(causal, S[-1], masked_score) if j < nb - 1 else S[-1] + mask_ref[...]
                top = functools.reduce(jnp.maximum, [jnp.max(s, 0, keepdims=True) for s in S])
                E = [jnp.exp2(s - top) for s in S]
                inv = 1.0 / total([jnp.sum(e, 0, keepdims=True) for e in E])
                soft = [e * inv for e in E]
                low = [p.astype(bf16) for p in soft]
                context.append(total([dot(VT[:, c], p) for c, p in zip(span, low)]).astype(bf16))
                back = [dot(V[c], o) for c in span]
                row = total([jnp.sum(d * p, 0, keepdims=True) for d, p in zip(back, soft)])
                dS = [(p * (d - row)).astype(bf16) for d, p in zip(back, soft)]
                dQT.append(total([dot(KT[:, c], s) for c, s in zip(span, dS)]) * score_scale)
                for b, p, s in zip(blocks, low, dS):
                    dK[b].append(dot(s, Q[BLK * j : BLK * j + BLK]))
                    dV[b].append(dot(p, O[BLK * j : BLK * j + BLK]))
            cT[r, :] = jnp.concatenate(context, 1)
            gq[r, :] = unrot(jnp.concatenate(dQT, 1)).astype(bf16)
            gk[r, :] = unrot(jnp.concatenate([total(d) for d in dK], 0).T * score_scale).astype(bf16)
            gv[r, :] = jnp.concatenate([total(d) for d in dV], 0).T.astype(bf16)
    @pl.when(g == 1)
    def _():
        part.s2(0)

    @pl.when(g == 2)
    def _():
        part.s2(1)

    @pl.when(g == 0)
    def _():
        loads[2].wait()
        loads[3].wait()

    n1T = n1T_ref[...]
    ones = jnp.ones((8, TOK), bf16)
    parts = []
    for k, (grads, w_ref) in enumerate(((gq, wq_ref), (gk, wk_ref), (gv, wv_ref))):
        G = grads[...]
        x2[:, :, 96 * k : 96 * k + 96] = dot(n1T, G, NT).reshape(4, 2, 96, BLK)
        vgrad_ref[HEADS_BIAS + k : HEADS_BIAS + k + 1, cols] = dot(ones, G, NT)[0:1]
        parts.append(dot(w_ref[...], G))

    @pl.when(g == 0)
    def _():
        part.s0(0)

    @pl.when(g == 1)
    def _():
        part.s0(1)

    heads_copy = pltpu.make_async_copy(x2, hh_out, os.at[2])
    part_copies = [pltpu.make_async_copy(T.at[k, 0], part_out.at[k], os.at[k]) for k in range(2)]

    @pl.when(g == 2)
    def _():
        heads_copy.start()

    ctx = cT[...]
    og_ref[...] = dot(ctx, dy_ref[...])
    out = dot(ctx, wo_ref[...], TN)

    @pl.when(g == 0)
    def _():
        bias = vec_ref[OUTPUT_BIAS : OUTPUT_BIAS + 1] + vec_ref[REDUCE_BIAS : REDUCE_BIAS + 1]
        base_ref[...] = out + (x_ref[...].astype(f32) + bias)
        dn1T[...] = total(parts)

    @pl.when(g > 0)
    def _():
        base_ref[...] += out
        dn1T[...] += total(parts)

    @pl.when(g == D // BLK - 1)
    def _():
        base_copy.start()
        vgrad_ref[GAIN_ONE : SHIFT_ONE + 1] = jnp.zeros((2, D), f32)
        vgrad_ref[OUTPUT_BIAS : OUTPUT_BIAS + 1] = jnp.zeros((1, D), f32)

        @pl.loop(0, TOK // TILE)
        def _(i):
            rows = pl.ds(pl.multiple_of(TILE * i, TILE), TILE)
            dy = dy_ref[rows].astype(f32)
            back, gain, shift = norm_back(
                x_ref[rows].astype(f32), vec_ref[GAIN_ONE : GAIN_ONE + 1], dn1T[:, rows].T
            )
            grad_ref[rows] = dy + back
            vgrad_ref[GAIN_ONE : GAIN_ONE + 1] += gain
            vgrad_ref[SHIFT_ONE : SHIFT_ONE + 1] += shift
            vgrad_ref[OUTPUT_BIAS : OUTPUT_BIAS + 1] += jnp.sum(dy, 0, keepdims=True)

        vgrad_ref[REDUCE_BIAS : REDUCE_BIAS + 1] = vgrad_ref[OUTPUT_BIAS : OUTPUT_BIAS + 1]
        part.plane(1)
        for copy in part_copies:
            copy.start()
        ge.finish()
        gr.finish()
        for copy in part_copies + [heads_copy, base_copy]:
            copy.wait()


def attention(x, n1, n1T, dy, W, Wo, vec, cos, sin, mask, eown, rown, cid):
    G = D // BLK
    S, V = jax.ShapeDtypeStruct, pltpu.VMEM
    block = lambda k: pl.BlockSpec((D, BLK), lambda g: (0, k * G + g))
    rows = pl.BlockSpec((BLK, D), lambda g: (g, 0))
    sem = pltpu.SemaphoreType.DMA
    return pl.pallas_call(
        attention_kernel,
        grid=(G,),
        in_specs=[
            any_spec(), whole((TOK, D)), any_spec(), whole((TOK, D)), block(0), block(1), block(2), rows,
            whole((16, D)), whole((8, TOK)), whole((8, TOK)), whole((BLK, BLK)),
            any_spec(), any_spec(),
        ],
        out_specs=[
            any_spec(), rows, any_spec(), whole((TOK, D)), whole((16, D)),
            any_spec(), any_spec(), any_spec(),
        ],
        out_shape=[
            S((4, 2, HROWS, BLK), f32), S((D, D), f32), S((TOK, D), f32), S((TOK, D), f32), S((16, D), f32),
            S((CHUNKS, D, CHUNK), bf16), S((CHUNKS, CHUNK, D), bf16), S((2, HROWS, BLK), f32),
        ],
        scratch_shapes=[V((BLK, TOK), bf16)] * 8 + [
            V((D, TOK), f32), sem((2, 6)), sem((2, 6)), sem((2,)), V((4, 2, HROWS, BLK), f32), V((2, 4, HROWS, BLK), f32),
            V((2, 2, HROWS, BLK), bf16), V((2, 2, HROWS, BLK), bf16), V((2, 2, HROWS, BLK), f32), V((2, HROWS, BLK), bf16),
            V((2, HROWS, BLK), bf16), sem((3, 2)), sem((3, 2)), sem((4,)),
            V((TOK, D), bf16), V((D, TOK), bf16), V(eown.shape, bf16), V(rown.shape, bf16), V((TOK, D), f32), sem((4,)),
        ],
        compiler_params=pltpu.CompilerParams(vmem_limit_bytes=60 << 20, collective_id=cid, has_side_effects=True),
    )(x, n1, n1T, dy, W, W, W, Wo, vec, cos, sin, mask, eown, rown)


def feed_kernel(
    digits, n2_ref, n2T_hbm, dy_ref, x_hbm, vec_ref, bias_ref, we_ref, wr_ref, base_hbm, grad_hbm, hh, og, pv, vg_ref,
    out_hbm, token_hbm, sum_h, sum_e, sum_r, sum_v, sum_o, sum_q,
    gh, gx, gr, gv, go, gq, os, acc, dn2, act_ref, hid_ref, sums, bge, ex, rx, vx, hx, ox, ls, bs, qT, qSZ, qRZ, qRM, qss, qrs, n2T_ref, x_ref, out_ref, token_ref, *scratch,
):
    t = pl.program_id(0)
    c = place()[2]
    parts = [scratch[STREAM * i : STREAM * i + STREAM] for i in range(5)]

    def stream(i, mine, other, gout):
        return Reduce(digits, mine, other, *parts[i][:9], gout, parts[i][9], parts[i][10])

    def heads_part(k, core):
        return hh.at[:, core, pl.ds(pl.multiple_of(96 * k, 16), 96)]

    H = stream(0, lambda k: hx.at[k % 2], lambda k: heads_part(k, 1 - c), gh)
    Q = Reduce(digits, None, None, None, None, None, qT, None, None, qSZ, qRZ, qRM, gq, qss, qrs)
    O = stream(4, lambda k: ox, lambda k: og.at[0, :, 1 - c], go)
    E = stream(1, lambda k: ex.at[:, c], lambda k: ex.at[:, 1 - c], gx)
    R = stream(2, lambda k: rx.at[:, c], lambda k: rx.at[:, 1 - c], gr)
    Z = stream(3, lambda k: vx.at[:, c], lambda k: vx.at[:, 1 - c], gv)

    ways = ((gh, sum_h), (gx, sum_e), (gr, sum_r), (gv, sum_v), (go, sum_o), (gq, sum_q))

    def hand(i, k):
        return pltpu.make_async_copy(ways[i][0].at[k], ways[i][1].at[k], os.at[i, k])

    def load_part(i, k):
        if i == 4:
            return pltpu.make_async_copy(og.at[0, :, c], ox, ls.at[3])
        if i == 5:
            return pltpu.make_async_copy(pv.at[k], qT.at[k, 0], ls.at[4 + k])
        return pltpu.make_async_copy(heads_part(k, c), hx.at[k % 2], ls.at[k])

    def load_base():
        return pltpu.make_async_copy(base_hbm, acc, bs.at[0])

    def load_grad():
        return pltpu.make_async_copy(grad_hbm, acc, bs.at[1])

    early = [
        pltpu.make_async_copy(n2T_hbm, n2T_ref, bs.at[2]), pltpu.make_async_copy(x_hbm, x_ref, bs.at[3]),
    ]
    late = [
        pltpu.make_async_copy(out_ref, out_hbm, bs.at[4]), pltpu.make_async_copy(token_ref, token_hbm, bs.at[5]),
    ]

    @pl.when(t == 0)
    def _():
        load_part(5, 0).start()
        load_part(5, 1).start()
        greet(reduce_peers(digits))
        load_base().start()
        for copy in early:
            copy.start()

    streams = [
        (s.stage_list(), n, first) for s, n, first in ((H, 3, 0), (E, CHUNKS, 0), (R, CHUNKS, 0), (Z, 1, CHUNKS - 1), (O, 1, 0))
    ] + [([None] + Q.chain(), 2, 0)]

    def advance(i):
        stages, n, first = streams[i]
        last = len(stages) - 1
        for j in range(last, 0, -1):

            @pl.when((t >= j + first) & (t < j + first + n))
            def _():
                k = t - j - first
                if j == 1 and i in (0, 4):
                    load_part(i, k).wait()
                stages[j](k)
                if j == last:
                    hand(i, k).start()

    advance(5)
    advance(0)
    advance(4)

    @pl.when(t < 2)
    def _():
        load_part(5, t).wait()
        Q.za(0, t)

    @pl.when(t < 3)
    def _():
        load_part(0, t).start()
        H.s0(t)

    @pl.when(t == 0)
    def _():
        load_part(4, 0).start()
        O.s0(0)

    @pl.when(t < CHUNKS)
    def _():
        we, wr = we_ref[0], wr_ref[0]
        bias = bias_ref[pl.ds(t, 1)][0]

        @pl.when(t == 0)
        def _():
            load_base().wait()
            for copy in early:
                copy.wait()
            dn2[...] = jnp.zeros_like(dn2)

        bge[pl.ds(t, 1)] = jnp.zeros((1, 1, CHUNK), f32)

        @pl.loop(0, TOK // FTILE)
        def _(i):
            rows = pl.ds(pl.multiple_of(FTILE * i, FTILE), FTILE)
            h = dot(n2_ref[rows], we) + bias
            cdf = 0.5 * (1.0 + lax.erf(h * 0.7071067811865476))
            pdf = jnp.exp2(h * h * (-0.5 * LOG2E)) * 0.3989422804014327
            active = (h * cdf).astype(bf16)
            hidden = (dot(dy_ref[rows], wr, NT) * (cdf + h * pdf)).astype(bf16)
            act_ref[rows] = active
            hid_ref[rows] = hidden
            bge[pl.ds(t, 1)] += jnp.sum(hidden.astype(f32), 0, keepdims=True)[None]
            acc[rows] += dot(active, wr)
            dn2[rows] += dot(hidden, we, NT)

    advance(2)

    @pl.when(t < CHUNKS)
    def _():
        rx[...] = dot(act_ref[...], dy_ref[...], TN).reshape(rx.shape)
        R.s0(t)

    advance(1)

    @pl.when(t < CHUNKS)
    def _():
        ex[...] = dot(n2T_ref[...], hid_ref[...]).reshape(ex.shape)
        E.s0(t)

    advance(3)

    @pl.when(t == CHUNKS - 1)
    def _():
        out_ref[...] = acc[...].astype(bf16)
        late[0].start()
        load_grad().start()
        sums[...] = jnp.zeros_like(sums)
        load_grad().wait()

        @pl.loop(0, TOK // TILE)
        def _(i):
            rows = pl.ds(pl.multiple_of(TILE * i, TILE), TILE)
            back, gain, shift = norm_back(x_ref[rows].astype(f32), vec_ref[GAIN_TWO : GAIN_TWO + 1], dn2[rows])
            token_ref[rows] = (acc[rows] + back).astype(bf16)
            sums[0:1] += gain
            sums[1:2] += shift

        rows = {k: vg_ref[k : k + 1] for k in range(VEC_ROWS) if k not in (2, 3, 8, 9, 10, 11)}
        rows[GAIN_TWO], rows[SHIFT_TWO] = sums[0:1], sums[1:2]
        for s in range(4):
            rows[EXPAND_BIAS + s] = jnp.concatenate([bge[g, :, BW * s : BW * s + BW] for g in range(CHUNKS)], 1)
        vx[...] = jnp.zeros_like(vx)
        for i in range(VEC_ROWS * 4):
            s, row = i // VEC_ROWS, i % VEC_ROWS
            vx[s, row // 8, row % 8 : row % 8 + 1, 0:SEG] = rows[i // 4][:, SEG * (i % 4) : SEG * (i % 4) + SEG]
        late[1].start()
        Z.s0(0)

    @pl.when(t == pl.num_programs(0) - 1)
    def _():
        for copy in late:
            copy.wait()
        for i, n in enumerate((3, CHUNKS, CHUNKS, 1, 1, 2)):
            for k in range(n):
                hand(i, k).wait()


def feed(n2, n2T, dy, x, vec, bias, We, Wr, base, grad, hh, og, part, vgrad, digits, cid):
    S, V, sem = jax.ShapeDtypeStruct, pltpu.VMEM, pltpu.SemaphoreType.DMA
    nd = len(digits)
    steps = CHUNKS + 4 + 3 * nd
    at = lambda t: jnp.minimum(t, CHUNKS - 1)
    vmem = pl.BlockSpec(memory_space=pltpu.VMEM)
    shapes = [((3, 2, 96, BLK), f32), ((CHUNKS, 2, 96, CHUNK), bf16), ((CHUNKS, 2, BW // 2, D), bf16), ((1, 2, 8, BLK), f32), ((1, 2, 96, D), f32), ((2, 2, HROWS, BLK), f32)]
    return pl.pallas_call(
        functools.partial(feed_kernel, digits),
        grid=(steps,),
        in_specs=[
            whole((TOK, D)), any_spec(), whole((TOK, D)), any_spec(), whole((16, D)), whole((CHUNKS, 1, CHUNK)),
            pl.BlockSpec((1, D, CHUNK), lambda t: (at(t), 0, 0)), pl.BlockSpec((1, CHUNK, D), lambda t: (at(t), 0, 0)),
            any_spec(), any_spec(), any_spec(), any_spec(), any_spec(), whole((16, D)),
        ],
        out_specs=[any_spec(), any_spec()] + [any_spec() for _ in shapes],
        out_shape=[S((TOK, D), bf16), S((TOK, D), bf16)] + [S(s, k) for s, k in shapes],
        scratch_shapes=[V(s, k) for s, k in shapes] + [
            sem((6, CHUNKS)), V((TOK, D), f32), V((TOK, D), f32), V((TOK, CHUNK), bf16), V((TOK, CHUNK), bf16), V((8, D), f32), V((CHUNKS, 1, CHUNK), f32), V((4, 2, 96, CHUNK), f32),
            V((4, 2, BW // 2, D), f32), V((4, 2, 8, BLK), f32), V((2, 4, 96, BLK), f32), V((4, 96, D), f32), sem((6,)), sem((6,)),
            V((2, 1, HROWS, BLK), f32), V((nd, 2, HROWS, BLK), bf16), V((nd, 3, HROWS, BLK), bf16),
            V((nd, 2, HROWS, BLK), bf16), sem((4 + 4 * nd, 2)), sem((4 + 4 * nd, 2)),
            V((D, TOK), bf16), V((TOK, D), bf16), V((TOK, D), bf16), V((TOK, D), bf16),
        ]
        + stream_scratch(3, 96, BLK, nd, bf16) + stream_scratch(CHUNKS, 96, CHUNK, nd, bf16)
        + stream_scratch(CHUNKS, BW // 2, D, nd, bf16) + stream_scratch(1, 8, BLK, nd, f32) + stream_scratch(1, 96, D, nd, bf16),
        compiler_params=pltpu.CompilerParams(vmem_limit_bytes=63 << 20, collective_id=cid, has_side_effects=True),
    )(n2, n2T, dy, x, vec, bias, We, Wr, base, grad, hh, og, part, vgrad)


def adam_step(master, moment, square, gradient, rate, decay):
    momentum = first_decay * moment + (1.0 - first_decay) * gradient
    squares = second_decay * square + (1.0 - second_decay) * gradient * gradient
    first_fix = momentum * (rate / (1.0 - first_decay**STEP))
    second_fix = squares * (1.0 / (1.0 - second_decay**STEP))
    updated = master - first_fix / (jnp.sqrt(second_fix) + adam_epsilon)
    if decay:
        updated = updated - (rate * decay) * master
    return (momentum, squares, updated)


def leave_kernel(lens, block, token, sq, sh, so, se, sr, *refs):
    ins, outs = refs[:12], refs[12:]
    g = pl.program_id(0)

    @pl.when(g < TOK // ATILE)
    def _():
        first, second = lens[0, 0], lens[0, 1]
        start = jnp.where(first == LONG, 0, jnp.where(second == LONG, first, first + second))
        want = lax.broadcasted_iota(jnp.int32, (ATILE, TOK), 0) + (g * ATILE - start)
        want = jnp.where(want < 0, want + TOK, want)
        turn = (want == lax.broadcasted_iota(jnp.int32, (ATILE, TOK), 1)).astype(bf16)
        outs[0][...] = dot(turn, block[...]).astype(bf16)
        outs[1][...] = dot(turn, token[...]).astype(bf16)

    def step(i, gradient):
        new = adam_step(*(ins[3 * i + j][...] for j in range(3)), gradient, matrix_rate, matrix_decay)
        for j in range(3):
            outs[2 + 3 * i + j][...] = new[j]

    step(0, jnp.concatenate([p for k in range(3) for p in (sq[0, 0, k, 0], sq[1, 0, k, 0], sh[k, 0, 0])], 1))
    step(1, so[0, 0])
    blocks = [se[k, 0, :, 128 * s : 128 * s + 128] for s in range(4) for k in range(CHUNKS)]
    step(2, jnp.concatenate(blocks, 1).astype(f32))
    step(3, sr[...].astype(f32))


def leave(lens, block, token, sums, state):
    S = jax.ShapeDtypeStruct
    sh, se, sr, so, sq = sums
    steps, per = QUARTER // AROWS, 96 // AROWS
    still = lambda *shape: pl.BlockSpec(shape, lambda g: (g, 0))
    specs = [still(AROWS, 3 * D), still(AROWS, D), still(AROWS, FF), still(D // steps, D)]
    turned = pl.BlockSpec((ATILE, D), lambda g: (jnp.minimum(g, TOK // ATILE - 1), 0))
    sums_specs = [
        pl.BlockSpec((2, 1, 3, 1, AROWS, BLK), lambda g: (0, g // per, 0, g % per, 0, 0)),
        pl.BlockSpec((3, 1, 1, AROWS, BLK), lambda g: (0, g // per, g % per, 0, 0)),
        pl.BlockSpec((1, 1, AROWS, D), lambda g: (0, g // per, g % per, 0)),
        pl.BlockSpec((CHUNKS, 1, AROWS, CHUNK), lambda g: (0, g // per, g % per, 0)),
        still(D // steps, D),
    ]
    shapes = [S((QUARTER, 3 * D), f32), S((QUARTER, D), f32), S((QUARTER, FF), f32), S((D, D), f32)]
    return pl.pallas_call(
        leave_kernel,
        grid=(steps,),
        in_specs=[pl.BlockSpec(memory_space=pltpu.SMEM), whole((TOK, D)), whole((TOK, D))] + sums_specs
        + [s for s in specs for _ in range(3)],
        out_specs=[turned] * 2 + [s for s in specs for _ in range(3)],
        out_shape=[S((TOK, D), bf16)] * 2 + [s for s in shapes for _ in range(3)],
        compiler_params=pltpu.CompilerParams(vmem_limit_bytes=60 << 20),
    )(lens, block, token, sq.reshape(2, 2, 3, per, AROWS, BLK), sh.reshape(3, 2, per, AROWS, BLK), so, se, sr.reshape(D, D), *state)


def per_device(
    tokens,
    lengths,
    cotangent,
    heads_master,
    output_master,
    expand_master,
    reduce_master,
    vector_master,
    heads_moment,
    output_moment,
    expand_moment,
    reduce_moment,
    vector_moment,
    heads_square,
    output_square,
    expand_square,
    reduce_square,
    vector_square,
):
    digits = ring_of(lax.axis_size("dp"))
    (x, dy, n1, n1T, n2, n2T, vectors, bias, cos, sin, mask, heads_weight, output_weight, expand_own, reduce_own) = enter(
        lengths, tokens, cotangent, vector_master.reshape(VEC_ROWS, SEG), heads_master, output_master, expand_master,
        reduce_master, 1)
    heads_grad, output_grad, base, grad, vector_grad, expand_weight, reduce_weight, part = attention(
        x, n1, n1T, dy, heads_weight, output_weight, vectors, cos, sin, mask, expand_own, reduce_own, 2)
    block, token, *sums = feed(
        n2, n2T, dy, x, vectors, bias, expand_weight, reduce_weight, base, grad, heads_grad,
        output_grad.reshape(1, 4, 2, 96, D), part, vector_grad, digits, 3)
    state = [
        heads_master, heads_moment, heads_square, output_master, output_moment, output_square,
        expand_master, expand_moment, expand_square, reduce_master, reduce_moment, reduce_square,
    ]
    sum_h, sum_e, sum_r, sum_v, sum_o, sum_q = sums
    vector_new = adam_step(
        vector_master, vector_moment, vector_square, sum_v.reshape(16, BLK)[:VEC_ROWS, :SEG].reshape(-1), vector_rate, 0.0)
    return (*leave(lengths, block, token, (sum_h, sum_e, sum_r, sum_o, sum_q), state), *vector_new)


def solution(mesh):
    placed = (
        P(("shard", "dp"), None),
        P(("shard", "dp"), None),
        P(("shard", "dp"), None),
        P("shard", None),
        P("shard", None),
        P("shard", None),
        P("shard", None),
        P("shard"),
        P("shard", None),
        P("shard", None),
        P("shard", None),
        P("shard", None),
        P("shard"),
        P("shard", None),
        P("shard", None),
        P("shard", None),
        P("shard", None),
        P("shard"),
    )
    return jax.shard_map(
        per_device,
        mesh=mesh,
        in_specs=placed,
        out_specs=(
            P(("shard", "dp"), None),
            P(("shard", "dp"), None),
            P("shard", None),
            P("shard", None),
            P("shard", None),
            P("shard", None),
            P("shard", None),
            P("shard", None),
            P("shard", None),
            P("shard", None),
            P("shard", None),
            P("shard", None),
            P("shard", None),
            P("shard", None),
            P("shard"),
            P("shard"),
            P("shard"),
        ),
        check_vma=False,
    )
```

```python
import functools

import jax
import jax.numpy as jnp
from jax import lax
from jax.experimental import pallas as pl
from jax.experimental.pallas import tpu as pltpu
from jax.sharding import PartitionSpec as P

D = 768
HEADS = 12
HEAD = 64
ROT = 16
FF = 3072
STEP = 10
TOK = 1024
LONG = 768
BLK = 256
CHUNK = 512
BW = CHUNK // 4
HROWS = 3 * 96
CHUNKS = FF // CHUNK
QUARTER = D // 4
SEG = 192
TILE = 128
ATILE = 512
AROWS = 96
FTILE = 512

first_decay = 0.9
second_decay = 0.95
adam_epsilon = 1e-08
matrix_decay = 0.1
matrix_rate = 0.04
vector_rate = 0.2
norm_epsilon = 1e-05
score_scale = 0.125
rotary_base = 10000.0
masked_score = -1e30
LOG2E = 1.4426950408889634

f32 = jnp.float32
bf16 = jnp.bfloat16
MESH = pl.DeviceIdType.MESH
NN = (((1,), (0,)), ((), ()))
NT = (((1,), (1,)), ((), ()))
TN = (((0,), (0,)), ((), ()))
TT = (((0,), (1,)), ((), ()))

GAIN_ONE, SHIFT_ONE, GAIN_TWO, SHIFT_TWO, HEADS_BIAS, OUTPUT_BIAS, EXPAND_BIAS, REDUCE_BIAS = 0, 1, 2, 3, 4, 7, 8, 12
VEC_ROWS = 13


def dot(a, b, dims=NN):
    return lax.dot_general(a, b, dims, preferred_element_type=f32)


def total(parts):
    return functools.reduce(jnp.add, parts)


def any_spec():
    return pl.BlockSpec(memory_space=pl.ANY)


def whole(shape):
    return pl.BlockSpec(shape, lambda g: (0,) * len(shape), pipeline_mode=pl.Buffered(1))


def norm_rows(values):
    centred = values - jnp.mean(values, -1, keepdims=True)
    inverse = lax.rsqrt(jnp.mean(centred * centred, -1, keepdims=True) + norm_epsilon)
    return centred * inverse, inverse


def norm_back(values, gain, grad):
    normed, inverse = norm_rows(values)
    scaled = grad * gain
    back = inverse * (
        scaled - jnp.mean(scaled, -1, keepdims=True) - normed * jnp.mean(scaled * normed, -1, keepdims=True)
    )
    return back, jnp.sum(grad * normed, 0, keepdims=True), jnp.sum(grad, 0, keepdims=True)


def place():
    s=lax.axis_index("shard"); d=lax.axis_index("dp")
    c=d%2
    s1=s+1-2*(s%2); s2=s+2-4*(s//2)
    a=(1-c)*s1+c*s2
    b=(1-c)*s2+c*s1
    return s,d,c,a,b

def rcopy(src,dst,ssem,rsem,sh,dp):
    return pltpu.make_async_remote_copy(src_ref=src,dst_ref=dst,send_sem=ssem,recv_sem=rsem,device_id=(sh,dp),device_id_type=MESH)

def greet(peers):
    bar=pltpu.get_barrier_semaphore()
    for sh,dp in peers:
        pl.semaphore_signal(bar,inc=1,device_id=(sh,dp),device_id_type=MESH)
    pl.semaphore_wait(bar,len(peers))

class Gather:
    def __init__(self,own,full,ssem,rsem,lsem,split=True,lo=0,n=None,skip=0):
        self.own,self.full,self.ss,self.rs,self.ls=own,full,ssem,rsem,lsem
        self.s,self.d,self.c,self.a,self.b=place()
        self.sib=self.d+1-2*self.c
        self.R=own.shape[-2]; self.split=split
        self.h=self.R//2 if split else self.R
        self.lo=lo; self.n=n or self.h; self.skip=skip
    def sl(self,ref,row,n):
        row=pl.multiple_of(row,16)
        if ref is self.full and self.skip: return ref.at[pl.ds(row,n),pl.ds(self.skip,ref.shape[1]-self.skip)]
        if len(ref.shape)==2: return ref.at[pl.ds(row,n)]
        return ref.at[:,pl.ds(row,n)]
    def region(self,sh,core):
        return self.sl(self.full,sh*self.R+(core*self.h if self.split else 0)+self.lo,self.n)
    def mine(self):
        return self.sl(self.own,(self.c*self.h if self.split else 0)+self.lo,self.n)
    def cp(self,k,src,reg,sh,dp): return rcopy(src,reg,self.ss.at[k],self.rs.at[k],sh,dp)
    def local(self):
        return pltpu.make_async_copy(self.own,self.sl(self.full,self.s*self.R,self.R),self.ls)
    def start(self):
        r=self.region(self.s,self.c)
        self.cp(0,self.mine(),r,self.a,self.d).start()
        self.cp(1,self.mine(),r,self.b,self.d).start()
        if self.lo==0: self.local().start()
    def _wait_recv(self,k,sh,core):
        r=self.region(sh,core)
        self.cp(k,r,r,self.s,self.sib).wait_recv()
    def _wait_send(self,k,sh,core):
        r=self.region(sh,core)
        self.cp(k,r,r,self.s,self.sib).wait_send()
    def forward(self):
        ra=self.region(self.a,self.c)
        self._wait_recv(0,self.a,self.c)
        self.cp(2,ra,ra,self.b,self.d).start()
        if self.split: self.cp(3,ra,ra,self.s,self.sib).start()
        self._wait_recv(1,self.b,self.c)
        rb=self.region(self.b,self.c)
        if self.split: self.cp(4,rb,rb,self.s,self.sib).start()
    def diag(self):
        x=3-self.s
        self._wait_recv(2,x,self.c)
        rx=self.region(x,self.c)
        if self.split: self.cp(5,rx,rx,self.s,self.sib).start()
    def finish(self):
        if self.lo==0: self.local().wait()
        x=3-self.s
        if self.split:
            o=1-self.c
            self._wait_recv(3,self.b,o)
            self._wait_recv(4,self.a,o)
            self._wait_recv(5,x,o)
        self.cp(0,self.mine(),self.region(self.s,self.c),self.a,self.d).wait_send()
        self.cp(1,self.mine(),self.region(self.s,self.c),self.b,self.d).wait_send()
        for k,sh in ((2,self.a),)+(((3,self.a),(4,self.b),(5,x)) if self.split else ()):
            self._wait_send(k,sh,self.c)

def gather_peers():
    s,d,c,a,b=place()
    return [(a,d),(b,d),(s,d+1-2*c)]

def ring_of(dp_size):
    digits=[]; n=dp_size//2; stride=1
    while n>1:
        assert n%4==0
        digits.append(stride); stride*=4; n//=4
    return digits

class Reduce:
    def __init__(self,digits,mine,other,Y,SA,RA,T,SB,RB,SZ,RZ,RM,gout,ss,rs):
        self.digits=digits; self.mine=mine; self.other=other
        self.Y,self.SA,self.RA,self.T,self.SB,self.RB,self.SZ,self.RZ,self.RM,self.gout,self.ss,self.rs=Y,SA,RA,T,SB,RB,SZ,RZ,RM,gout,ss,rs
        self.s,self.d,self.c,self.a,self.b=place()
        self.sib=self.d+1-2*self.c
        self.x=3-self.s
    def cp(self,j,k,src,dst,sh,dp): return rcopy(src,dst,self.ss.at[j,k],self.rs.at[j,k],sh,dp)
    def role(self,i):
        st=self.digits[i]; p=((self.d//2)//st)%4
        end=(p==0)|(p==3)
        mate=self.d+2*st*jnp.where(p==0,1,jnp.where(p==3,-1,jnp.where(p==1,1,-1)))
        tip=self.d+2*st*jnp.where(p==1,-1,1)
        return end,mate,tip
    def stages(self): return 4+3*len(self.digits)+1
    def c0(self,k): return self.cp(0,k,self.other(k),self.Y.at[k%2],self.s,self.sib)
    def cA(self,k): return self.cp(1,k,self.SA.at[k%2],self.RA.at[k%2],self.a,self.d)
    def cB(self,k): return self.cp(2,k,self.SB.at[k%2],self.RB.at[k%2],self.b,self.d)
    def nt(self,k): return k%self.T.shape[0]
    def s0(self,k):
        self.c0(k).start()
    def s1(self,k):
        self.c0(k).wait()
        X=self.mine(k)
        def U(p): return X[p]+self.Y[k%2,p]
        self.SA[k%2,0]=U(self.a).astype(self.SA.dtype)
        self.SA[k%2,1]=U(self.x).astype(self.SA.dtype)
        self.cA(k).start()
        t=self.nt(k)
        self.T[t,0]=U(self.s)
        self.T[t,1]=U(self.b)
    def s2(self,k):
        self.cA(k).wait()
        t=self.nt(k)
        self.SB[k%2]=(self.T[t,1]+self.RA[k%2,1].astype(f32)).astype(self.SB.dtype)
        self.cB(k).start()
        self.T[t,0]=self.T[t,0]+self.RA[k%2,0].astype(f32)
    def plane(self,k):
        self.cB(k).wait()
        t=self.nt(k)
        self.T[t,0]=self.T[t,0]+self.RB[k%2].astype(f32)
    def s3(self,k):
        self.plane(k)
        self.za(0,k)
    def g(self,k): return self.gout.at[k,self.c]
    def zcp(self,i,j,k,src,dst,dp): return self.cp(3+4*i+j,k,src,dst,self.s,dp)
    def za(self,i,k):
        t=self.nt(k); end,mate,tip=self.role(i)
        @pl.when(end)
        def _():
            self.SZ[i,k%2]=self.T[t,0].astype(self.SZ.dtype)
            self.zcp(i,0,k,self.SZ.at[i,k%2],self.RZ.at[i,k%3],mate).start()
    def zb(self,i,k):
        t=self.nt(k); end,mate,tip=self.role(i)
        @pl.when(jnp.logical_not(end))
        def _():
            self.zcp(i,0,k,self.SZ.at[i,k%2],self.RZ.at[i,k%3],tip).wait_recv()
            self.SZ[i,k%2]=(self.T[t,0]+self.RZ[i,k%3].astype(f32)).astype(self.SZ.dtype)
            self.zcp(i,1,k,self.SZ.at[i,k%2],self.RM.at[i,k%2],mate).start()
        @pl.when(end)
        def _():
            self.zcp(i,0,k,self.SZ.at[i,k%2],self.RZ.at[i,k%3],mate).wait_send()
    def to_sib(self,k):
        return self.cp(3+4*len(self.digits),k,self.g(k),self.g(k),self.s,self.sib)
    def zc(self,i,k):
        end,mate,tip=self.role(i); last=i==len(self.digits)-1
        @pl.when(jnp.logical_not(end))
        def _():
            self.zcp(i,1,k,self.SZ.at[i,k%2],self.RM.at[i,k%2],mate).wait()
            self.gout[k,self.c]=(self.SZ[i,k%2].astype(f32)+self.RM[i,k%2].astype(f32)).astype(self.gout.dtype)
            self.zcp(i,2,k,self.g(k),self.g(k),tip).start()
            if last: self.to_sib(k).start()
    def zd(self,i,k):
        end,mate,tip=self.role(i); last=i==len(self.digits)-1
        @pl.when(jnp.logical_not(end))
        def _():
            self.zcp(i,2,k,self.g(k),self.g(k),tip).wait_send()
        @pl.when(end)
        def _():
            self.zcp(i,2,k,self.g(k),self.g(k),mate).wait_recv()
            if last: self.to_sib(k).start()
        if not last:
            self.T[self.nt(k),0]=self.gout[k,self.c].astype(f32)
            self.za(i+1,k)
    def fin(self,k):
        self.to_sib(k).wait_send()
        g=self.gout.at[k,1-self.c]
        self.cp(3+4*len(self.digits),k,g,g,self.s,self.sib).wait_recv()
    def stage_list(self):
        return [self.s0,self.s1,self.s2,self.s3]+self.chain()
    def chain(self):
        out=[]
        for i in range(len(self.digits)):
            out+=[functools.partial(self.zb,i),functools.partial(self.zc,i),functools.partial(self.zd,i)]
        return out+[self.fin]

def reduce_peers(digits):
    s,d,c,a,b=place()
    peers=[(a,d),(b,d),(s,d+1-2*c)]
    for st in digits:
        p=((d//2)//st)%4
        up=d+2*st*jnp.where(p==3,-3,1); down=d+2*st*jnp.where(p==0,3,-1)
        peers+=[(s,up),(s,down)]
    return peers

def stream_scratch(n, r, w, nd, kind):
    V, S = pltpu.VMEM, pltpu.SemaphoreType.DMA
    ring = min(n, 4 + 3 * (nd - 1))
    return [
        V((2, 4, r, w), f32), V((2, 2, r, w), kind), V((2, 2, r, w), kind), V((ring, 2, r, w), f32),
        V((2, r, w), kind), V((2, r, w), kind), V((nd, 2, r, w), kind), V((nd, 3, r, w), kind), V((nd, 2, r, w), kind),
        S((4 + 4 * nd, n)), S((4 + 4 * nd, n)),
    ]


STREAM = 11


def enter_kernel(
    lens, x_hbm, dy_hbm, vec_own, heads_hbm, output_hbm, expand_hbm, reduce_hbm,
    x_out, dy_out, n1_out, n1T_out, n2_out, n2T_out, vec_ref, bias_ref, cos_ref, sin_ref, mask_ref, heads_full, output_full, e_out, r_out, h_out,
    vec_full, vec_low, xs, ds, normed, n1, n1T, n2, n2T, heads_in, output_in, expand_in, reduce_in, heads_own, heads_rest, output_own,
    eown, rown, ss, rs, ls, ins, outs,
):
    loads = [
        pltpu.make_async_copy(src, dst, ins.at[i])
        for i, (src, dst) in enumerate((
            (heads_hbm, heads_in), (output_hbm, output_in), (x_hbm, xs), (dy_hbm, ds), (expand_hbm, expand_in),
            (reduce_hbm, reduce_in),
        ))
    ]
    stores = [
        pltpu.make_async_copy(src, dst, outs.at[i])
        for i, (src, dst) in enumerate((
            (xs, x_out), (ds, dy_out), (n1, n1_out), (n1T, n1T_out), (n2, n2_out), (n2T, n2T_out), (eown, e_out),
            (rown, r_out), (heads_rest, h_out),
        ))
    ]
    for copy in loads:
        copy.start()
    gv = Gather(vec_low, vec_full, ss.at[0], rs.at[0], ls.at[0], False)
    gh = Gather(heads_own, heads_full, ss.at[1], rs.at[1], ls.at[1])
    go = Gather(output_own, output_full, ss.at[2], rs.at[2], ls.at[2])
    vec_low[...] = jnp.zeros_like(vec_low)
    vec_low[0:VEC_ROWS, 0:SEG] = vec_own[...].astype(bf16)
    greet(gather_peers())
    gv.start()
    loads[0].wait()
    for k in range(3):
        heads_own[:, BLK * k : BLK * k + BLK] = heads_in[:, D * k : D * k + BLK].astype(bf16)
    gh.start()
    loads[1].wait()
    output_own[...] = output_in[...].astype(bf16)
    go.start()
    first, second, third = lens[0, 0], lens[0, 1], lens[0, 2]
    start = jnp.where(first == LONG, 0, jnp.where(second == LONG, first, first + second))
    short = jnp.where(first == LONG, second, jnp.where(second == LONG, third, first))
    from_row = lax.broadcasted_iota(jnp.int32, (BLK, TOK), 1)

    def turn(ref):
        values, parts = ref[...], []
        for i in range(TOK // BLK):
            want = lax.broadcasted_iota(jnp.int32, (BLK, TOK), 0) + (i * BLK + start)
            want = jnp.where(want >= TOK, want - TOK, want)
            parts.append(dot((want == from_row).astype(bf16), values).astype(bf16))
        for i, part in enumerate(parts):
            ref[BLK * i : BLK * i + BLK] = part

    loads[2].wait()
    turn(xs)
    stores[0].start()
    for i in range(TOK // BLK):
        normed[BLK * i : BLK * i + BLK] = norm_rows(xs[BLK * i : BLK * i + BLK].astype(f32))[0]
    gv.forward()
    loads[3].wait()
    turn(ds)
    stores[1].start()
    gv.diag()
    row = lax.broadcasted_iota(jnp.int32, (8, TOK), 1)
    late = row - LONG
    position = jnp.where(late < 0, row, jnp.where(late >= short, late - short, late)).astype(f32)
    step = lax.broadcasted_iota(jnp.int32, (8, TOK), 0).astype(f32)
    angles = position * jnp.exp2(step * (-2.0 / ROT * 13.287712379549449))
    cos_ref[...] = jnp.cos(angles)
    sin_ref[...] = jnp.sin(angles)
    key = lax.broadcasted_iota(jnp.int32, (BLK, BLK), 0)
    query = lax.broadcasted_iota(jnp.int32, (BLK, BLK), 1)
    allowed = ((key >= short) == (query >= short)) & (key <= query)
    mask_ref[...] = jnp.where(allowed, 0.0, masked_score)
    gv.finish()
    vec_ref[...] = jnp.zeros_like(vec_ref)
    for i in range(4 * VEC_ROWS):
        s, r = i // VEC_ROWS, i % VEC_ROWS
        piece = vec_full[16 * s : 16 * s + 16].astype(f32)[r : r + 1, 0:SEG]
        vec_ref[i // 4 : i // 4 + 1, SEG * (i % 4) : SEG * (i % 4) + SEG] = piece
    for g in range(CHUNKS):
        for s in range(4):
            bias_ref[g, :, BW * s : BW * s + BW] = vec_ref[EXPAND_BIAS + s : EXPAND_BIAS + s + 1, BW * g : BW * g + BW]
    gh.forward()
    go.forward()
    for out, outT, gain, shift, k in ((n1, n1T, GAIN_ONE, SHIFT_ONE, 2), (n2, n2T, GAIN_TWO, SHIFT_TWO, 4)):
        for i in range(TOK // BLK):
            rows = slice(BLK * i, BLK * i + BLK)
            low = (normed[rows] * vec_ref[gain : gain + 1] + vec_ref[shift : shift + 1]).astype(bf16)
            out[rows] = low
            outT[:, rows] = low.T
        stores[k].start()
        stores[k + 1].start()
        if k == 2:
            gh.diag()
    for k in range(3):
        for g in (1, 2):
            at = D * (g - 1) + BLK * k
            heads_rest[:, at : at + BLK] = heads_in[:, D * k + BLK * g : D * k + BLK * g + BLK].astype(bf16)
    stores[8].start()
    loads[4].wait()
    for g in range(CHUNKS):
        for s in range(4):
            eown[g, :, BW * s : BW * s + BW] = expand_in[:, D * s + BW * g : D * s + BW * g + BW].astype(bf16)
    stores[6].start()
    loads[5].wait()
    rown[...] = reduce_in[...].astype(bf16).reshape(rown.shape)
    stores[7].start()
    go.diag()
    gh.finish()
    go.finish()
    for copy in stores:
        copy.wait()


def enter(lens, x, dy, vec, heads, output, expand, reduce, cid):
    S, V, sem = jax.ShapeDtypeStruct, pltpu.VMEM, pltpu.SemaphoreType.DMA
    vmem = pl.BlockSpec(memory_space=pltpu.VMEM)
    tall, wide = (TOK, D), (D, TOK)
    return pl.pallas_call(
        enter_kernel,
        in_specs=[pl.BlockSpec(memory_space=pltpu.SMEM), any_spec(), any_spec(), vmem] + [any_spec()] * 4,
        out_specs=[any_spec()] * 6 + [vmem] * 5 + [any_spec()] * 5,
        out_shape=[S(tall, bf16), S(tall, bf16), S(tall, bf16), S(wide, bf16), S(tall, bf16), S(wide, bf16)]
        + [S((16, D), f32), S((CHUNKS, 1, CHUNK), f32), S((8, TOK), f32), S((8, TOK), f32), S((BLK, BLK), f32)]
        + [S((D, D), bf16), S((D, D), bf16), S((CHUNKS, QUARTER, CHUNK), bf16), S((CHUNKS, BW, D), bf16)]
        + [S((QUARTER, 2 * D), bf16)],
        scratch_shapes=[
            V((64, BLK), bf16), V((16, BLK), bf16), V(tall, bf16), V(tall, bf16), V(tall, f32), V(tall, bf16),
            V(wide, bf16), V(tall, bf16), V(wide, bf16), V((QUARTER, 3 * D), f32), V((QUARTER, D), f32),
            V((QUARTER, FF), f32), V((D, D), f32), V((QUARTER, D), bf16), V((QUARTER, 2 * D), bf16), V((QUARTER, D), bf16),
            V((CHUNKS, QUARTER, CHUNK), bf16), V((CHUNKS, BW, D), bf16), sem((3, 6)), sem((3, 6)), sem((3,)), sem((6,)),
            sem((9,)),
        ],
        compiler_params=pltpu.CompilerParams(vmem_limit_bytes=60 << 20, collective_id=cid, has_side_effects=True),
    )(lens, x, dy, vec, heads, output, expand, reduce)


def attention_kernel(
    x_hbm, n1_ref, n1T_hbm, dy_ref, w_hbm, h_hbm, wo_ref, vec_ref, cos_ref, sin_ref, mask_ref, e_hbm, r_hbm,
    hh_out, og_ref, base_out, grad_ref, vgrad_ref, efull, rfull, part_out,
    qT, kT, vT, oT, cT, gq, gk, gv, dn1T, ss, rs, ls, x2, Y, SA, RA, T, SB, RB, ps, pr, os,
    x_ref, n1T_ref, eown, rown, base_ref, w_all, hown, ins,
):
    g = pl.program_id(0)
    ge = Gather(eown, efull, ss.at[0], rs.at[0], ls.at[0])
    gr = Gather(rown, rfull, ss.at[1], rs.at[1], ls.at[1])
    gw = Gather(hown, w_all, ss.at[2], rs.at[2], ls.at[2], skip=D)
    c = place()[2]
    part = Reduce((), lambda k: x2.at[:, c], lambda k: x2.at[:, 1 - c], Y, SA, RA, T, SB, RB, None, None, None, None, ps, pr)

    loads = [
        pltpu.make_async_copy(src, dst, ins.at[i])
        for i, (src, dst) in enumerate(((h_hbm, hown), (w_hbm, w_all.at[:, 0:D]), (e_hbm, eown), (r_hbm, rown), (n1T_hbm, n1T_ref), (x_hbm, x_ref)))
    ]
    base_copy = pltpu.make_async_copy(base_ref, base_out, os.at[3])

    @pl.when(g == 0)
    def _():
        for copy in loads:
            copy.start()
        greet(gather_peers())
        loads[0].wait()
        gw.start()
        loads[1].wait()
        vgrad_ref[...] = jnp.zeros_like(vgrad_ref)

    @pl.when(g == 2)
    def _():
        gr.forward()

    heads = BLK // HEAD
    n1 = n1_ref[...]
    cos, sin = cos_ref[...], sin_ref[...]
    cols = pl.ds(pl.multiple_of(g * BLK, BLK), BLK)

    def column(row):
        return jnp.transpose(jnp.broadcast_to(vec_ref[row : row + 1, cols], (8, BLK)))[:, 0:1]

    def weight(k):
        return w_all[:, pl.ds(pl.multiple_of(g * D + BLK * k, BLK), BLK)]

    def proj(k):
        return dot(weight(k), n1, TT) + column(HEADS_BIAS + k)

    def rot(x):
        parts = []
        for h in range(heads):
            a, b = x[64 * h : 64 * h + 8], x[64 * h + 8 : 64 * h + 16]
            parts += [a * cos - b * sin, b * cos + a * sin, x[64 * h + 16 : 64 * h + 64]]
        return jnp.concatenate(parts, 0)

    def unrot(x):
        a, b = x[0:8], x[8:16]
        return jnp.concatenate([a * cos + b * sin, b * cos - a * sin, x[16:64]], 0)

    qT[...] = rot(proj(0)).astype(bf16)
    kT[...] = rot(proj(1)).astype(bf16)
    vT[...] = proj(2).astype(bf16)
    oT[...] = dot(wo_ref[...], dy_ref[...], NT).astype(bf16)
    key = lax.broadcasted_iota(jnp.int32, (BLK, BLK), 0)
    query = lax.broadcasted_iota(jnp.int32, (BLK, BLK), 1)
    causal = key <= query
    scale = score_scale * LOG2E
    nb = TOK // BLK
    @pl.loop(0, heads // 2)
    def _(pair):
        @pl.when((g == 0) & (pair == 1))
        def _():
            gw.forward()
            loads[2].wait()
            ge.start()

        @pl.when((g == 1) & (pair == 0))
        def _():
            part.s1(0)
            ge.forward()

        @pl.when((g == 2) & (pair == 0))
        def _():
            ge.diag()
            part.s2(0)
            part.s1(1)

        for h in (2 * pair, 2 * pair + 1):
            r = pl.ds(pl.multiple_of(HEAD * h, HEAD), HEAD)
            QT, KT, VT, OT = qT[r, :], kT[r, :], vT[r, :], oT[r, :]
            K, V, Q, O = KT.T, VT.T, QT.T, OT.T
            dK, dV, dQT, context = [[] for _ in range(nb)], [[] for _ in range(nb)], [], []
            for j in range(nb):
                blocks = list(range(0 if j < nb - 1 else j, j + 1))
                span = [slice(BLK * b, BLK * b + BLK) for b in blocks]
                q, o = QT[:, BLK * j : BLK * j + BLK], OT[:, BLK * j : BLK * j + BLK]
                S = [dot(K[c], q) * scale for c in span]
                S[-1] = jnp.where(causal, S[-1], masked_score) if j < nb - 1 else S[-1] + mask_ref[...]
                top = functools.reduce(jnp.maximum, [jnp.max(s, 0, keepdims=True) for s in S])
                E = [jnp.exp2(s - top) for s in S]
                inv = 1.0 / total([jnp.sum(e, 0, keepdims=True) for e in E])
                soft = [e * inv for e in E]
                low = [p.astype(bf16) for p in soft]
                context.append(total([dot(VT[:, c], p) for c, p in zip(span, low)]).astype(bf16))
                back = [dot(V[c], o) for c in span]
                row = total([jnp.sum(d * p, 0, keepdims=True) for d, p in zip(back, soft)])
                dS = [(p * (d - row)).astype(bf16) for d, p in zip(back, soft)]
                dQT.append(total([dot(KT[:, c], s) for c, s in zip(span, dS)]) * score_scale)
                for b, p, s in zip(blocks, low, dS):
                    dK[b].append(dot(s, Q[BLK * j : BLK * j + BLK]))
                    dV[b].append(dot(p, O[BLK * j : BLK * j + BLK]))
            cT[r, :] = jnp.concatenate(context, 1)
            gq[r, :] = unrot(jnp.concatenate(dQT, 1)).astype(bf16)
            gk[r, :] = unrot(jnp.concatenate([total(d) for d in dK], 0).T * score_scale).astype(bf16)
            gv[r, :] = jnp.concatenate([total(d) for d in dV], 0).T.astype(bf16)
    @pl.when(g == 2)
    def _():
        gr.diag()
        part.plane(0)
        part.s2(1)

    @pl.when(g == 0)
    def _():
        gw.diag()
        loads[3].wait()
        gr.start()
        loads[4].wait()
        loads[5].wait()

    n1T = n1T_ref[...]
    ones = jnp.ones((8, TOK), bf16)
    parts = []
    for k, grads in enumerate((gq, gk, gv)):
        G = grads[...]
        x2[:, :, 96 * k : 96 * k + 96] = dot(n1T, G, NT).reshape(4, 2, 96, BLK)
        vgrad_ref[HEADS_BIAS + k : HEADS_BIAS + k + 1, cols] = dot(ones, G, NT)[0:1]
        parts.append(dot(weight(k), G))

    @pl.when(g == 0)
    def _():
        part.s0(0)

    @pl.when(g == 1)
    def _():
        part.s0(1)

    heads_copy = pltpu.make_async_copy(x2, hh_out, os.at[2])
    part_copies = [pltpu.make_async_copy(T.at[k, 0], part_out.at[k], os.at[k]) for k in range(2)]

    @pl.when(g == 2)
    def _():
        heads_copy.start()

    ctx = cT[...]
    og_ref[...] = dot(ctx, dy_ref[...])
    out = dot(ctx, wo_ref[...], TN)

    @pl.when(g == 0)
    def _():
        bias = vec_ref[OUTPUT_BIAS : OUTPUT_BIAS + 1] + vec_ref[REDUCE_BIAS : REDUCE_BIAS + 1]
        gw.finish()
        base_ref[...] = out + (x_ref[...].astype(f32) + bias)
        dn1T[...] = total(parts)

    @pl.when(g > 0)
    def _():
        base_ref[...] += out
        dn1T[...] += total(parts)

    @pl.when(g == D // BLK - 1)
    def _():
        base_copy.start()
        vgrad_ref[GAIN_ONE : SHIFT_ONE + 1] = jnp.zeros((2, D), f32)
        vgrad_ref[OUTPUT_BIAS : OUTPUT_BIAS + 1] = jnp.zeros((1, D), f32)

        @pl.loop(0, TOK // TILE)
        def _(i):
            rows = pl.ds(pl.multiple_of(TILE * i, TILE), TILE)
            dy = dy_ref[rows].astype(f32)
            back, gain, shift = norm_back(
                x_ref[rows].astype(f32), vec_ref[GAIN_ONE : GAIN_ONE + 1], dn1T[:, rows].T
            )
            grad_ref[rows] = dy + back
            vgrad_ref[GAIN_ONE : GAIN_ONE + 1] += gain
            vgrad_ref[SHIFT_ONE : SHIFT_ONE + 1] += shift
            vgrad_ref[OUTPUT_BIAS : OUTPUT_BIAS + 1] += jnp.sum(dy, 0, keepdims=True)

        vgrad_ref[REDUCE_BIAS : REDUCE_BIAS + 1] = vgrad_ref[OUTPUT_BIAS : OUTPUT_BIAS + 1]
        part.plane(1)
        for copy in part_copies:
            copy.start()
        ge.finish()
        gr.finish()
        for copy in part_copies + [heads_copy, base_copy]:
            copy.wait()


def attention(x, n1, n1T, dy, W, rest, Wo, vec, cos, sin, mask, eown, rown, cid):
    G = D // BLK
    S, V = jax.ShapeDtypeStruct, pltpu.VMEM
    rows = pl.BlockSpec((BLK, D), lambda g: (g, 0))
    sem = pltpu.SemaphoreType.DMA
    return pl.pallas_call(
        attention_kernel,
        grid=(G,),
        in_specs=[
            any_spec(), whole((TOK, D)), any_spec(), whole((TOK, D)), any_spec(), any_spec(), rows,
            whole((16, D)), whole((8, TOK)), whole((8, TOK)), whole((BLK, BLK)),
            any_spec(), any_spec(),
        ],
        out_specs=[
            any_spec(), rows, any_spec(), whole((TOK, D)), whole((16, D)),
            any_spec(), any_spec(), any_spec(),
        ],
        out_shape=[
            S((4, 2, HROWS, BLK), f32), S((D, D), f32), S((TOK, D), f32), S((TOK, D), f32), S((16, D), f32),
            S((CHUNKS, D, CHUNK), bf16), S((CHUNKS, CHUNK, D), bf16), S((2, HROWS, BLK), f32),
        ],
        scratch_shapes=[V((BLK, TOK), bf16)] * 8 + [
            V((D, TOK), f32), sem((3, 6)), sem((3, 6)), sem((3,)), V((4, 2, HROWS, BLK), f32), V((2, 4, HROWS, BLK), f32),
            V((2, 2, HROWS, BLK), bf16), V((2, 2, HROWS, BLK), bf16), V((2, 2, HROWS, BLK), f32), V((2, HROWS, BLK), bf16),
            V((2, HROWS, BLK), bf16), sem((3, 2)), sem((3, 2)), sem((4,)),
            V((TOK, D), bf16), V((D, TOK), bf16), V(eown.shape, bf16), V(rown.shape, bf16), V((TOK, D), f32),
            V((D, 3 * D), bf16), V((QUARTER, 2 * D), bf16), sem((6,)),
        ],
        compiler_params=pltpu.CompilerParams(vmem_limit_bytes=60 << 20, collective_id=cid, has_side_effects=True),
    )(x, n1, n1T, dy, W, rest, Wo, vec, cos, sin, mask, eown, rown)


def feed_kernel(
    digits, n2_ref, n2T_hbm, dy_ref, x_hbm, vec_ref, bias_ref, we_ref, wr_ref, base_hbm, grad_hbm, hh, og, pv, vg_ref,
    out_hbm, token_hbm, sum_h, sum_e, sum_r, sum_v, sum_o, sum_q,
    gh, gx, gr, gv, go, gq, os, acc, dn2, act_ref, hid_ref, sums, bge, ex, rx, vx, hx, ox, ls, bs, qT, qSZ, qRZ, qRM, qss, qrs, n2T_ref, x_ref, out_ref, token_ref, *scratch,
):
    t = pl.program_id(0)
    c = place()[2]
    parts = [scratch[STREAM * i : STREAM * i + STREAM] for i in range(5)]

    def stream(i, mine, other, gout):
        return Reduce(digits, mine, other, *parts[i][:9], gout, parts[i][9], parts[i][10])

    def heads_part(k, core):
        return hh.at[:, core, pl.ds(pl.multiple_of(96 * k, 16), 96)]

    H = stream(0, lambda k: hx.at[k % 2], lambda k: heads_part(k, 1 - c), gh)
    Q = Reduce(digits, None, None, None, None, None, qT, None, None, qSZ, qRZ, qRM, gq, qss, qrs)
    O = stream(4, lambda k: ox, lambda k: og.at[0, :, 1 - c], go)
    E = stream(1, lambda k: ex.at[:, c], lambda k: ex.at[:, 1 - c], gx)
    R = stream(2, lambda k: rx.at[:, c], lambda k: rx.at[:, 1 - c], gr)
    Z = stream(3, lambda k: vx.at[:, c], lambda k: vx.at[:, 1 - c], gv)

    ways = ((gh, sum_h), (gx, sum_e), (gr, sum_r), (gv, sum_v), (go, sum_o), (gq, sum_q))

    def hand(i, k):
        return pltpu.make_async_copy(ways[i][0].at[k], ways[i][1].at[k], os.at[i, k])

    def load_part(i, k):
        if i == 4:
            return pltpu.make_async_copy(og.at[0, :, c], ox, ls.at[3])
        if i == 5:
            return pltpu.make_async_copy(pv.at[k], qT.at[k, 0], ls.at[4 + k])
        return pltpu.make_async_copy(heads_part(k, c), hx.at[k % 2], ls.at[k])

    def load_base():
        return pltpu.make_async_copy(base_hbm, acc, bs.at[0])

    def load_grad():
        return pltpu.make_async_copy(grad_hbm, acc, bs.at[1])

    early = [
        pltpu.make_async_copy(n2T_hbm, n2T_ref, bs.at[2]), pltpu.make_async_copy(x_hbm, x_ref, bs.at[3]),
    ]
    late = [
        pltpu.make_async_copy(out_ref, out_hbm, bs.at[4]), pltpu.make_async_copy(token_ref, token_hbm, bs.at[5]),
    ]

    @pl.when(t == 0)
    def _():
        load_part(5, 0).start()
        load_part(5, 1).start()
        greet(reduce_peers(digits))
        load_base().start()
        for copy in early:
            copy.start()

    streams = [
        (s.stage_list(), n, first) for s, n, first in ((H, 3, 0), (E, CHUNKS, 0), (R, CHUNKS, 0), (Z, 1, CHUNKS - 1), (O, 1, 0))
    ] + [([None] + Q.chain(), 2, 0)]

    def advance(i):
        stages, n, first = streams[i]
        last = len(stages) - 1

        @pl.when((t > first) & (t < first + n + last))
        def _():
            for j in range(last, 0, -1):

                @pl.when((t >= j + first) & (t < j + first + n))
                def _():
                    k = t - j - first
                    if j == 1 and i in (0, 4):
                        load_part(i, k).wait()
                    stages[j](k)
                    if j == last:
                        hand(i, k).start()

    advance(5)
    advance(0)
    advance(4)

    @pl.when(t < 2)
    def _():
        load_part(5, t).wait()
        Q.za(0, t)

    @pl.when(t < 3)
    def _():
        load_part(0, t).start()
        H.s0(t)

    @pl.when(t == 0)
    def _():
        load_part(4, 0).start()
        O.s0(0)

    @pl.when(t < CHUNKS)
    def _():
        we, wr = we_ref[0], wr_ref[0]
        bias = bias_ref[pl.ds(t, 1)][0]

        @pl.when(t == 0)
        def _():
            load_base().wait()
            for copy in early:
                copy.wait()
            dn2[...] = jnp.zeros_like(dn2)

        bge[pl.ds(t, 1)] = jnp.zeros((1, 1, CHUNK), f32)

        @pl.loop(0, TOK // FTILE)
        def _(i):
            rows = pl.ds(pl.multiple_of(FTILE * i, FTILE), FTILE)
            h = dot(n2_ref[rows], we) + bias
            cdf = 0.5 * (1.0 + lax.erf(h * 0.7071067811865476))
            pdf = jnp.exp2(h * h * (-0.5 * LOG2E)) * 0.3989422804014327
            active = (h * cdf).astype(bf16)
            hidden = (dot(dy_ref[rows], wr, NT) * (cdf + h * pdf)).astype(bf16)
            act_ref[rows] = active
            hid_ref[rows] = hidden
            bge[pl.ds(t, 1)] += jnp.sum(hidden.astype(f32), 0, keepdims=True)[None]
            acc[rows] += dot(active, wr)
            dn2[rows] += dot(hidden, we, NT)

    advance(2)

    @pl.when(t < CHUNKS)
    def _():
        rx[...] = dot(act_ref[...], dy_ref[...], TN).reshape(rx.shape)
        R.s0(t)

    advance(1)

    @pl.when(t < CHUNKS)
    def _():
        ex[...] = dot(n2T_ref[...], hid_ref[...]).reshape(ex.shape)
        E.s0(t)

    advance(3)

    @pl.when(t == CHUNKS - 1)
    def _():
        out_ref[...] = acc[...].astype(bf16)
        late[0].start()
        load_grad().start()
        sums[...] = jnp.zeros_like(sums)
        load_grad().wait()

        @pl.loop(0, TOK // TILE)
        def _(i):
            rows = pl.ds(pl.multiple_of(TILE * i, TILE), TILE)
            back, gain, shift = norm_back(x_ref[rows].astype(f32), vec_ref[GAIN_TWO : GAIN_TWO + 1], dn2[rows])
            token_ref[rows] = (acc[rows] + back).astype(bf16)
            sums[0:1] += gain
            sums[1:2] += shift

        rows = {k: vg_ref[k : k + 1] for k in range(VEC_ROWS) if k not in (2, 3, 8, 9, 10, 11)}
        rows[GAIN_TWO], rows[SHIFT_TWO] = sums[0:1], sums[1:2]
        for s in range(4):
            rows[EXPAND_BIAS + s] = jnp.concatenate([bge[g, :, BW * s : BW * s + BW] for g in range(CHUNKS)], 1)
        vx[...] = jnp.zeros_like(vx)
        for i in range(VEC_ROWS * 4):
            s, row = i // VEC_ROWS, i % VEC_ROWS
            vx[s, row // 8, row % 8 : row % 8 + 1, 0:SEG] = rows[i // 4][:, SEG * (i % 4) : SEG * (i % 4) + SEG]
        late[1].start()
        Z.s0(0)

    @pl.when(t == pl.num_programs(0) - 1)
    def _():
        for copy in late:
            copy.wait()
        for i, n in enumerate((3, CHUNKS, CHUNKS, 1, 1, 2)):
            for k in range(n):
                hand(i, k).wait()


def feed(n2, n2T, dy, x, vec, bias, We, Wr, base, grad, hh, og, part, vgrad, digits, cid):
    S, V, sem = jax.ShapeDtypeStruct, pltpu.VMEM, pltpu.SemaphoreType.DMA
    nd = len(digits)
    steps = CHUNKS + 4 + 3 * nd
    at = lambda t: jnp.minimum(t, CHUNKS - 1)
    vmem = pl.BlockSpec(memory_space=pltpu.VMEM)
    shapes = [((3, 2, 96, BLK), f32), ((CHUNKS, 2, 96, CHUNK), bf16), ((CHUNKS, 2, BW // 2, D), bf16), ((1, 2, 8, BLK), f32), ((1, 2, 96, D), f32), ((2, 2, HROWS, BLK), f32)]
    return pl.pallas_call(
        functools.partial(feed_kernel, digits),
        grid=(steps,),
        in_specs=[
            whole((TOK, D)), any_spec(), whole((TOK, D)), any_spec(), whole((16, D)), whole((CHUNKS, 1, CHUNK)),
            pl.BlockSpec((1, D, CHUNK), lambda t: (at(t), 0, 0)), pl.BlockSpec((1, CHUNK, D), lambda t: (at(t), 0, 0)),
            any_spec(), any_spec(), any_spec(), any_spec(), any_spec(), whole((16, D)),
        ],
        out_specs=[any_spec(), any_spec()] + [any_spec() for _ in shapes],
        out_shape=[S((TOK, D), bf16), S((TOK, D), bf16)] + [S(s, k) for s, k in shapes],
        scratch_shapes=[V(s, k) for s, k in shapes] + [
            sem((6, CHUNKS)), V((TOK, D), f32), V((TOK, D), f32), V((TOK, CHUNK), bf16), V((TOK, CHUNK), bf16), V((8, D), f32), V((CHUNKS, 1, CHUNK), f32), V((4, 2, 96, CHUNK), f32),
            V((4, 2, BW // 2, D), f32), V((4, 2, 8, BLK), f32), V((2, 4, 96, BLK), f32), V((4, 96, D), f32), sem((6,)), sem((6,)),
            V((2, 1, HROWS, BLK), f32), V((nd, 2, HROWS, BLK), bf16), V((nd, 3, HROWS, BLK), bf16),
            V((nd, 2, HROWS, BLK), bf16), sem((4 + 4 * nd, 2)), sem((4 + 4 * nd, 2)),
            V((D, TOK), bf16), V((TOK, D), bf16), V((TOK, D), bf16), V((TOK, D), bf16),
        ]
        + stream_scratch(3, 96, BLK, nd, bf16) + stream_scratch(CHUNKS, 96, CHUNK, nd, bf16)
        + stream_scratch(CHUNKS, BW // 2, D, nd, bf16) + stream_scratch(1, 8, BLK, nd, f32) + stream_scratch(1, 96, D, nd, bf16),
        compiler_params=pltpu.CompilerParams(vmem_limit_bytes=63 << 20, collective_id=cid, has_side_effects=True),
    )(n2, n2T, dy, x, vec, bias, We, Wr, base, grad, hh, og, part, vgrad)


def adam_step(master, moment, square, gradient, rate, decay):
    momentum = first_decay * moment + (1.0 - first_decay) * gradient
    squares = second_decay * square + (1.0 - second_decay) * gradient * gradient
    first_fix = momentum * (rate / (1.0 - first_decay**STEP))
    second_fix = squares * (1.0 / (1.0 - second_decay**STEP))
    updated = master - first_fix / (jnp.sqrt(second_fix) + adam_epsilon)
    if decay:
        updated = updated - (rate * decay) * master
    return (momentum, squares, updated)


def leave_kernel(lens, block, token, sq, sh, so, se, sr, *refs):
    ins, outs = refs[:12], refs[12:]
    g = pl.program_id(0)

    @pl.when(g < TOK // ATILE)
    def _():
        first, second = lens[0, 0], lens[0, 1]
        start = jnp.where(first == LONG, 0, jnp.where(second == LONG, first, first + second))
        want = lax.broadcasted_iota(jnp.int32, (ATILE, TOK), 0) + (g * ATILE - start)
        want = jnp.where(want < 0, want + TOK, want)
        turn = (want == lax.broadcasted_iota(jnp.int32, (ATILE, TOK), 1)).astype(bf16)
        outs[0][...] = dot(turn, block[...]).astype(bf16)
        outs[1][...] = dot(turn, token[...]).astype(bf16)

    def step(i, gradient):
        new = adam_step(*(ins[3 * i + j][...] for j in range(3)), gradient, matrix_rate, matrix_decay)
        for j in range(3):
            outs[2 + 3 * i + j][...] = new[j]

    step(0, jnp.concatenate([p for k in range(3) for p in (sq[0, 0, k, 0], sq[1, 0, k, 0], sh[k, 0, 0])], 1))
    step(1, so[0, 0])
    blocks = [se[k, 0, :, 128 * s : 128 * s + 128] for s in range(4) for k in range(CHUNKS)]
    step(2, jnp.concatenate(blocks, 1).astype(f32))
    step(3, sr[...].astype(f32))


def leave(lens, block, token, sums, state):
    S = jax.ShapeDtypeStruct
    sh, se, sr, so, sq = sums
    steps, per = QUARTER // AROWS, 96 // AROWS
    still = lambda *shape: pl.BlockSpec(shape, lambda g: (g, 0))
    specs = [still(AROWS, 3 * D), still(AROWS, D), still(AROWS, FF), still(D // steps, D)]
    turned = pl.BlockSpec((ATILE, D), lambda g: (jnp.minimum(g, TOK // ATILE - 1), 0))
    sums_specs = [
        pl.BlockSpec((2, 1, 3, 1, AROWS, BLK), lambda g: (0, g // per, 0, g % per, 0, 0)),
        pl.BlockSpec((3, 1, 1, AROWS, BLK), lambda g: (0, g // per, g % per, 0, 0)),
        pl.BlockSpec((1, 1, AROWS, D), lambda g: (0, g // per, g % per, 0)),
        pl.BlockSpec((CHUNKS, 1, AROWS, CHUNK), lambda g: (0, g // per, g % per, 0)),
        still(D // steps, D),
    ]
    shapes = [S((QUARTER, 3 * D), f32), S((QUARTER, D), f32), S((QUARTER, FF), f32), S((D, D), f32)]
    return pl.pallas_call(
        leave_kernel,
        grid=(steps,),
        in_specs=[pl.BlockSpec(memory_space=pltpu.SMEM), whole((TOK, D)), whole((TOK, D))] + sums_specs
        + [s for s in specs for _ in range(3)],
        out_specs=[turned] * 2 + [s for s in specs for _ in range(3)],
        out_shape=[S((TOK, D), bf16)] * 2 + [s for s in shapes for _ in range(3)],
        compiler_params=pltpu.CompilerParams(vmem_limit_bytes=60 << 20),
    )(lens, block, token, sq.reshape(2, 2, 3, per, AROWS, BLK), sh.reshape(3, 2, per, AROWS, BLK), so, se, sr.reshape(D, D), *state)


def per_device(
    tokens,
    lengths,
    cotangent,
    heads_master,
    output_master,
    expand_master,
    reduce_master,
    vector_master,
    heads_moment,
    output_moment,
    expand_moment,
    reduce_moment,
    vector_moment,
    heads_square,
    output_square,
    expand_square,
    reduce_square,
    vector_square,
):
    digits = ring_of(lax.axis_size("dp"))
    (x, dy, n1, n1T, n2, n2T, vectors, bias, cos, sin, mask, heads_weight, output_weight, expand_own, reduce_own, heads_rest) = enter(
        lengths, tokens, cotangent, vector_master.reshape(VEC_ROWS, SEG), heads_master, output_master, expand_master,
        reduce_master, 1)
    heads_grad, output_grad, base, grad, vector_grad, expand_weight, reduce_weight, part = attention(
        x, n1, n1T, dy, heads_weight, heads_rest, output_weight, vectors, cos, sin, mask, expand_own, reduce_own, 2)
    block, token, *sums = feed(
        n2, n2T, dy, x, vectors, bias, expand_weight, reduce_weight, base, grad, heads_grad,
        output_grad.reshape(1, 4, 2, 96, D), part, vector_grad, digits, 3)
    state = [
        heads_master, heads_moment, heads_square, output_master, output_moment, output_square,
        expand_master, expand_moment, expand_square, reduce_master, reduce_moment, reduce_square,
    ]
    sum_h, sum_e, sum_r, sum_v, sum_o, sum_q = sums
    vector_new = adam_step(
        vector_master, vector_moment, vector_square, sum_v.reshape(16, BLK)[:VEC_ROWS, :SEG].reshape(-1), vector_rate, 0.0)
    return (*leave(lengths, block, token, (sum_h, sum_e, sum_r, sum_o, sum_q), state), *vector_new)


def solution(mesh):
    placed = (
        P(("shard", "dp"), None),
        P(("shard", "dp"), None),
        P(("shard", "dp"), None),
        P("shard", None),
        P("shard", None),
        P("shard", None),
        P("shard", None),
        P("shard"),
        P("shard", None),
        P("shard", None),
        P("shard", None),
        P("shard", None),
        P("shard"),
        P("shard", None),
        P("shard", None),
        P("shard", None),
        P("shard", None),
        P("shard"),
    )
    return jax.shard_map(
        per_device,
        mesh=mesh,
        in_specs=placed,
        out_specs=(
            P(("shard", "dp"), None),
            P(("shard", "dp"), None),
            P("shard", None),
            P("shard", None),
            P("shard", None),
            P("shard", None),
            P("shard", None),
            P("shard", None),
            P("shard", None),
            P("shard", None),
            P("shard", None),
            P("shard", None),
            P("shard", None),
            P("shard", None),
            P("shard"),
            P("shard"),
            P("shard"),
        ),
        check_vma=False,
    )
```
